32 devices in a mesh: pipe: 2 (over x), clip: 4 (over z), head: 4 (over y, core).
Axes of the slice: x: 2, y: 2, z: 4, core: 2. Of those that a mesh axis runs over, the one named last changes fastest.
Arguments:
- enc_in: bfloat16 [8, 512, 768], P('clip', 'head'), may hold values from -6 to 6
- dec_in: bfloat16 [8, 448, 768], P('clip', 'head'), may hold values from -6 to 6
- stamp_flags: int32 [8], P('clip'), may hold values from 0 to 1, as said below
- dec_lengths: int32 [8], P('clip'), may hold values from 1 to 448, as said below
- proj_w: bfloat16 [2, 6, 768, 768], P('pipe', None, None, 'head'), may hold values from -6 to 6
- fc_in: bfloat16 [2, 768, 3072], P('pipe', None, 'head'), may hold values from -0.21875 to 0.21875
- fc_out: bfloat16 [2, 768, 3072], P('pipe', None, 'head'), may hold values from -0.109375 to 0.109375
- col_bias: float32 [2, 3, 768], P('pipe', None, 'head'), may hold values from -0.5 to 0.5
- ff_bias: float32 [2, 3072], P('pipe', 'head'), may hold values from -3 to 3
- norm_gain: float32 [2, 3, 768], P('pipe'), may hold values from 0.25 to 1.75
- row_bias: float32 [2, 5, 768], P('pipe'), may hold values from -0.5 to 0.5
- enc_cot: bfloat16 [8, 512, 768], P('clip', 'head'), may hold values from -6 to 6
- dec_cot: bfloat16 [8, 448, 768], P('clip', 'head'), may hold values from -6 to 6
Outputs:
- enc_out: bfloat16 [8, 512, 768], P('clip', 'head', 'pipe')
- dec_out: bfloat16 [8, 448, 768], P('clip', 'head', 'pipe')
- enc_in_grad: bfloat16 [8, 512, 768], P('clip', 'head', 'pipe')
- dec_in_grad: bfloat16 [8, 448, 768], P('clip', 'head', 'pipe')
- proj_w_grad: float32 [2, 6, 768, 768], P('pipe', None, 'clip', 'head')
- fc_in_grad: float32 [2, 768, 3072], P('pipe', 'clip', 'head')
- fc_out_grad: float32 [2, 768, 3072], P('pipe', 'clip', 'head')
- col_bias_grad: float32 [2, 3, 768], P('pipe', None, 'head')
- ff_bias_grad: float32 [2, 3072], P('pipe', 'head')
- norm_gain_grad: float32 [2, 3, 768], P('pipe')
- row_bias_grad: float32 [2, 5, 768], P('pipe')
The draws below stay inside these ranges and needn't reach their ends.
Inputs may be any that keep to these rules, and one draw needn't show every extreme that they name: `stamp_flags`: in every aligned group of 2 clips, one clip has a set flag. `dec_lengths`: in every aligned group of 2 clips, one clip with a set flag asks for all 448 positions.
All inputs are finite; a program needn't handle non-finite values.
Results may differ from the reference program's by a relative error of at most 0.024.
Values may be sent and summed in bfloat16 or wider, within the bound.
No kernel may reach another device: no remote copies, remote signals or barrier semaphores. Data moves between devices by JAX's collectives and lax.ppermute only.
A program may use at most 192 MiB of HBM per device.

```python
import jax
import jax.numpy as jnp
from jax import lax

HEADS = 12
HEAD_DIM = 64
D = 768
FF = 3072
FRAMES = 512
DEC = 448
DEC_SHORT = 224
MICRO = 2
CLIPS_DEV = 1
CLIPS = 8


def clip_layout(key):
    per_group = MICRO * CLIPS_DEV
    group_count = CLIPS // per_group
    pick_key, flag_key, length_key = jax.random.split(key, 3)
    chosen_slot = jax.random.randint(pick_key, (group_count,), 0, per_group)
    position = jnp.arange(CLIPS)
    chosen = position % per_group == jnp.repeat(chosen_slot, per_group)
    random_flags = jax.random.randint(flag_key, (CLIPS,), 0, 2)
    random_lengths = jax.random.randint(length_key, (CLIPS,), 1, DEC + 1)
    return (chosen, random_flags, random_lengths)


def draw_stamp_flags(key, part):
    chosen, random_flags, random_lengths = clip_layout(key)
    return jnp.where(chosen, 1, random_flags).astype(jnp.int32)


def draw_dec_lengths(key, part):
    chosen, random_flags, random_lengths = clip_layout(key)
    return jnp.where(chosen, DEC, random_lengths).astype(jnp.int32)


def draw_proj_w(key, part):
    key = jax.random.fold_in(key, 7)
    normal_draw = jnp.clip(jax.random.normal(key, (2, 6, D, D), jnp.float32), -6.0, 6.0)
    inner_scale = D ** (-0.5)
    score_scale = (2.0 / D) ** 0.5
    out_scale = (6.0 / D) ** 0.5
    scale_table = jnp.array([[score_scale, score_scale, inner_scale, out_scale, score_scale, inner_scale], [score_scale, score_scale, inner_scale, out_scale, score_scale, out_scale]], jnp.float32)
    return (normal_draw * scale_table[:, :, None, None]).astype(jnp.bfloat16)


def steps_of(own_key, extent, cuts, smallest, high):
    def one(dim, shards_of):
        heights = jax.random.uniform(jax.random.fold_in(jax.random.fold_in(own_key, 6), dim), (shards_of,), jnp.float32, smallest / len(cuts), high / len(cuts))
        return jnp.repeat(jnp.exp(heights), extent[dim] // shards_of).reshape((-1,) + (1,) * (len(extent) - dim - 1))

    factor_of = one(*cuts[0])
    for cut in cuts[1:]:
        factor_of = factor_of * one(*cut)
    return factor_of


def bell_draw(rng, extent, deviation, reach, shards=(), dtype=jnp.bfloat16):
    drawn = deviation * jax.random.normal(rng, extent, jnp.float32)
    if shards:
        drawn = drawn * steps_of(rng, extent, shards, -0.22, 0.18)
    return jnp.clip(drawn, -reach, reach).astype(dtype)


def setup_inputs(seed: int = 0) -> dict:
    seeds = jax.random.split(jax.random.key(seed), 14)
    enc_in = bell_draw(seeds[0], (CLIPS, FRAMES, D), 1.0, 6.0, ((0, 4), (1, 4)))
    dec_in = bell_draw(seeds[1], (CLIPS, DEC, D), 1.0, 6.0, ((0, 4), (1, 4)))
    stamp_flags = draw_stamp_flags(jax.random.fold_in(seeds[13], 71), 0)
    dec_lengths = draw_dec_lengths(jax.random.fold_in(seeds[13], 71), 0)
    proj_w = draw_proj_w(jax.random.fold_in(seeds[13], 71), 0)
    fc_in = bell_draw(seeds[5], (2, D, FF), D ** -0.5, 0.21875, ((0, 2), (2, 4)))
    fc_out = bell_draw(seeds[6], (2, D, FF), FF ** -0.5, 0.109375, ((0, 2), (2, 4)))
    col_bias = bell_draw(seeds[7], (2, 3, D), 0.1, 0.5, ((0, 2), (2, 4)), jnp.float32)
    ff_bias = bell_draw(seeds[8], (2, FF), 0.5, 3.0, ((0, 2), (1, 4)), jnp.float32)
    norm_gain = jnp.clip(1.0 + 0.15 * jax.random.normal(seeds[9], (2, 3, D), jnp.float32), 0.25, 1.75)
    row_bias = bell_draw(seeds[10], (2, 5, D), 0.1, 0.5, ((0, 2),), jnp.float32)
    enc_cot = bell_draw(seeds[11], (CLIPS, FRAMES, D), 1.0, 6.0, ((0, 4), (1, 4)))
    dec_cot = bell_draw(seeds[12], (CLIPS, DEC, D), 1.0, 6.0, ((0, 4), (1, 4)))
    return dict(enc_in=enc_in, dec_in=dec_in, stamp_flags=stamp_flags, dec_lengths=dec_lengths, proj_w=proj_w, fc_in=fc_in, fc_out=fc_out, col_bias=col_bias, ff_bias=ff_bias, norm_gain=norm_gain, row_bias=row_bias, enc_cot=enc_cot, dec_cot=dec_cot)


@jax.custom_vjp
def low(v):
    return lax.optimization_barrier(v.astype(jnp.bfloat16)).astype(jnp.float32)

@jax.custom_vjp
def low_back(v):
    return v

def low_keep(v):
    return (low(v), None)

def low_pass(kept, grad):
    return (grad,)

def back_keep(v):
    return (v, None)

def back_low(kept, grad):
    return (low(grad),)
low.defvjp(low_keep, low_pass)
low_back.defvjp(back_keep, back_low)

def matmul_hi(left, right):
    return jnp.dot(left, right, precision=lax.Precision.HIGHEST)

def layer_norm(inputs, gain_vec, bias_vec):
    centered = inputs - lax.optimization_barrier(jnp.mean(inputs, axis=-1, keepdims=True))
    variance = lax.optimization_barrier(jnp.mean(centered * centered, axis=-1, keepdims=True))
    return centered * lax.rsqrt(variance + 1e-05) * gain_vec + bias_vec

def attend(queries, all_keys, values, allowed):
    score_scale = HEAD_DIM ** (-0.5)

    def split_heads(matrix):
        return matrix.reshape(matrix.shape[0], HEADS, HEAD_DIM).transpose(1, 0, 2)

    def one_head(pieces):
        head_q, head_k, head_v = pieces
        scores = low_back(matmul_hi(head_q, head_k.T) * score_scale)
        if allowed is not None:
            scores = jnp.where(allowed, scores, -1e+30)
        shifted = jnp.exp(scores - lax.optimization_barrier(jnp.max(scores, axis=-1, keepdims=True)))
        weights_low = low(shifted / lax.optimization_barrier(jnp.sum(shifted, axis=-1, keepdims=True)))
        return matmul_hi(weights_low, head_v)
    mixed_heads = lax.map(jax.checkpoint(one_head), (split_heads(queries), split_heads(all_keys), split_heads(values)))
    return mixed_heads.transpose(1, 0, 2).reshape(queries.shape[0], HEADS * HEAD_DIM)

def feed_forward(residual, fc_first, fc_second, ff_vec, gain_vec, bias_vec, out_bias):
    normed = low(layer_norm(residual, gain_vec, bias_vec))
    hidden_pre = low_back(matmul_hi(normed, fc_first) + ff_vec)
    activated = low(jax.nn.gelu(hidden_pre, approximate=False))
    return residual + low_back(matmul_hi(activated, fc_second.T)) + out_bias

def self_block(residual, projections, col_vec, gain_vec, bias_vec, out_bias, allowed):
    normed = low(layer_norm(residual, gain_vec, bias_vec))
    queries = low_back(low(matmul_hi(normed, projections[0]) + col_vec[0]))
    all_keys = low_back(low(matmul_hi(normed, projections[1])))
    values = low_back(low(matmul_hi(normed, projections[2]) + col_vec[1]))
    mixed_heads = low_back(low(attend(queries, all_keys, values, allowed)))
    return residual + low_back(matmul_hi(mixed_heads, projections[3].T)) + out_bias

def encoder_block(frames, weights):
    projections, fc_first, fc_second, col_vec, ff_vec, norm_gains, row_vec = weights
    after_attn = self_block(frames, projections, col_vec, norm_gains[0], row_vec[0], row_vec[3], None)
    result = feed_forward(after_attn, fc_first, fc_second, ff_vec, norm_gains[2], row_vec[2], row_vec[4])
    states = low(layer_norm(result, norm_gains[1], row_vec[1]))
    cross_keys = low_back(low(matmul_hi(states, projections[4])))
    cross_values = low_back(low(matmul_hi(states, projections[5]) + col_vec[2]))
    return (result, cross_keys, cross_values)

def decoder_block(tokens, cross_keys, cross_values, allowed, weights):
    projections, fc_first, fc_second, col_vec, ff_vec, norm_gains, row_vec = weights
    after_self = self_block(tokens, projections, col_vec, norm_gains[0], row_vec[0], row_vec[3], allowed)
    normed = low(layer_norm(after_self, norm_gains[1], row_vec[1]))
    cross_q = low_back(low(matmul_hi(normed, projections[4]) + col_vec[2]))
    cross_mix = low_back(low(attend(cross_q, cross_keys, cross_values, None)))
    after_cross = after_self + low_back(matmul_hi(cross_mix, projections[5].T))
    return feed_forward(after_cross, fc_first, fc_second, ff_vec, norm_gains[2], row_vec[2], row_vec[4])

def reference(enc_in, dec_in, stamp_flags, dec_lengths, proj_w, fc_in, fc_out, col_bias, ff_bias, norm_gain, row_bias, enc_cot, dec_cot):
    weights = (proj_w.astype(jnp.float32), fc_in.astype(jnp.float32), fc_out.astype(jnp.float32), col_bias.astype(jnp.float32), ff_bias.astype(jnp.float32), norm_gain.astype(jnp.float32), row_bias.astype(jnp.float32))
    positions = jnp.arange(DEC).astype(jnp.int32)
    effective = jnp.minimum(dec_lengths, DEC_SHORT * (1 + stamp_flags)).astype(jnp.int32)

    def one_clip(running, inputs):
        frames, tokens, length, frame_cot, token_cot = inputs
        allowed = (positions[None, :] <= positions[:, None]) & (positions[None, :] < length)

        def forward(params, frames_in, tokens_in):
            enc_params = tuple((stacked[0] for stacked in params))
            dec_params = tuple((stacked[1] for stacked in params))
            enc_result, cross_keys, cross_values = encoder_block(frames_in, enc_params)
            return (enc_result, decoder_block(tokens_in, cross_keys, cross_values, allowed, dec_params))
        outputs_pair, pullback = jax.vjp(forward, weights, frames.astype(jnp.float32), tokens.astype(jnp.float32))
        grad_params, grad_frames, grad_tokens = pullback((frame_cot.astype(jnp.float32), token_cot.astype(jnp.float32)))
        running = jax.tree.map(jnp.add, running, grad_params)
        return (running, (outputs_pair[0].astype(jnp.bfloat16), outputs_pair[1].astype(jnp.bfloat16), grad_frames.astype(jnp.bfloat16), grad_tokens.astype(jnp.bfloat16)))
    zero_grads = jax.tree.map(jnp.zeros_like, weights)
    running, outputs = lax.scan(one_clip, zero_grads, (enc_in, dec_in, effective, enc_cot, dec_cot))
    return (outputs[0], outputs[1], outputs[2], outputs[3], running[0], running[1], running[2], running[3], running[4], running[5], running[6])
```

```python
import jax
import jax.numpy as jnp
from jax import lax
from jax.sharding import PartitionSpec as P

HEAD_DIM = 64
DEC_SHORT = 224
SCALE = HEAD_DIM ** (-0.5)
F32 = jnp.float32
BF16 = jnp.bfloat16

CORE_PAIRS = [(0, 1), (1, 0), (2, 3), (3, 2)]
ROW_PAIRS = [(0, 2), (2, 0), (1, 3), (3, 1)]
PIPE_PAIRS = [(0, 1), (1, 0)]


def swap_core(entry):
    return lax.ppermute(entry, "head", CORE_PAIRS)


def swap_row(entry):
    return lax.ppermute(entry, "head", ROW_PAIRS)


def swap_pipe(entry):
    return lax.ppermute(entry, "pipe", PIPE_PAIRS)


def dot(pattern, left, right):
    return jnp.einsum(pattern, left, right, preferred_element_type=F32)


def lowered(entry):
    return entry.astype(BF16)


def norm_parts(rows):
    centered = rows - jnp.mean(rows, axis=-1, keepdims=True)
    variance = jnp.mean(centered * centered, axis=-1, keepdims=True)
    inverse = lax.rsqrt(variance + 1e-05)
    return centered * inverse, inverse


def norm(rows, gain, bias):
    return norm_parts(rows)[0] * gain + bias


def norm_back(rows, gain, grad):
    unit, inverse = norm_parts(rows)
    scaled = grad * gain
    back = inverse * (
        scaled
        - jnp.mean(scaled, axis=-1, keepdims=True)
        - unit * jnp.mean(scaled * unit, axis=-1, keepdims=True)
    )
    own = rows.shape[0] // 2
    return back, jnp.sum((grad * unit)[:own], axis=0), jnp.sum(grad[:own], axis=0)


def both_cores(half):
    return jnp.concatenate([half, swap_core(half)])


def core_sum(partial):
    half = partial.shape[0] // 2
    return partial[:half] + swap_core(lowered(partial[half:])).astype(F32)


def half_sum(partial):
    mine = core_sum(partial)
    got = swap_row(lowered(mine)).astype(F32)
    block = got.shape[0] // 2
    return mine + jnp.concatenate([got[block:], got[:block]])


def block_sum(partial):
    mine = core_sum(partial)
    block = mine.shape[0] // 2
    return mine[:block] + swap_row(lowered(mine[block:])).astype(F32)


def attend(queries, keys, values, allowed):
    outs, totals = [], []
    for start in range(0, queries.shape[-1], HEAD_DIM):
        cut = slice(start, start + HEAD_DIM)
        scores = dot("nd,md->nm", queries[:, cut], keys[:, cut]) * SCALE
        if allowed is not None:
            scores = jnp.where(allowed, scores, -1e30)
        highest = jnp.max(scores, axis=-1, keepdims=True)
        shifted = jnp.exp(scores - highest)
        summed = jnp.sum(shifted, axis=-1, keepdims=True)
        outs.append(dot("nm,md->nd", lowered(shifted / summed), values[:, cut]))
        totals.append(highest + jnp.log(summed))
    return lowered(jnp.concatenate(outs, axis=-1)), totals


def attend_back(queries, keys, values, allowed, totals, grad):
    grad_q, grad_k, grad_v = [], [], []
    for index, start in enumerate(range(0, queries.shape[-1], HEAD_DIM)):
        cut = slice(start, start + HEAD_DIM)
        scores = dot("nd,md->nm", queries[:, cut], keys[:, cut]) * SCALE
        if allowed is not None:
            scores = jnp.where(allowed, scores, -1e30)
        weights = jnp.exp(scores - totals[index])
        grad_w = dot("nd,md->nm", grad[:, cut], values[:, cut])
        grad_s = lowered(
            weights * (grad_w - jnp.sum(weights * grad_w, axis=-1, keepdims=True))
        )
        grad_v.append(dot("nm,nd->md", lowered(weights), grad[:, cut]))
        grad_q.append(dot("nm,md->nd", grad_s, keys[:, cut]) * SCALE)
        grad_k.append(dot("nm,nd->md", grad_s, queries[:, cut]) * SCALE)
    return tuple(lowered(jnp.concatenate(part, axis=-1)) for part in (grad_q, grad_k, grad_v))


def gelu(pre):
    return 0.5 * pre * (1.0 + lax.erf(pre * (0.5 ** 0.5)))


def gelu_slope(pre):
    bell = jnp.exp(-0.5 * pre * pre) * 0.3989422804014327
    return 0.5 * (1.0 + lax.erf(pre * (0.5 ** 0.5))) + pre * bell


def wgrad(rows, grads):
    return lowered(dot("nd,ne->de", rows, grads))


def total(entry):
    return jnp.sum(entry.astype(F32), axis=0)


def butterfly(entry, axis):
    size = lax.axis_size(axis)
    step = 1
    while step < size:
        entry = entry + lax.ppermute(entry, axis, [(i, i ^ step) for i in range(size)])
        step *= 2
    return entry


def ring_scatter(entry, axis, dim):
    size = lax.axis_size(axis)
    place = lax.axis_index(axis)
    width = entry.shape[dim] // size

    def part(index):
        return lax.dynamic_slice_in_dim(entry, (index % size) * width, width, dim)

    route = [(i, (i + 1) % size) for i in range(size)]
    running = part(place + size - 1)
    for step in range(size - 1):
        running = lax.ppermute(running, axis, route) + part(place + 2 * size - step - 2)
    return running


def local(
    enc_in, dec_in, stamp_flags, dec_lengths, proj_w, fc_in, fc_out,
    col_bias, ff_bias, norm_gain, row_bias, enc_cot, dec_cot,
):
    place = lax.axis_index("pipe")
    first = place == 0
    spot = lax.axis_index("head")

    def mine(entry):
        return lax.dynamic_index_in_dim(entry, place, 0, keepdims=False)

    def pair(own):
        other = swap_pipe(own)
        return jnp.where(first, own, other), jnp.where(first, other, own)

    def two_rows(own):
        return jnp.concatenate([own, swap_row(own)])

    x = two_rows(mine(enc_in)).astype(F32)
    z = two_rows(mine(dec_in)).astype(F32)
    enc_gain, dec_gain = pair(norm_gain[0])
    enc_row, dec_row = pair(row_bias[0])
    enc_col, dec_col = pair(col_bias[0])
    enc_ff, dec_ff = pair(ff_bias[0])
    enc_p, dec_p = [list(t) for t in zip(*[pair(proj_w[0, i]) for i in range(4)])]
    enc_w1, dec_w1 = pair(fc_in[0])
    enc_w2, dec_w2 = pair(fc_out[0])
    for i in (4, 5):
        e, d = pair(proj_w[0, i])
        enc_p.append(e)
        dec_p.append(d)

    dec_rows = 4 * dec_in.shape[1]
    block = dec_in.shape[1]
    blocks = jnp.stack([spot, spot ^ 2, spot ^ 1, spot ^ 3])
    positions = (blocks[:, None] * block + jnp.arange(block)[None, :]).reshape(-1)
    length = jnp.minimum(mine(dec_lengths), DEC_SHORT * (1 + mine(stamp_flags)))
    allowed = (positions[None, :] <= positions[:, None]) & (positions[None, :] < length)

    def qkv(rows, weights, col):
        return (
            lowered(dot("nd,de->ne", rows, weights[0]) + col[0]),
            lowered(dot("nd,de->ne", rows, weights[1])),
            lowered(dot("nd,de->ne", rows, weights[2]) + col[1]),
        )

    h1 = both_cores(lowered(norm(x, enc_gain[0], enc_row[0])))
    q, k, v = qkv(h1, enc_p, enc_col)
    a, a_tot = attend(q, k, v, None)
    x1 = x + half_sum(dot("ne,de->nd", a, enc_p[3])) + enc_row[3]

    t1 = both_cores(lowered(norm(z, dec_gain[0], dec_row[0])))
    dq_, dk_, dv_ = qkv(t1, dec_p, dec_col)
    da, da_tot = attend(dq_, dk_, dv_, allowed)
    z1 = z + half_sum(dot("ne,de->nd", da, dec_p[3])) + dec_row[3]

    h2 = both_cores(lowered(norm(x1, enc_gain[2], enc_row[2])))
    u = dot("nd,df->nf", h2, enc_w1) + enc_ff
    g = lowered(gelu(u))
    y = x1 + half_sum(dot("nf,df->nd", g, enc_w2)) + enc_row[4]
    e = both_cores(lowered(norm(y, enc_gain[1], enc_row[1])))
    keys = lowered(dot("nd,de->ne", e, enc_p[4]))
    vals = lowered(dot("nd,de->ne", e, enc_p[5]) + enc_col[2])

    t2 = both_cores(lowered(norm(z1, dec_gain[1], dec_row[1])))
    cq = lowered(dot("nd,de->ne", t2, dec_p[4]) + dec_col[2])
    c, c_tot = attend(cq, keys, vals, None)
    z2 = z1 + half_sum(dot("ne,de->nd", c, dec_p[5]))
    t3 = both_cores(lowered(norm(z2, dec_gain[2], dec_row[2])))
    w_pre = dot("nd,df->nf", t3, dec_w1) + dec_ff
    w = lowered(gelu(w_pre))
    r = z2[:block] + block_sum(dot("nf,df->nd", w, dec_w2)) + dec_row[4]

    dec_cot_half = two_rows(mine(dec_cot))
    enc_cot_half = two_rows(mine(enc_cot))
    grad_br = both_cores(dec_cot_half)

    def ff_back(grad_br, pre, w1, w2):
        grad_pre = lowered(gelu_slope(pre) * dot("nd,df->nf", grad_br, w2))
        return grad_pre, dot("nf,df->nd", grad_pre, w1)

    dec_g, enc_g = {}, {}
    grad_pre, part = ff_back(grad_br, w_pre, dec_w1, dec_w2)
    dec_g["first"] = wgrad(t3, grad_pre)
    dec_g["second"] = wgrad(grad_br, w)
    dec_g["inner"] = total(grad_pre)
    back, dec_g["gain2"], dec_g["row2"] = norm_back(z2, dec_gain[2], half_sum(part))
    dec_g["row4"] = total(dec_cot_half[:block])
    gz2 = dec_cot_half.astype(F32) + back

    gbr = both_cores(lowered(gz2))
    gc = lowered(dot("nd,de->ne", gbr, dec_p[5]))
    gcq, gkeys, gvals = attend_back(cq, keys, vals, None, c_tot, gc)
    dec_g["proj5"] = wgrad(gbr, c)
    dec_g["proj4"] = wgrad(t2, gcq)
    dec_g["col2"] = total(gcq)
    ge = half_sum(dot("ne,de->nd", gkeys, enc_p[4]) + dot("ne,de->nd", gvals, enc_p[5]))
    gt2 = half_sum(dot("ne,de->nd", gcq, dec_p[4]))
    enc_g["proj4"] = wgrad(e, gkeys)
    enc_g["proj5"] = wgrad(e, gvals)
    enc_g["col2"] = total(gvals)

    back, enc_g["gain1"], enc_g["row1"] = norm_back(y, enc_gain[1], ge)
    gy = enc_cot_half.astype(F32) + back
    enc_block = x.shape[0] // 2
    enc_g["row4"] = total(gy[:enc_block])
    gbr_e = both_cores(lowered(gy))
    grad_pre, part = ff_back(gbr_e, u, enc_w1, enc_w2)
    enc_g["first"] = wgrad(h2, grad_pre)
    enc_g["second"] = wgrad(gbr_e, g)
    enc_g["inner"] = total(grad_pre)

    back, dec_g["gain1"], dec_g["row1"] = norm_back(z1, dec_gain[1], gt2)
    gz1 = gz2 + back
    dec_g["row3"] = total(gz1[:block])

    def self_back(gres, weights, normed, queries, keys, values, mixed, totals, mask, found):
        gbr = both_cores(lowered(gres))
        ga = lowered(dot("nd,de->ne", gbr, weights[3]))
        gq, gk, gv = attend_back(queries, keys, values, mask, totals, ga)
        found["proj3"] = wgrad(gbr, mixed)
        found["proj0"] = wgrad(normed, gq)
        found["proj1"] = wgrad(normed, gk)
        found["proj2"] = wgrad(normed, gv)
        found["col0"] = total(gq)
        found["col1"] = total(gv)
        return block_sum(
            dot("ne,de->nd", gq, weights[0])
            + dot("ne,de->nd", gk, weights[1])
            + dot("ne,de->nd", gv, weights[2])
        )

    def own_norm_back(rows, gain, grad):
        unit, inverse = norm_parts(rows)
        scaled = grad * gain
        back = inverse * (
            scaled
            - jnp.mean(scaled, axis=-1, keepdims=True)
            - unit * jnp.mean(scaled * unit, axis=-1, keepdims=True)
        )
        return back, jnp.sum(grad * unit, axis=0), jnp.sum(grad, axis=0)

    gt1 = self_back(gz1, dec_p, t1, dq_, dk_, dv_, da, da_tot, allowed, dec_g)
    back, dec_g["gain0"], dec_g["row0"] = own_norm_back(z[:block], dec_gain[0], gt1)
    gz = gz1[:block] + back

    back, enc_g["gain2"], enc_g["row2"] = norm_back(x1, enc_gain[2], half_sum(part))
    gx1 = gy + back
    enc_g["row3"] = total(gx1[:enc_block])
    gh1 = self_back(gx1, enc_p, h1, q, k, v, a, a_tot, None, enc_g)
    back, enc_g["gain0"], enc_g["row0"] = own_norm_back(x[:enc_block], enc_gain[0], gh1)
    gx = gx1[:enc_block] + back

    def placed(own):
        low = lowered(own)
        half = low.shape[-1] // 2
        left, right = low[:, :half], low[:, half:]
        got = swap_pipe(jnp.where(first, right, left))
        keep = jnp.where(first, left, right)
        return jnp.stack([jnp.where(first, keep, got), jnp.where(first, got, keep)])

    def reduced(enc_part, dec_part, dim):
        keep = jnp.where(first, enc_part, dec_part)
        got = swap_pipe(jnp.where(first, dec_part, enc_part))
        return ring_scatter(keep + got, "clip", dim).astype(F32)[None]

    def stacked(found):
        return jnp.stack([found[f"proj{i}"] for i in range(6)])

    out_first = reduced(enc_g["first"], dec_g["first"], 0)
    out_second = reduced(enc_g["second"], dec_g["second"], 0)
    out_proj = reduced(stacked(enc_g), stacked(dec_g), 1)

    def vectors(names):
        return jnp.concatenate(
            [jnp.stack([found[name] for name in names]) for found in (enc_g, dec_g)]
        )

    wide = vectors(("gain0", "gain1", "gain2", "row0", "row1", "row2", "row3", "row4"))
    slim = jnp.stack(
        [
            jnp.concatenate([found["col0"], found["col1"], found["col2"], found["inner"]])
            for found in (enc_g, dec_g)
        ]
    )
    wide = butterfly(wide, "head")
    packed = jnp.concatenate([wide.reshape(2, -1), slim], axis=1)
    packed = butterfly(butterfly(packed, "clip"), "pipe")
    packed = lax.dynamic_index_in_dim(packed, place, 0, keepdims=False)
    width = norm_gain.shape[-1]
    wide = packed[: 8 * width].reshape(8, width)
    slim = packed[8 * width :]
    col_width = col_bias.shape[-1]
    return (
        placed(y[:enc_block]),
        placed(r),
        placed(gx),
        placed(gz),
        out_proj,
        out_first,
        out_second,
        slim[: 3 * col_width].reshape(1, 3, col_width),
        slim[3 * col_width :][None],
        wide[:3][None],
        wide[3:][None],
    )


def solution(mesh):
    return jax.shard_map(
        local,
        mesh=mesh,
        in_specs=(
            P("clip", "head", None),
            P("clip", "head", None),
            P("clip"),
            P("clip"),
            P("pipe", None, None, "head"),
            P("pipe", None, "head"),
            P("pipe", None, "head"),
            P("pipe", None, "head"),
            P("pipe", "head"),
            P("pipe", None, None),
            P("pipe", None, None),
            P("clip", "head", None),
            P("clip", "head", None),
        ),
        out_specs=(
            P("clip", "head", "pipe"),
            P("clip", "head", "pipe"),
            P("clip", "head", "pipe"),
            P("clip", "head", "pipe"),
            P("pipe", None, "clip", "head"),
            P("pipe", "clip", "head"),
            P("pipe", "clip", "head"),
            P("pipe", None, "head"),
            P("pipe", "head"),
            P("pipe", None, None),
            P("pipe", None, None),
        ),
        check_vma=False,
    )
```

```python
import functools

import jax
import jax.numpy as jnp
from jax import lax
from jax.experimental import pallas as pl
from jax.experimental.pallas import tpu as pltpu
from jax.sharding import PartitionSpec as P

HEAD_DIM = 64
DEC_SHORT = 224
SCALE = HEAD_DIM ** (-0.5)
F32 = jnp.float32
BF16 = jnp.bfloat16
ENC, DEC = 0, 1

CORE_GROUPS = [[0, 1], [2, 3]]
CORE_PAIRS = [(0, 1), (1, 0), (2, 3), (3, 2)]
ROW_PAIRS = [(0, 2), (2, 0), (1, 3), (3, 1)]
PIPE_PAIRS = [(0, 1), (1, 0)]

GAIN, ROW, FF, COL = 0, 3, 8, 9


def both_cores(entry):
    return lax.all_gather(entry, "head", axis=0, axis_index_groups=CORE_GROUPS, tiled=True)


def swap_core(entry):
    return lax.ppermute(entry, "head", CORE_PAIRS)


def swap_row(entry):
    return lax.ppermute(entry, "head", ROW_PAIRS)


def swap_pipe(entry):
    return lax.ppermute(entry, "pipe", PIPE_PAIRS)


def swap_pair(entry):
    size = lax.axis_size("clip")
    return lax.ppermute(entry, "clip", [(i, i ^ 1) for i in range(size)])


def over_clips(entry):
    size = lax.axis_size("clip")
    place = lax.axis_index("clip")
    width = entry.shape[0] // size

    def part(index):
        return lax.dynamic_slice_in_dim(entry, (index % size) * width, width, 0)

    route = [(i, (i + 1) % size) for i in range(size)]
    running = part(place + size - 1)
    for step in range(size - 1):
        running = lax.ppermute(running, "clip", route) + part(place + 2 * size - step - 2)
    return running


def to_section(entry, section):
    return lax.ppermute(entry, "pipe", [(1 - section, section)])


def nn(left, right):
    return lax.dot_general(left, right, (((1,), (0,)), ((), ())), preferred_element_type=F32)


def nt(left, right):
    return lax.dot_general(left, right, (((1,), (1,)), ((), ())), preferred_element_type=F32)


def tn(left, right):
    return lax.dot_general(left, right, (((0,), (0,)), ((), ())), preferred_element_type=F32)


def shape(*dims, dtype=BF16):
    return jax.ShapeDtypeStruct(dims, dtype)


ORDER = [None]
COST = dict(
    self_fwd=6.3, self_bwd=6.7, cross_fwd=5.9, cross_bwd=6.7, ff_fwd=2.2, ff_bwd=2.4, wgrad=1.7,
    both_wgrad=1.7, norm_in=0.8, res_norm=0.9, norm_back=1.2, take=1.2, last_back=1.2,
    join_two=1.9, finish=2.5, place=1.3,
)


def call(body, outs, *ins, flops=0, limit=12, scratch=(), anywhere=(), out_anywhere=False, also=()):
    vmem = pl.BlockSpec(memory_space=pltpu.VMEM)
    smem = pl.BlockSpec(memory_space=pltpu.SMEM)
    any_space = pl.BlockSpec(memory_space=pl.ANY)
    hbm = pl.BlockSpec(memory_space=pltpu.HBM)
    specs = [
        hbm if place in anywhere else smem if a.dtype == jnp.int32 else vmem
        for place, a in enumerate(ins)
    ]
    count = len(ins)
    before = (*(() if ORDER[0] is None else (ORDER[0],)), *also)

    def ordered(*refs):
        body(*refs[:count], *refs[count + len(before) :])

    name = getattr(body, "func", body).__name__[:-5]
    found = pl.pallas_call(
        ordered,
        name=name,
        out_shape=outs,
        in_specs=[*specs, *[any_space] * len(before)],
        out_specs=[hbm if out_anywhere else vmem] * len(outs),
        scratch_shapes=scratch,
        compiler_params=pltpu.CompilerParams(vmem_limit_bytes=limit << 20),
        cost_estimate=pl.CostEstimate(
            flops=int(COST.get(name, 0.6) * 1.15e9), bytes_accessed=1, transcendentals=0
        ),
    )(*ins, *before)
    ORDER[0] = found[-1]
    return found


def pick(sel, section, own, near, far):
    is_own = sel[0] == section
    even = sel[1] == 0
    half = near.shape[0]
    top = jnp.where(is_own, own[:half], jnp.where(even, near, far))
    bottom = jnp.where(is_own, own[half:], jnp.where(even, far, near))
    return jnp.concatenate([top, bottom])


def choose(sel, section, own, got):
    return jnp.where(sel[0] == section, own, got)


def vector(sel, section, vecs, row, width=None):
    own, got = vecs
    cut = slice(0, width if width else own.shape[1])
    return jnp.where(sel[0] == section, own[row : row + 1, cut], got[row : row + 1, cut])


def norm_parts(rows):
    centered = rows - jnp.mean(rows, axis=-1, keepdims=True)
    variance = jnp.mean(centered * centered, axis=-1, keepdims=True)
    inverse = lax.rsqrt(variance + 1e-05)
    return centered * inverse, inverse


def take_body(count, sel, *refs):
    out, sems = refs[-2:]
    copies, at = [], 0
    for i in range(count):
        rows = refs[i].shape[1]
        copies.append(
            pltpu.make_async_copy(refs[i].at[sel[0]], out.at[at : at + rows], sems.at[i])
        )
        at += rows
    for copy in copies:
        copy.start()
    for copy in copies:
        copy.wait()


def take(sel, *arrays, limit=12):
    count = len(arrays)
    rows = sum(a.shape[1] for a in arrays)
    return call(
        functools.partial(take_body, count), [shape(rows, arrays[0].shape[2])], sel, *arrays,
        anywhere=range(1, 1 + count), scratch=[pltpu.SemaphoreType.DMA((count,))], limit=limit,
    )[0]


def split_body(cuts, sel, *refs):
    count = max(source for source, _, _ in cuts) + 1
    sems = refs[-1]
    copies = []
    for place, (source, start, stop) in enumerate(cuts):
        out = refs[count + place]
        half = out.shape[1]
        rows = pl.ds(pl.multiple_of(sel[1] * half, half), half)
        if half == refs[source].shape[1]:
            rows = slice(None)
        copies.append(
            pltpu.make_async_copy(refs[source].at[start:stop, rows], out, sems.at[place])
        )
    for copy in copies:
        copy.start()
    for copy in copies:
        copy.wait()


def split(sel, arrays, cuts, also=(), limit=12, parts=2):
    outs = [
        shape(stop - start, arrays[source].shape[1] // parts, arrays[source].shape[2])
        for source, start, stop in cuts
    ]
    return call(
        functools.partial(split_body, cuts), outs, sel, *arrays,
        anywhere=range(1, 1 + len(arrays)), out_anywhere=True,
        scratch=[pltpu.SemaphoreType.DMA((len(cuts),))], also=also, limit=limit,
    )


def pack_body(gain, row, ff, col, out):
    out[...] = jnp.zeros_like(out)
    out[GAIN : GAIN + 3] = gain[...]
    out[ROW : ROW + 5] = row[...]
    out[FF : FF + 1] = ff[...]
    out[COL : COL + 3, : col.shape[1]] = col[...]


def add_body(start, pm, recv, low):
    low[...] = (pm[start:] + recv[start:].astype(F32)).astype(BF16)


def add_low(pm, recv, start=0):
    rows, width = pm.shape
    return call(functools.partial(add_body, start), [shape(rows - start, width)], pm, recv)[0]


def norm_in_body(section, sel, own, got, vown, vgot, hm_ref):
    gain = vector(sel, section, (vown, vgot), GAIN)
    bias = vector(sel, section, (vown, vgot), ROW)
    block = own.shape[0]
    for start, part in ((0, own), (block, got)):
        unit, _ = norm_parts(part[...].astype(F32))
        hm_ref[start : start + block] = (unit * gain + bias).astype(BF16)


def norm_in(section, sel, pieces, vecs):
    block, width = pieces[0].shape
    return call(
        functools.partial(norm_in_body, section), [shape(2 * block, width)], sel, *pieces, *vecs
    )[0]


def summed(pm, recv, got, rows, other):
    return pm[rows] + recv[rows].astype(F32) + got[other].astype(F32)


def halves(block):
    return ((slice(0, block), slice(block, 2 * block)), (slice(block, 2 * block), slice(0, block)))


def res_norm_body(section, out_row, index, split, *refs):
    sel = refs[0]
    res = refs[1 : 3 if split else 2]
    pm, recv, got, vown, vgot, x_ref, hm_ref = refs[3 if split else 2 :]
    vecs = (vown, vgot)
    gain = vector(sel, section, vecs, GAIN + index)
    bias = vector(sel, section, vecs, ROW + index)
    block = pm.shape[0] // 2
    for place, (rows, other) in enumerate(halves(block)):
        base = res[place][...].astype(F32) if split else res[0][rows]
        now = base + summed(pm, recv, got, rows, other)
        if out_row is not None:
            now = now + vector(sel, section, vecs, ROW + out_row)
        x_ref[rows] = now
        unit, _ = norm_parts(now)
        hm_ref[rows] = (unit * gain + bias).astype(BF16)


def res_norm(section, sel, res, sums, vecs, out_row, index):
    split = isinstance(res, tuple)
    rows, width = sums[0].shape
    return call(
        functools.partial(res_norm_body, section, out_row, index, split),
        [shape(rows, width, dtype=F32), shape(rows, width)],
        sel, *(res if split else (res,)), *sums, *vecs,
    )


def norm_grad(rows, gain, grad):
    unit, inverse = norm_parts(rows)
    scaled = grad * gain
    back = inverse * (
        scaled
        - jnp.mean(scaled, axis=-1, keepdims=True)
        - unit * jnp.mean(scaled * unit, axis=-1, keepdims=True)
    )
    return back, unit


def col_sum(entry):
    return jnp.sum(entry, axis=0, keepdims=True)


def norm_back_body(section, index, split, *refs):
    sel, x = refs[:2]
    res = refs[2 : 4 if split else 3]
    pm, recv, got, vown, vgot, g_ref, gm_ref, sum_ref = refs[4 if split else 3 :]
    gain = vector(sel, section, (vown, vgot), GAIN + index)
    block = pm.shape[0] // 2
    for place, (rows, other) in enumerate(halves(block)):
        grad = summed(pm, recv, got, rows, other)
        base = res[place][...].astype(F32) if split else res[0][rows]
        back, unit = norm_grad(x[rows], gain, grad)
        now = base + back
        g_ref[rows] = now
        gm_ref[rows] = now.astype(BF16)
        if place == 0:
            sum_ref[0:1] = col_sum(grad * unit)
            sum_ref[1:2] = col_sum(grad)
            sum_ref[2:3] = col_sum(now)
            sum_ref[3:4] = col_sum(base)


def norm_back(section, sel, x, res, sums, vecs, index):
    split = isinstance(res, tuple)
    rows, width = x.shape
    return call(
        functools.partial(norm_back_body, section, index, split),
        [shape(rows, width, dtype=F32), shape(rows, width), shape(4, width, dtype=F32)],
        sel, x, *(res if split else (res,)), *sums, *vecs,
    )


def send_halves(sel, rows, low, keep_ref, send_ref):
    width = low.shape[1] // 2
    left, right = low[:, :width], low[:, width:]
    keep_ref[rows] = jnp.where(sel[0] == 0, left, right)
    send_ref[rows] = jnp.where(sel[0] == 0, right, left)


def last_fwd_body(sel, y, z2, pm, recv, got, vown, vgot, keep_ref, send_ref):
    block = got.shape[0]
    e_block = y.shape[0] // 2
    rows = slice(0, block)
    r = z2[rows] + pm[rows] + recv[rows].astype(F32) + got[...].astype(F32)
    r = r + vector(sel, DEC, (vown, vgot), ROW + 4)
    send_halves(sel, slice(0, e_block), y[:e_block].astype(BF16), keep_ref, send_ref)
    send_halves(sel, slice(e_block, e_block + block), r.astype(BF16), keep_ref, send_ref)


def last_fwd(sel, y, z2, sums, vecs):
    rows = y.shape[0] // 2 + sums[2].shape[0]
    width = y.shape[1] // 2
    return call(
        last_fwd_body, [shape(rows, width), shape(rows, width)], sel, y, z2, *sums, *vecs
    )


def last_back_body(
    sel, x, z, gx1, gz1, xm, xr, xg, zm, zr, zg, vown, vgot,
    keep_ref, send_ref, sum_x, sum_z,
):
    start = 0
    for section, own, res, pm, recv, got, out in (
        (ENC, x, gx1, xm, xr, xg, sum_x), (DEC, z, gz1, zm, zr, zg, sum_z)
    ):
        gain = vector(sel, section, (vown, vgot), GAIN)
        block = own.shape[0]
        rows = slice(0, block)
        grad = pm[rows] + recv[rows].astype(F32) + got[...].astype(F32)
        back, unit = norm_grad(own[...].astype(F32), gain, grad)
        low = (res[rows] + back).astype(BF16)
        send_halves(sel, slice(start, start + block), low, keep_ref, send_ref)
        out[0:1] = col_sum(grad * unit)
        out[1:2] = col_sum(grad)
        start += block


def last_back(sel, x, z, gx1, gz1, x_sums, z_sums, vecs):
    rows, width = x.shape[0] + z.shape[0], x.shape[1]
    return call(
        last_back_body,
        [
            shape(rows, width // 2), shape(rows, width // 2),
            shape(2, width, dtype=F32), shape(2, width, dtype=F32),
        ],
        sel, x, z, gx1, gz1, *x_sums, *z_sums, *vecs,
    )


def place_body(sel, keep, got, e_ref, d_ref):
    block = e_ref.shape[1]
    for ref, rows in ((e_ref, slice(0, block)), (d_ref, slice(block, keep.shape[0]))):
        ref[0] = jnp.where(sel[0] == 0, keep[rows], got[rows])
        ref[1] = jnp.where(sel[0] == 0, got[rows], keep[rows])


def placed(sel, keep, got, block):
    rows, width = keep.shape
    return call(
        place_body, [shape(2, block, width), shape(2, rows - block, width)], sel, keep, got
    )


def allowed(sel, flags, lengths, start, tile, rows):
    length = jnp.minimum(lengths[sel[0]], DEC_SHORT * (1 + flags[sel[0]]))
    keys = lax.broadcasted_iota(jnp.int32, (tile, rows), 1)
    shift = sel[5] - 3
    for block in (2, 1, 0):
        shift = jnp.where(keys < (block + 1) * tile, sel[2 + block] - block, shift)
    keys = keys + shift * tile
    queries = lax.broadcasted_iota(jnp.int32, (tile, rows), 0) + sel[2 + start // tile] * tile
    return (keys <= queries) & (keys < length)


def attend(q_ref, q_at, kv_ref, k_at, v_at, tile, mask, a_ref, lse_ref):
    rows, width = a_ref.shape
    for head in range(width // HEAD_DIM):
        cut = slice(head * HEAD_DIM, (head + 1) * HEAD_DIM)
        k_head = kv_ref[:, k_at + cut.start : k_at + cut.stop]
        v_head = kv_ref[:, v_at + cut.start : v_at + cut.stop]
        for start in range(0, rows, tile):
            spot = slice(start, start + tile)
            scores = nt(q_ref[spot, q_at + cut.start : q_at + cut.stop], k_head) * SCALE
            if mask:
                scores = jnp.where(allowed(*mask, start, tile, rows), scores, -1e30)
            top = jnp.max(scores, axis=-1, keepdims=True)
            shifted = jnp.exp(scores - top)
            total = jnp.sum(shifted, axis=-1, keepdims=True)
            low = (shifted * (1.0 / total)).astype(BF16)
            a_ref[spot, cut] = nn(low, v_head).astype(BF16)
            lse_ref[spot, head : head + 1] = top + jnp.log(total)


def attend_back(
    q_ref, q_at, kv_ref, k_at, v_at, grad, lse, tile, mask, gq_ref, gq_at, gkv_ref, gk_at, gv_at
):
    rows, width = grad.shape
    for head in range(width // HEAD_DIM):
        cut = slice(head * HEAD_DIM, (head + 1) * HEAD_DIM)
        k_head = kv_ref[:, k_at + cut.start : k_at + cut.stop]
        v_head = kv_ref[:, v_at + cut.start : v_at + cut.stop]
        gk = gv = None
        for start in range(0, rows, tile):
            spot = slice(start, start + tile)
            q_tile = q_ref[spot, q_at + cut.start : q_at + cut.stop]
            o_tile = grad[spot, cut]
            scores = nt(q_tile, k_head) * SCALE
            if mask:
                scores = jnp.where(allowed(*mask, start, tile, rows), scores, -1e30)
            weights = jnp.exp(scores - lse[spot, head : head + 1])
            grad_w = nt(o_tile, v_head)
            both = weights * grad_w
            grad_s = (both - weights * jnp.sum(both, axis=-1, keepdims=True)).astype(BF16)
            gq_ref[spot, gq_at + cut.start : gq_at + cut.stop] = (
                nn(grad_s, k_head) * SCALE
            ).astype(BF16)
            part_k = tn(grad_s, q_tile)
            part_v = tn(weights.astype(BF16), o_tile)
            gk = part_k if gk is None else gk + part_k
            gv = part_v if gv is None else gv + part_v
        gkv_ref[:, gk_at + cut.start : gk_at + cut.stop] = (gk * SCALE).astype(BF16)
        gkv_ref[:, gv_at + cut.start : gv_at + cut.stop] = gv.astype(BF16)


def halves_of(sel, half):
    mine = pl.ds(pl.multiple_of(sel[6] * half, half), half)
    other = pl.ds(pl.multiple_of((1 - sel[6]) * half, half), half)
    return mine, other


def project_out(sel, mixed_ref, weight, pm_ref, po_ref, by=nn):
    mine, other = halves_of(sel, pm_ref.shape[0])
    pm_ref[...] = by(mixed_ref[mine], weight)
    po_ref[...] = by(mixed_ref[other], weight).astype(BF16)


def self_fwd_body(section, masked, *refs):
    sel, h, own, near_a, far_a, near_b, far_b, vown, vgot = refs[:9]
    mask = (sel, *refs[9:11]) if masked else None
    qkv_ref, a_ref, lse_ref, pm_ref, po_ref = refs[11 if masked else 9 :]
    width = a_ref.shape[1]
    wq = pick(sel, section, own[0], near_a[0], far_a[0])
    wk = pick(sel, section, own[1], near_a[1], far_a[1])
    wv = pick(sel, section, own[2], near_b[0], far_b[0])
    bq = vector(sel, section, (vown, vgot), COL, width)
    bv = vector(sel, section, (vown, vgot), COL + 1, width)
    rows = h[...]
    qkv_ref[:, :width] = (nt(rows, wq) + bq).astype(BF16)
    qkv_ref[:, width : 2 * width] = nt(rows, wk).astype(BF16)
    qkv_ref[:, 2 * width :] = (nt(rows, wv) + bv).astype(BF16)
    attend(qkv_ref, 0, qkv_ref, width, 2 * width, h.shape[0] // 4, mask, a_ref, lse_ref)
    wo = pick(sel, section, own[3], near_b[1], far_b[1])
    project_out(sel, a_ref, wo, pm_ref, po_ref)


def self_fwd(section, sel, h, weights, vecs, mask):
    rows, width = h.shape
    heads = weights[0].shape[1]
    outs = [
        shape(rows, 3 * heads), shape(rows, heads), shape(rows, heads // HEAD_DIM, dtype=F32),
        shape(rows // 2, width, dtype=F32), shape(rows // 2, width),
    ]
    return call(
        functools.partial(self_fwd_body, section, bool(mask)), outs, sel, h, *weights, *vecs, *mask
    )


def self_bwd_body(section, masked, *refs):
    sel, g, qkv, lse, own, near_a, far_a, near_b, far_b = refs[:9]
    mask = (sel, *refs[9:11]) if masked else None
    gqkv_ref, pm_ref, po_ref, sum_ref, ga = refs[11 if masked else 9 :]
    width = ga.shape[1]
    wo = pick(sel, section, own[3], near_b[1], far_b[1])
    ga[...] = nt(g[...], wo).astype(BF16)
    attend_back(
        qkv, 0, qkv, width, 2 * width, ga, lse, g.shape[0] // 4, mask,
        gqkv_ref, 0, gqkv_ref, width, 2 * width,
    )
    weight = jnp.concatenate(
        [
            pick(sel, section, own[0], near_a[0], far_a[0]),
            pick(sel, section, own[1], near_a[1], far_a[1]),
            pick(sel, section, own[2], near_b[0], far_b[0]),
        ]
    )
    project_out(sel, gqkv_ref, weight, pm_ref, po_ref)
    sum_ref[...] = col_sum(gqkv_ref[...].astype(F32))


def self_bwd(section, sel, g, qkv, lse, weights, mask):
    rows, width = g.shape
    heads = weights[0].shape[1]
    outs = [
        shape(rows, 3 * heads), shape(rows // 2, width, dtype=F32), shape(rows // 2, width),
        shape(1, 3 * heads, dtype=F32),
    ]
    return call(
        functools.partial(self_bwd_body, section, bool(mask)), outs, sel, g, qkv, lse,
        *weights, *mask, scratch=[pltpu.VMEM((rows, heads), BF16)],
    )


def cross_fwd_body(
    sel, t, e, own, got, vown, vgot, cq_ref, kv_ref, c_ref, lse_ref, pm_ref, po_ref
):
    width = cq_ref.shape[1]
    vecs = (vown, vgot)
    w4 = choose(sel, ENC, own[4], got[0])
    w5 = choose(sel, ENC, own[5], got[1])
    rows = e[...]
    kv_ref[:, :width] = nt(rows, w4).astype(BF16)
    kv_ref[:, width:] = (nt(rows, w5) + vector(sel, ENC, vecs, COL + 2, width)).astype(BF16)
    wq = choose(sel, DEC, own[4], got[0])
    cq_ref[...] = (nt(t[...], wq) + vector(sel, DEC, vecs, COL + 2, width)).astype(BF16)
    attend(cq_ref, 0, kv_ref, 0, width, t.shape[0] // 4, None, c_ref, lse_ref)
    wo = choose(sel, DEC, own[5], got[1])
    project_out(sel, c_ref, wo, pm_ref, po_ref)


def cross_fwd(sel, t, e, weights, vecs):
    rows, width = t.shape
    e_rows, heads = e.shape[0], weights[0].shape[1]
    outs = [
        shape(rows, heads), shape(e_rows, 2 * heads), shape(rows, heads),
        shape(rows, heads // HEAD_DIM, dtype=F32), shape(rows // 2, width, dtype=F32),
        shape(rows // 2, width),
    ]
    return call(cross_fwd_body, outs, sel, t, e, *weights, *vecs)


def cross_bwd_body(
    sel, g, cq, kv, lse, own, got,
    gcq_ref, gkv_ref, pm_ref, po_ref, em_ref, eo_ref, sum_ref, gc,
):
    width = cq.shape[1]
    wo = choose(sel, DEC, own[5], got[1])
    gc[...] = nt(g[...], wo).astype(BF16)
    attend_back(
        cq, 0, kv, 0, width, gc, lse, g.shape[0] // 4, None, gcq_ref, 0, gkv_ref, 0, width
    )
    weight = jnp.concatenate(
        [
            choose(sel, ENC, own[4], got[0]),
            choose(sel, ENC, own[5], got[1]),
        ]
    )
    project_out(sel, gkv_ref, weight, em_ref, eo_ref)
    project_out(sel, gcq_ref, choose(sel, DEC, own[4], got[0]), pm_ref, po_ref)
    sum_ref[0:1] = col_sum(gkv_ref[:, width:].astype(F32))
    sum_ref[1:2] = col_sum(gcq_ref[...].astype(F32))


def cross_bwd(sel, g, cq, kv, lse, weights):
    rows, width = g.shape
    e_rows, heads = kv.shape[0], cq.shape[1]
    outs = [
        shape(rows, heads), shape(e_rows, 2 * heads),
        shape(rows // 2, width, dtype=F32), shape(rows // 2, width),
        shape(e_rows // 2, width, dtype=F32), shape(e_rows // 2, width),
        shape(2, heads, dtype=F32),
    ]
    return call(
        cross_bwd_body, outs, sel, g, cq, kv, lse, *weights,
        scratch=[pltpu.VMEM((rows, heads), BF16)],
    )


def gelu(pre):
    return 0.5 * pre * (1.0 + lax.erf(pre * (0.5 ** 0.5)))


def pick_ff(sel, section, weights):
    own1, near1, far1, own2, got2 = weights
    w1 = pick(sel, section, own1[...], near1[...], far1[...])
    return w1, choose(sel, section, own2[...], got2[...])


def ff_fwd_body(section, sel, h, own1, near1, far1, own2, got2, vown, vgot, u_ref, g_ref, pm_ref, po_ref):
    w1, w2 = pick_ff(sel, section, (own1, near1, far1, own2, got2))
    u = nn(h[...], w1) + vector(sel, section, (vown, vgot), FF)
    u_ref[...] = u
    g_ref[...] = gelu(u).astype(BF16)
    project_out(sel, g_ref, w2, pm_ref, po_ref, nt)


def ff_fwd(section, sel, h, weights, vecs):
    rows, width = h.shape
    hidden = weights[0].shape[-1]
    outs = [
        shape(rows, hidden, dtype=F32), shape(rows, hidden),
        shape(rows // 2, width, dtype=F32), shape(rows // 2, width),
    ]
    return call(functools.partial(ff_fwd_body, section), outs, sel, h, *weights, *vecs)


def ff_bwd_body(section, sel, g, u, own1, near1, far1, own2, got2, gp_ref, pm_ref, po_ref, sum_ref):
    w1, w2 = pick_ff(sel, section, (own1, near1, far1, own2, got2))
    pre = u[...]
    bell = jnp.exp(-0.5 * pre * pre) * 0.3989422804014327
    slope = 0.5 * (1.0 + lax.erf(pre * (0.5 ** 0.5))) + pre * bell
    low = (slope * nn(g[...], w2)).astype(BF16)
    gp_ref[...] = low
    sum_ref[...] = col_sum(low.astype(F32))
    project_out(sel, gp_ref, w1, pm_ref, po_ref, nt)


def ff_bwd(section, sel, g, u, weights):
    rows, width = g.shape
    hidden = weights[0].shape[-1]
    outs = [
        shape(rows, hidden), shape(rows // 2, width, dtype=F32), shape(rows // 2, width),
        shape(1, hidden, dtype=F32),
    ]
    return call(functools.partial(ff_bwd_body, section), outs, sel, g, u, *weights)


def wgrad_body(cuts, sel, *refs):
    out = refs[-1]
    for place, (start, stop) in enumerate(cuts):
        left, right = refs[2 * place : 2 * place + 2]
        out[:, start:stop] = tn(left[...], right[...]).astype(BF16)


def columns(pairs):
    cuts, at = [], 0
    for _, right in pairs:
        cuts.append((at, at + right.shape[1]))
        at += right.shape[1]
    return cuts, at


def wgrads(sel, *pairs):
    cuts, wide = columns(pairs)
    return call(
        functools.partial(wgrad_body, cuts), [shape(pairs[0][0].shape[1], wide)], sel,
        *[entry for pair in pairs for entry in pair],
    )[0]


def wgrad_sides_body(cuts, sel, other, *refs):
    keep, send = refs[-2:]
    wgrad_body(cuts, sel, *refs[:-2], keep)
    e, d = keep[...], other[...]
    first = sel[0] == 0
    keep[...] = jnp.where(first, e, d)
    send[...] = jnp.where(first, d, e)


def wgrad_sides(sel, other, *pairs):
    cuts, wide = columns(pairs)
    out = shape(pairs[0][0].shape[1], wide)

    return call(
        functools.partial(wgrad_sides_body, cuts), [out, out], sel, other,
        *[entry for pair in pairs for entry in pair],
    )


def join_body(own, got, out):
    out[...] = (own[...].astype(F32) + got[...].astype(F32)).astype(BF16)


def joined(own, got):
    return call(join_body, [shape(*own.shape)], own, got)[0]


def sides_body(sel, ff_e, ff_d, cross, keep, send):
    first = sel[0] == 0
    wide, half = ff_e.shape[1], cross.shape[1] // 2
    e, d = ff_e[...], ff_d[...]
    keep[:, :wide] = jnp.where(first, e, d)
    send[:, :wide] = jnp.where(first, d, e)
    e, d = cross[:, :half], cross[:, half:]
    keep[:, wide:] = jnp.where(first, e, d)
    send[:, wide:] = jnp.where(first, d, e)


def sides(sel, ff_e, ff_d, cross):
    out = shape(ff_e.shape[0], ff_e.shape[1] + cross.shape[1] // 2)
    return call(sides_body, [out, out], sel, ff_e, ff_d, cross)


def finish_body(keep, got, own, w1, w2, proj):
    hidden, heads = w1.shape[2], proj.shape[3]
    total = keep[...].astype(F32) + got[...].astype(F32)
    w2[0] = total[:, :hidden]
    w1[0] = total[:, hidden : 2 * hidden]
    for place in range(2):
        start = 2 * hidden + place * heads
        proj[0, 4 + place] = total[:, start : start + heads]
    mine = own[...].astype(F32)
    for place in range(4):
        proj[0, place] = mine[:, place * heads : (place + 1) * heads]


def pack_sums_body(ey, ex1, ex, dz2, dz1, dz, wide):
    rows = (
        (ex, 0), (ey, 0), (ex1, 0), (ex, 1), (ey, 1), (ex1, 1), (ex1, 2), (ey, 2),
        (dz, 0), (dz1, 0), (dz2, 0), (dz, 1), (dz1, 1), (dz2, 1), (dz1, 2), (dz2, 3),
    )
    for at, (ref, row) in enumerate(rows):
        wide[at : at + 1] = ref[row : row + 1]


def pack_slim_body(wide, self_e, self_d, cross, inner_e, inner_d, out):
    width = cross.shape[1]
    count = wide.shape[0]
    out[:count] = wide[...]
    out[count:] = jnp.zeros((out.shape[0] - count, out.shape[1]), F32)
    for at, (own, place, inner) in enumerate(((self_e, 0, inner_e), (self_d, 1, inner_d))):
        row = count + 2 * at
        out[row : row + 1, :width] = own[:, :width]
        out[row : row + 1, width : 2 * width] = own[:, 2 * width :]
        out[row : row + 1, 2 * width : 3 * width] = cross[place : place + 1]
        out[row + 1 : row + 2] = inner[...]


def butterfly(entry, axis):
    size = lax.axis_size(axis)
    step = 1
    while step < size:
        entry = entry + lax.ppermute(entry, axis, [(i, i ^ step) for i in range(size)])
        step *= 2
    return entry


def local(
    enc_in, dec_in, stamp_flags, dec_lengths, proj_w, fc_in, fc_out,
    col_bias, ff_bias, norm_gain, row_bias, enc_cot, dec_cot,
):
    ORDER[0] = None
    place = lax.axis_index("pipe")
    spot = lax.axis_index("head")
    parity = lax.axis_index("clip") % 2
    row, core = spot // 2, spot % 2
    sel = [place, parity, 2 * row, 2 - 2 * row, 2 * row + 1, 3 - 2 * row, core]
    sel = jnp.stack(sel).astype(jnp.int32)
    width = norm_gain.shape[-1]

    own = jnp.swapaxes(proj_w[0], 1, 2)
    half_a, half_b = split(sel, [own], [(0, 0, 2), (0, 2, 4)])
    near_a, near_b = swap_pipe(half_a), swap_pipe(half_b)
    x_own = take(sel, enc_in)
    x = (x_own, swap_row(x_own))
    vown = call(
        pack_body, [shape(16, width, dtype=F32)],
        norm_gain[0], row_bias[0], ff_bias, col_bias[0],
    )[0]
    vecs = (vown, swap_pipe(vown))
    e_block, block = enc_in.shape[1], dec_in.shape[1]
    rest_own = take(sel, dec_in, dec_cot, enc_cot)
    rest_got = swap_row(rest_own)

    def rest(start, stop):
        return rest_own[start:stop], rest_got[start:stop]

    z, dec_cots, enc_cots = rest(0, block), rest(block, 2 * block), rest(2 * block, None)
    z_own = z[0]
    h1 = both_cores(norm_in(ENC, sel, x, vecs))
    far_a, far_b = swap_pair(near_a), swap_pair(near_b)
    self_w = (own, near_a, far_a, near_b, far_b)
    (half_1,) = split(sel, [fc_in], [(0, 0, 1)], also=vecs[1:])
    near_1 = swap_pipe(half_1)
    (whole_2,) = split(sel, [fc_out], [(0, 0, 1)], parts=1)
    got_2 = swap_pipe(whole_2)
    t1 = both_cores(norm_in(DEC, sel, z, vecs))
    mask = (stamp_flags, dec_lengths)

    qkv, a, lse, x_pm, po = self_fwd(ENC, sel, h1, self_w, vecs, ())
    x_recv = swap_core(po)
    x_got = swap_row(add_low(x_pm, x_recv))
    (whole_c,) = split(sel, [own], [(0, 4, 6)], also=(near_1,), parts=1)
    far_1, got_c = swap_pair(near_1), swap_pipe(whole_c)
    dqkv, da, dlse, z_pm, po = self_fwd(DEC, sel, t1, self_w, vecs, mask)
    z_recv = swap_core(po)
    x1, hm = res_norm(ENC, sel, x, (x_pm, x_recv, x_got), vecs, 3, 2)
    h2 = both_cores(hm)
    z_got = swap_row(add_low(z_pm, z_recv))
    ff_w = (fc_in[0], near_1[0], far_1[0], fc_out[0], got_2[0])
    u, g, y_pm, po = ff_fwd(ENC, sel, h2, ff_w, vecs)
    y_recv = swap_core(po)
    cross_w = (own, got_c)
    y_got = swap_row(add_low(y_pm, y_recv))
    z1, tm = res_norm(DEC, sel, z, (z_pm, z_recv, z_got), vecs, 3, 1)
    t2 = both_cores(tm)
    y, em = res_norm(ENC, sel, x1, (y_pm, y_recv, y_got), vecs, 4, 1)
    e = both_cores(em)
    cq, kv, c, clse, z_pm, po = cross_fwd(sel, t2, e, cross_w, vecs)
    z_recv = swap_core(po)
    z_got = swap_row(add_low(z_pm, z_recv))
    gbr_z2 = both_cores(jnp.concatenate(dec_cots))
    z2, tm = res_norm(DEC, sel, z1, (z_pm, z_recv, z_got), vecs, None, 2)
    t3 = both_cores(tm)
    w_pre, w, r_pm, po = ff_fwd(DEC, sel, t3, ff_w, vecs)
    r_recv = swap_core(po)

    gp_d, z_pm, po, inner_d = ff_bwd(DEC, sel, gbr_z2, w_pre, ff_w)
    z_recv = swap_core(po)
    z_got = swap_row(add_low(z_pm, z_recv))
    ff_d = over_clips(wgrads(sel, (gbr_z2, w), (t3, gp_d)))
    gz2, gm, sums_z2 = norm_back(DEC, sel, z2, dec_cots, (z_pm, z_recv, z_got), vecs, 2)
    gbr_c = both_cores(gm)

    gcq, gkv, z_pm, zo, y_pm, yo, sums_c = cross_bwd(sel, gbr_c, cq, kv, clse, cross_w)
    y_recv = swap_core(yo)
    z_recv = swap_core(zo)
    y_got = swap_row(add_low(y_pm, y_recv))
    z_got = swap_row(add_low(z_pm, z_recv))
    cross = over_clips(wgrads(sel, (e, gkv), (t2, gcq), (gbr_c, c)))
    gy, gm, sums_y = norm_back(ENC, sel, y, enc_cots, (y_pm, y_recv, y_got), vecs, 1)
    gbr_y = both_cores(gm)
    gp_e, x_pm, po, inner_e = ff_bwd(ENC, sel, gbr_y, u, ff_w)
    x_recv = swap_core(po)
    x_got = swap_row(add_low(x_pm, x_recv))
    ff_e = over_clips(wgrads(sel, (gbr_y, g), (h2, gp_e)))
    gz1, gm, sums_z1 = norm_back(DEC, sel, z1, gz2, (z_pm, z_recv, z_got), vecs, 1)
    gbr_z1 = both_cores(gm)
    gqkv_d, z_pm, po, self_d = self_bwd(DEC, sel, gbr_z1, dqkv, dlse, self_w, mask)
    z_recv = swap_core(po)
    gx1, gm, sums_x1 = norm_back(ENC, sel, x1, gy, (x_pm, x_recv, x_got), vecs, 2)
    gbr_x1 = both_cores(gm)
    z_got = swap_row(add_low(z_pm, z_recv, block))
    gqkv_e, x_pm, po, self_e = self_bwd(ENC, sel, gbr_x1, qkv, lse, self_w, ())
    x_recv = swap_core(po)
    x_got = swap_row(add_low(x_pm, x_recv, x_pm.shape[0] // 2))
    own_d = wgrads(sel, (t1, gqkv_d), (gbr_z1, da))
    own_keep, own_send = wgrad_sides(sel, own_d, (h1, gqkv_e), (gbr_x1, a))
    own_got = swap_pipe(own_send)
    keep, send, sums_x, sums_z = last_back(
        sel, x_own, z_own, gx1, gz1, (x_pm, x_recv, x_got), (z_pm, z_recv, z_got), vecs
    )
    r_got = swap_row(add_low(r_pm, r_recv, block))
    wide = call(
        pack_sums_body, [shape(16, width, dtype=F32)],
        sums_y, sums_x1, sums_x, sums_z2, sums_z1, sums_z,
    )[0]
    wide = butterfly(wide, "head")
    packed = call(
        pack_slim_body, [shape(24, width, dtype=F32)],
        wide, self_e, self_d, sums_c, inner_e, inner_d,
    )[0]
    packed = butterfly(packed, "clip")
    out_own = over_clips(joined(own_keep, own_got))
    keep_fwd, send_fwd = last_fwd(sel, y, z2, (r_pm, r_recv, r_got), vecs)
    got_fwd = swap_pipe(send_fwd)
    got = swap_pipe(send)
    packed = butterfly(packed, "pipe")
    side_keep, side_send = sides(sel, ff_e, ff_d, cross)
    side_got = swap_pipe(side_send)
    e_out, d_out = placed(sel, keep_fwd, got_fwd, x_own.shape[0])
    ge_out, gd_out = placed(sel, keep, got, x_own.shape[0])
    heads, hidden, cut = own.shape[1], fc_in.shape[-1], out_own.shape[0]
    out_first, out_second, out_proj = call(
        finish_body,
        [
            shape(1, cut, hidden, dtype=F32),
            shape(1, cut, hidden, dtype=F32),
            shape(1, 6, cut, heads, dtype=F32),
        ],
        side_keep, side_got, out_own,
    )
    first = place == 0
    wide = jnp.where(first, packed[:8], packed[8:16])
    slim = jnp.where(first, packed[16:18], packed[18:20])
    return (
        e_out,
        d_out,
        ge_out,
        gd_out,
        out_proj,
        out_first,
        out_second,
        slim[0, : 3 * heads].reshape(1, 3, heads),
        slim[1:2],
        wide[:3][None],
        wide[3:][None],
    )


def solution(mesh):
    return jax.shard_map(
        local,
        mesh=mesh,
        in_specs=(
            P("clip", "head", None),
            P("clip", "head", None),
            P("clip"),
            P("clip"),
            P("pipe", None, None, "head"),
            P("pipe", None, "head"),
            P("pipe", None, "head"),
            P("pipe", None, "head"),
            P("pipe", "head"),
            P("pipe", None, None),
            P("pipe", None, None),
            P("clip", "head", None),
            P("clip", "head", None),
        ),
        out_specs=(
            P("clip", "head", "pipe"),
            P("clip", "head", "pipe"),
            P("clip", "head", "pipe"),
            P("clip", "head", "pipe"),
            P("pipe", None, "clip", "head"),
            P("pipe", "clip", "head"),
            P("pipe", "clip", "head"),
            P("pipe", None, "head"),
            P("pipe", "head"),
            P("pipe", None, None),
            P("pipe", None, None),
        ),
        check_vma=False,
    )
```

```python
import functools

import jax
import jax.numpy as jnp
from jax import lax
from jax.experimental import pallas as pl
from jax.experimental.pallas import tpu as pltpu
from jax.sharding import PartitionSpec as P

HEAD_DIM = 64
DEC_SHORT = 224
SCALE = HEAD_DIM ** (-0.5)
SCALE_2 = SCALE * 1.4426950408889634
F32 = jnp.float32
BF16 = jnp.bfloat16
ENC, DEC = 0, 1

CORE_GROUPS = [[0, 1], [2, 3]]
CORE_PAIRS = [(0, 1), (1, 0), (2, 3), (3, 2)]
ROW_PAIRS = [(0, 2), (2, 0), (1, 3), (3, 1)]
PIPE_PAIRS = [(0, 1), (1, 0)]

GAIN, ROW, FF, COL = 0, 3, 8, 9


def both_cores(entry):
    return lax.all_gather(entry, "head", axis=0, axis_index_groups=CORE_GROUPS, tiled=True)


def swap_core(entry):
    return lax.ppermute(entry, "head", CORE_PAIRS)


def swap_row(entry):
    return lax.ppermute(entry, "head", ROW_PAIRS)


def swap_pipe(entry):
    return lax.ppermute(entry, "pipe", PIPE_PAIRS)


def swap_pair(entry):
    size = lax.axis_size("clip")
    return lax.ppermute(entry, "clip", [(i, i ^ 1) for i in range(size)])


def next_clip(entry):
    size = lax.axis_size("clip")
    return lax.ppermute(entry, "clip", [(i, (i + 1) % size) for i in range(size)])


def to_section(entry, section):
    return lax.ppermute(entry, "pipe", [(1 - section, section)])


def nn(left, right):
    return lax.dot_general(left, right, (((1,), (0,)), ((), ())), preferred_element_type=F32)


def nt(left, right):
    return lax.dot_general(left, right, (((1,), (1,)), ((), ())), preferred_element_type=F32)


def tn(left, right):
    return lax.dot_general(left, right, (((0,), (0,)), ((), ())), preferred_element_type=F32)


def shape(*dims, dtype=BF16):
    return jax.ShapeDtypeStruct(dims, dtype)


ORDER = [None]
COST = dict(
    self_fwd=3.4, self_bwd=4.8, cross_fwd=3.5, cross_bwd=5.4, ff_fwd=2.4, ff_bwd=2.8, wgrad=1.7,
    both_wgrad=1.7, norm_in=0.8, res_norm=0.9, norm_back=1.2, take=1.2, last_back=1.2,
    join_two=1.9, finish=2.5, place=1.3,
)


def call(body, outs, *ins, flops=0, limit=12, scratch=(), anywhere=(), out_anywhere=False, also=()):
    vmem = pl.BlockSpec(memory_space=pltpu.VMEM)
    smem = pl.BlockSpec(memory_space=pltpu.SMEM)
    any_space = pl.BlockSpec(memory_space=pl.ANY)
    hbm = pl.BlockSpec(memory_space=pltpu.HBM)
    specs = [
        hbm if place in anywhere else smem if a.dtype == jnp.int32 else vmem
        for place, a in enumerate(ins)
    ]
    count = len(ins)
    before = (*(() if ORDER[0] is None else (ORDER[0],)), *also)

    def ordered(*refs):
        body(*refs[:count], *refs[count + len(before) :])

    name = getattr(body, "func", body).__name__[:-5]
    found = pl.pallas_call(
        ordered,
        name=name,
        out_shape=outs,
        in_specs=[*specs, *[any_space] * len(before)],
        out_specs=[hbm if out_anywhere else vmem] * len(outs),
        scratch_shapes=scratch,
        compiler_params=pltpu.CompilerParams(vmem_limit_bytes=limit << 20),
        cost_estimate=pl.CostEstimate(
            flops=int(COST.get(name, 0.6) * 1.15e9), bytes_accessed=1, transcendentals=0
        ),
    )(*ins, *before)
    ORDER[0] = found[-1]
    return found


def pick(sel, section, own, near, far):
    is_own = sel[0] == section
    even = sel[1] == 0
    half = near.shape[0]
    top = jnp.where(is_own, own[:half], jnp.where(even, near, far))
    bottom = jnp.where(is_own, own[half:], jnp.where(even, far, near))
    return jnp.concatenate([top, bottom])


def choose(sel, section, own, got):
    return jnp.where(sel[0] == section, own, got)


def vector(sel, section, vecs, row, width=None):
    own, got = vecs
    cut = slice(0, width if width else own.shape[1])
    return jnp.where(sel[0] == section, own[row : row + 1, cut], got[row : row + 1, cut])


def norm_parts(rows):
    centered = rows - jnp.mean(rows, axis=-1, keepdims=True)
    variance = jnp.mean(centered * centered, axis=-1, keepdims=True)
    inverse = lax.rsqrt(variance + 1e-05)
    return centered * inverse, inverse


def take_body(count, sel, *refs):
    out, sems = refs[-2:]
    copies, at = [], 0
    for i in range(count):
        rows = refs[i].shape[1]
        copies.append(
            pltpu.make_async_copy(refs[i].at[sel[0]], out.at[at : at + rows], sems.at[i])
        )
        at += rows
    for copy in copies:
        copy.start()
    for copy in copies:
        copy.wait()


def take(sel, *arrays, limit=12, also=()):
    count = len(arrays)
    rows = sum(a.shape[1] for a in arrays)
    return call(
        functools.partial(take_body, count), [shape(rows, arrays[0].shape[2])], sel, *arrays,
        anywhere=range(1, 1 + count), scratch=[pltpu.SemaphoreType.DMA((count,))], limit=limit,
        also=also,
    )[0]


def split_body(cuts, sel, *refs):
    count = max(source for source, _, _ in cuts) + 1
    sems = refs[-1]
    copies = []
    for place, (source, start, stop) in enumerate(cuts):
        out = refs[count + place]
        half = out.shape[1]
        rows = pl.ds(pl.multiple_of(sel[1] * half, half), half)
        if half == refs[source].shape[1]:
            rows = slice(None)
        copies.append(
            pltpu.make_async_copy(refs[source].at[start:stop, rows], out, sems.at[place])
        )
    for copy in copies:
        copy.start()
    for copy in copies:
        copy.wait()


def split(sel, arrays, cuts, also=(), limit=12, parts=2):
    outs = [
        shape(stop - start, arrays[source].shape[1] // parts, arrays[source].shape[2])
        for source, start, stop in cuts
    ]
    return call(
        functools.partial(split_body, cuts), outs, sel, *arrays,
        anywhere=range(1, 1 + len(arrays)), out_anywhere=True,
        scratch=[pltpu.SemaphoreType.DMA((len(cuts),))], also=also, limit=limit,
    )


def pack_body(gain, row, ff, col, out):
    out[...] = jnp.zeros_like(out)
    out[GAIN : GAIN + 3] = gain[...]
    out[ROW : ROW + 5] = row[...]
    out[FF : FF + 1] = ff[...]
    out[COL : COL + 3, : col.shape[1]] = col[...]


def add_body(start, sel, pm, recv, low):
    count = low.shape[0]
    there = pl.ds(pl.multiple_of((1 - sel[6]) * pm.shape[0] + start, count), count)
    low[...] = (pm[start : start + count] + recv[there].astype(F32)).astype(BF16)


def add_low(sel, pm, recv, start=0, also=()):
    rows, width = pm.shape
    return call(
        functools.partial(add_body, start), [shape(rows - start, width)], sel, pm, recv, also=also
    )[0]


def add_last_body(sel, xm, xr, zm, zr, low):
    at = 0
    for pm, recv in ((xm, xr), (zm, zr)):
        count = pm.shape[0] // 2
        there = pl.ds(pl.multiple_of((1 - sel[6]) * pm.shape[0] + count, count), count)
        low[at : at + count] = (pm[count:] + recv[there].astype(F32)).astype(BF16)
        at += count


def add_last(sel, xm, xr, zm, zr, also=()):
    rows = (xm.shape[0] + zm.shape[0]) // 2
    return call(
        add_last_body, [shape(rows, xm.shape[1])], sel, xm, xr, zm, zr, also=also
    )[0]


def stack_body(start, block, own, got, out):
    out[:block] = own[start : start + block]
    out[block:] = got[start : start + block]


def stacked(rows):
    own, got, start, block = rows
    return call(
        functools.partial(stack_body, start, block), [shape(2 * block, own.shape[1])], own, got
    )[0]


def norm_in_body(section, at, sel, own, got, vown, vgot, hm_ref):
    gain = vector(sel, section, (vown, vgot), GAIN)
    bias = vector(sel, section, (vown, vgot), ROW)
    block = hm_ref.shape[0] // 2
    for start, part in ((0, own), (block, got)):
        unit, _ = norm_parts(part[at : at + block].astype(F32))
        hm_ref[start : start + block] = (unit * gain + bias).astype(BF16)


def norm_in(section, sel, rows, vecs, also=()):
    own, got, start, block = rows
    return call(
        functools.partial(norm_in_body, section, start), [shape(2 * block, own.shape[1])],
        sel, own, got, *vecs, also=also,
    )[0]


def summed(sel, pm, recv, got, rows, other):
    block = rows.stop - rows.start
    there = pl.ds(pl.multiple_of((1 - sel[6]) * pm.shape[0] + rows.start, block), block)
    return pm[rows] + recv[there].astype(F32) + got[other].astype(F32)


def halves(block):
    return ((slice(0, block), slice(block, 2 * block)), (slice(block, 2 * block), slice(0, block)))


def res_norm_body(section, out_row, index, at, *refs):
    split = at is not None
    sel = refs[0]
    res = refs[1 : 3 if split else 2]
    pm, recv, got, vown, vgot, x_ref, hm_ref = refs[3 if split else 2 :]
    vecs = (vown, vgot)
    gain = vector(sel, section, vecs, GAIN + index)
    bias = vector(sel, section, vecs, ROW + index)
    block = pm.shape[0] // 2
    for place, (rows, other) in enumerate(halves(block)):
        base = res[place][at : at + block].astype(F32) if split else res[0][rows]
        now = base + summed(sel, pm, recv, got, rows, other)
        if out_row is not None:
            now = now + vector(sel, section, vecs, ROW + out_row)
        x_ref[rows] = now
        unit, _ = norm_parts(now)
        hm_ref[rows] = (unit * gain + bias).astype(BF16)


def res_norm(section, sel, res, sums, vecs, out_row, index, also=()):
    rows, width = sums[0].shape
    at, res = (res[2], res[:2]) if isinstance(res, tuple) else (None, (res,))
    return call(
        functools.partial(res_norm_body, section, out_row, index, at),
        [shape(rows, width, dtype=F32), shape(rows, width)],
        sel, *res, *sums, *vecs, also=also,
    )


def norm_grad(rows, gain, grad):
    unit, inverse = norm_parts(rows)
    scaled = grad * gain
    back = inverse * (
        scaled
        - jnp.mean(scaled, axis=-1, keepdims=True)
        - unit * jnp.mean(scaled * unit, axis=-1, keepdims=True)
    )
    return back, unit


def col_sum(entry):
    return jnp.sum(entry, axis=0, keepdims=True)


def norm_back_body(section, index, at, *refs):
    split = at is not None
    sel, x = refs[:2]
    res = refs[2 : 4 if split else 3]
    pm, recv, got, vown, vgot, g_ref, gm_ref, sum_ref = refs[4 if split else 3 :]
    gain = vector(sel, section, (vown, vgot), GAIN + index)
    block = pm.shape[0] // 2
    for place, (rows, other) in enumerate(halves(block)):
        grad = summed(sel, pm, recv, got, rows, other)
        base = res[place][at : at + block].astype(F32) if split else res[0][rows]
        back, unit = norm_grad(x[rows], gain, grad)
        now = base + back
        g_ref[rows] = now
        gm_ref[rows] = now.astype(BF16)
        if place == 0:
            sum_ref[0:1] = col_sum(grad * unit)
            sum_ref[1:2] = col_sum(grad)
            sum_ref[2:3] = col_sum(now)
            sum_ref[3:4] = col_sum(base)


def norm_back(section, sel, x, res, sums, vecs, index):
    rows, width = x.shape
    at, res = (res[2], res[:2]) if isinstance(res, tuple) else (None, (res,))
    return call(
        functools.partial(norm_back_body, section, index, at),
        [shape(rows, width, dtype=F32), shape(rows, width), shape(4, width, dtype=F32)],
        sel, x, *res, *sums, *vecs,
    )


def send_halves(sel, rows, low, keep_ref, send_ref):
    width = low.shape[1] // 2
    left, right = low[:, :width], low[:, width:]
    keep_ref[rows] = jnp.where(sel[0] == 0, left, right)
    send_ref[rows] = jnp.where(sel[0] == 0, right, left)


def last_fwd_body(sel, y, z2, pm, recv, got, vown, vgot, keep_ref, send_ref):
    block = got.shape[0]
    e_block = y.shape[0] // 2
    rows = slice(0, block)
    r = z2[rows] + summed(sel, pm, recv, got, rows, rows)
    r = r + vector(sel, DEC, (vown, vgot), ROW + 4)
    send_halves(sel, slice(0, e_block), y[:e_block].astype(BF16), keep_ref, send_ref)
    send_halves(sel, slice(e_block, e_block + block), r.astype(BF16), keep_ref, send_ref)


def last_fwd(sel, y, z2, sums, vecs):
    rows = y.shape[0] // 2 + sums[2].shape[0]
    width = y.shape[1] // 2
    return call(
        last_fwd_body, [shape(rows, width), shape(rows, width)], sel, y, z2, *sums, *vecs
    )


def last_back_body(
    sel, rows_in, gx1, gz1, xm, xr, zm, zr, all_got, vown, vgot,
    keep_ref, send_ref, sum_x, sum_z,
):
    start = 0
    for section, res, pm, recv, out in ((ENC, gx1, xm, xr, sum_x), (DEC, gz1, zm, zr, sum_z)):
        gain = vector(sel, section, (vown, vgot), GAIN)
        block = pm.shape[0] // 2
        rows = slice(0, block)
        grad = summed(sel, pm, recv, all_got, rows, slice(start, start + block))
        back, unit = norm_grad(rows_in[start : start + block].astype(F32), gain, grad)
        low = (res[rows] + back).astype(BF16)
        send_halves(sel, slice(start, start + block), low, keep_ref, send_ref)
        out[0:1] = col_sum(grad * unit)
        out[1:2] = col_sum(grad)
        start += block


def last_back(sel, rows_in, gx1, gz1, sums, vecs):
    rows, width = rows_in.shape
    return call(
        last_back_body,
        [
            shape(rows, width // 2), shape(rows, width // 2),
            shape(2, width, dtype=F32), shape(2, width, dtype=F32),
        ],
        sel, rows_in, gx1, gz1, *sums, *vecs,
    )


def place_body(sel, keep, got, e_ref, d_ref):
    block = e_ref.shape[1]
    for ref, rows in ((e_ref, slice(0, block)), (d_ref, slice(block, keep.shape[0]))):
        ref[0] = jnp.where(sel[0] == 0, keep[rows], got[rows])
        ref[1] = jnp.where(sel[0] == 0, got[rows], keep[rows])


def placed(sel, keep, got, block):
    rows, width = keep.shape
    return call(
        place_body, [shape(2, block, width), shape(2, rows - block, width)], sel, keep, got
    )


def places(sel, axis, dims):
    at = lax.broadcasted_iota(jnp.int32, dims, axis)
    size = dims[axis] // 4
    shift = sel[5] - 3
    for block in (2, 1, 0):
        shift = jnp.where(at < (block + 1) * size, sel[2 + block] - block, shift)
    return at + shift * size


def text_length(sel, flags, lengths):
    return jnp.minimum(lengths[sel[0]], DEC_SHORT * (1 + flags[sel[0]]))


def allowed(sel, flags, lengths, rows, key_axis):
    shapes = ((1, rows), (rows, 1)) if key_axis == 1 else ((rows, 1), (1, rows))
    keys = places(sel, key_axis, shapes[0])
    keys = jnp.where(keys < text_length(sel, flags, lengths), keys, rows)
    return keys <= places(sel, 1 - key_axis, shapes[1])


def attend(q_ref, q_at, kv_ref, k_at, v_at, mask, a_ref, lse_ref):
    rows, width = a_ref.shape
    ones = jnp.ones((kv_ref.shape[0], HEAD_DIM), BF16)
    if mask:
        keep = allowed(*mask, rows, 1)
    for head in range(width // HEAD_DIM):
        cut = slice(head * HEAD_DIM, (head + 1) * HEAD_DIM)
        k_head = kv_ref[:, k_at + cut.start : k_at + cut.stop]
        v_head = kv_ref[:, v_at + cut.start : v_at + cut.stop]
        scores = nt(q_ref[:, q_at + cut.start : q_at + cut.stop], k_head)
        if mask:
            scores = jnp.where(keep, scores, -1e30)
        top = jnp.max(scores, axis=-1, keepdims=True)
        low = jnp.exp2((scores - top) * SCALE_2).astype(BF16)
        both = nn(low, jnp.concatenate([v_head, ones], axis=1))
        total = both[:, HEAD_DIM : HEAD_DIM + 1]
        a_ref[:, cut] = (both[:, :HEAD_DIM] * (1.0 / total)).astype(BF16)
        lse_ref[:, head : head + 1] = top * SCALE_2 + jnp.log2(total)


def attend_back(
    q_ref, q_at, kv_ref, k_at, v_at, grad, lse, mask, gq_ref, gq_at, gkv_ref, gk_at, gv_at,
    rows_ref,
):
    rows, width = grad.shape
    rows_ref[:, : lse.shape[1]] = lse[...]
    sums = rows_ref[...].T
    if mask:
        keep = allowed(*mask, rows, 0)
    for head in range(width // HEAD_DIM):
        cut = slice(head * HEAD_DIM, (head + 1) * HEAD_DIM)
        q_head = q_ref[:, q_at + cut.start : q_at + cut.stop]
        o_head = grad[:, cut]
        k_head = kv_ref[:, k_at + cut.start : k_at + cut.stop]
        v_head = kv_ref[:, v_at + cut.start : v_at + cut.stop]
        scores = nt(k_head, q_head)
        if mask:
            scores = jnp.where(keep, scores, -1e30)
        weights = jnp.exp2(scores * SCALE_2 - sums[head : head + 1])
        both = weights * nt(v_head, o_head)
        grad_s = (both - weights * jnp.sum(both, axis=0, keepdims=True)).astype(BF16)
        gv = nn(weights.astype(BF16), o_head)
        gk = nn(grad_s, q_head) * SCALE
        gq = tn(grad_s, k_head) * SCALE
        gkv_ref[:, gk_at + cut.start : gk_at + cut.stop] = gk.astype(BF16)
        gkv_ref[:, gv_at + cut.start : gv_at + cut.stop] = gv.astype(BF16)
        gq_ref[:, gq_at + cut.start : gq_at + cut.stop] = gq.astype(BF16)


def halves_of(sel, half):
    mine = pl.ds(pl.multiple_of(sel[6] * half, half), half)
    other = pl.ds(pl.multiple_of((1 - sel[6]) * half, half), half)
    return mine, other


def project_out(sel, mixed_ref, weight, pm_ref, po_ref, by=nn):
    mine, other = halves_of(sel, pm_ref.shape[0])
    pm_ref[...] = by(mixed_ref[mine], weight)
    po_ref[...] = by(mixed_ref[other], weight).astype(BF16)


def self_fwd_body(section, masked, *refs):
    sel, h, own, near_a, far_a, near_b, far_b, vown, vgot = refs[:9]
    mask = (sel, *refs[9:11]) if masked else None
    qkv_ref, a_ref, lse_ref, pm_ref, po_ref = refs[11 if masked else 9 :]
    width = a_ref.shape[1]
    wq = pick(sel, section, own[0], near_a[0], far_a[0])
    wk = pick(sel, section, own[1], near_a[1], far_a[1])
    wv = pick(sel, section, own[2], near_b[0], far_b[0])
    bq = vector(sel, section, (vown, vgot), COL, width)
    bv = vector(sel, section, (vown, vgot), COL + 1, width)
    rows = h[...]
    qkv_ref[:, :width] = (nt(rows, wq) + bq).astype(BF16)
    qkv_ref[:, width : 2 * width] = nt(rows, wk).astype(BF16)
    qkv_ref[:, 2 * width :] = (nt(rows, wv) + bv).astype(BF16)
    attend(qkv_ref, 0, qkv_ref, width, 2 * width, mask, a_ref, lse_ref)
    wo = pick(sel, section, own[3], near_b[1], far_b[1])
    project_out(sel, a_ref, wo, pm_ref, po_ref)


def self_fwd(section, sel, h, weights, vecs, mask, also=()):
    rows, width = h.shape
    heads = weights[0].shape[1]
    outs = [
        shape(rows, 3 * heads), shape(rows, heads), shape(rows, heads // HEAD_DIM, dtype=F32),
        shape(rows // 2, width, dtype=F32), shape(rows // 2, width),
    ]
    return call(
        functools.partial(self_fwd_body, section, bool(mask)), outs, sel, h, *weights, *vecs, *mask,
        also=also,
    )


def back_scratch(rows, heads):
    return [pltpu.VMEM((rows, heads), BF16), pltpu.VMEM((rows, 128), F32)]


def self_bwd_body(section, masked, *refs):
    sel, g, qkv, lse, own, near_a, far_a, near_b, far_b = refs[:9]
    mask = (sel, *refs[9:11]) if masked else None
    gqkv_ref, pm_ref, po_ref, sum_ref, ga, spare = refs[11 if masked else 9 :]
    width = ga.shape[1]
    wo = pick(sel, section, own[3], near_b[1], far_b[1])
    ga[...] = nt(g[...], wo).astype(BF16)
    attend_back(
        qkv, 0, qkv, width, 2 * width, ga, lse, mask,
        gqkv_ref, 0, gqkv_ref, width, 2 * width, spare,
    )
    weight = jnp.concatenate(
        [
            pick(sel, section, own[0], near_a[0], far_a[0]),
            pick(sel, section, own[1], near_a[1], far_a[1]),
            pick(sel, section, own[2], near_b[0], far_b[0]),
        ]
    )
    project_out(sel, gqkv_ref, weight, pm_ref, po_ref)
    sum_ref[...] = col_sum(gqkv_ref[...].astype(F32))


def self_bwd(section, sel, g, qkv, lse, weights, mask):
    rows, width = g.shape
    heads = weights[0].shape[1]
    outs = [
        shape(rows, 3 * heads), shape(rows // 2, width, dtype=F32), shape(rows // 2, width),
        shape(1, 3 * heads, dtype=F32),
    ]
    return call(
        functools.partial(self_bwd_body, section, bool(mask)), outs, sel, g, qkv, lse,
        *weights, *mask, scratch=back_scratch(rows, heads),
    )


def cross_fwd_body(
    sel, t, e, own, got, vown, vgot, cq_ref, kv_ref, c_ref, lse_ref, pm_ref, po_ref
):
    width = cq_ref.shape[1]
    vecs = (vown, vgot)
    w4 = choose(sel, ENC, own[4], got[0])
    w5 = choose(sel, ENC, own[5], got[1])
    rows = e[...]
    kv_ref[:, :width] = nt(rows, w4).astype(BF16)
    kv_ref[:, width:] = (nt(rows, w5) + vector(sel, ENC, vecs, COL + 2, width)).astype(BF16)
    wq = choose(sel, DEC, own[4], got[0])
    cq_ref[...] = (nt(t[...], wq) + vector(sel, DEC, vecs, COL + 2, width)).astype(BF16)
    attend(cq_ref, 0, kv_ref, 0, width, None, c_ref, lse_ref)
    wo = choose(sel, DEC, own[5], got[1])
    project_out(sel, c_ref, wo, pm_ref, po_ref)


def cross_fwd(sel, t, e, weights, vecs):
    rows, width = t.shape
    e_rows, heads = e.shape[0], weights[0].shape[1]
    outs = [
        shape(rows, heads), shape(e_rows, 2 * heads), shape(rows, heads),
        shape(rows, heads // HEAD_DIM, dtype=F32), shape(rows // 2, width, dtype=F32),
        shape(rows // 2, width),
    ]
    return call(cross_fwd_body, outs, sel, t, e, *weights, *vecs)


def cross_bwd_body(
    sel, g, cq, kv, lse, own, got,
    gcq_ref, gkv_ref, pm_ref, po_ref, em_ref, eo_ref, sum_ref, gc, spare,
):
    width = cq.shape[1]
    wo = choose(sel, DEC, own[5], got[1])
    gc[...] = nt(g[...], wo).astype(BF16)
    attend_back(
        cq, 0, kv, 0, width, gc, lse, None, gcq_ref, 0, gkv_ref, 0, width, spare
    )
    weight = jnp.concatenate(
        [
            choose(sel, ENC, own[4], got[0]),
            choose(sel, ENC, own[5], got[1]),
        ]
    )
    project_out(sel, gkv_ref, weight, em_ref, eo_ref)
    project_out(sel, gcq_ref, choose(sel, DEC, own[4], got[0]), pm_ref, po_ref)
    sum_ref[0:1] = col_sum(gkv_ref[:, width:].astype(F32))
    sum_ref[1:2] = col_sum(gcq_ref[...].astype(F32))


def cross_bwd(sel, g, cq, kv, lse, weights):
    rows, width = g.shape
    e_rows, heads = kv.shape[0], cq.shape[1]
    outs = [
        shape(rows, heads), shape(e_rows, 2 * heads),
        shape(rows // 2, width, dtype=F32), shape(rows // 2, width),
        shape(e_rows // 2, width, dtype=F32), shape(e_rows // 2, width),
        shape(2, heads, dtype=F32),
    ]
    return call(
        cross_bwd_body, outs, sel, g, cq, kv, lse, *weights,
        scratch=back_scratch(rows, heads),
    )


def gelu(pre):
    return 0.5 * pre * (1.0 + lax.erf(pre * (0.5 ** 0.5)))


def pick_ff(sel, section, weights):
    own1, near1, far1, own2, got2 = weights
    w1 = pick(sel, section, own1[...], near1[...], far1[...])
    return w1, choose(sel, section, own2[...], got2[...])


def ff_fwd_body(section, sel, h, own1, near1, far1, own2, got2, vown, vgot, u_ref, g_ref, pm_ref, po_ref):
    w1, w2 = pick_ff(sel, section, (own1, near1, far1, own2, got2))
    u = nn(h[...], w1) + vector(sel, section, (vown, vgot), FF)
    u_ref[...] = u
    g_ref[...] = gelu(u).astype(BF16)
    project_out(sel, g_ref, w2, pm_ref, po_ref, nt)


def ff_fwd(section, sel, h, weights, vecs):
    rows, width = h.shape
    hidden = weights[0].shape[-1]
    outs = [
        shape(rows, hidden, dtype=F32), shape(rows, hidden),
        shape(rows // 2, width, dtype=F32), shape(rows // 2, width),
    ]
    return call(functools.partial(ff_fwd_body, section), outs, sel, h, *weights, *vecs)


def ff_bwd_body(section, sel, g, u, own1, near1, far1, own2, got2, gp_ref, pm_ref, po_ref, sum_ref):
    w1, w2 = pick_ff(sel, section, (own1, near1, far1, own2, got2))
    pre = u[...]
    bell = jnp.exp(-0.5 * pre * pre) * 0.3989422804014327
    slope = 0.5 * (1.0 + lax.erf(pre * (0.5 ** 0.5))) + pre * bell
    low = (slope * nn(g[...], w2)).astype(BF16)
    gp_ref[...] = low
    sum_ref[...] = col_sum(low.astype(F32))
    project_out(sel, gp_ref, w1, pm_ref, po_ref, nt)


def ff_bwd(section, sel, g, u, weights):
    rows, width = g.shape
    hidden = weights[0].shape[-1]
    outs = [
        shape(rows, hidden), shape(rows // 2, width, dtype=F32), shape(rows // 2, width),
        shape(1, hidden, dtype=F32),
    ]
    return call(functools.partial(ff_bwd_body, section), outs, sel, g, u, *weights)


def ring_block(sel, count, step):
    return lax.rem(sel[7] + 2 * count - step - 2, count)


def product_blocks(left, right, out_ref, start):
    found = tn(left[...], right[...])
    size = out_ref.shape[1]
    for block in range(out_ref.shape[0]):
        part = found[block * size : (block + 1) * size].astype(BF16)
        out_ref[block, :, start : start + found.shape[1]] = part


def wgrad_body(cuts, sel, *refs):
    grad_ref, send_ref = refs[-2:]
    for place, start in enumerate(cuts):
        product_blocks(refs[2 * place], refs[2 * place + 1], grad_ref, start)
    send_ref[...] = grad_ref[ring_block(sel, grad_ref.shape[0], -1)]


def columns(pairs):
    cuts, at = [], 0
    for _, right in pairs:
        cuts.append(at)
        at += right.shape[1]
    return cuts, at


def wgrads(sel, count, *pairs):
    cuts, wide = columns(pairs)
    rows = pairs[0][0].shape[1] // count
    return call(
        functools.partial(wgrad_body, cuts), [shape(count, rows, wide), shape(rows, wide)], sel,
        *[entry for pair in pairs for entry in pair],
    )


def both_wgrad_body(e_cuts, d_cuts, sel, *refs):
    keep_ref, send_ref, other = refs[-3:]
    first = sel[0] == 0
    at = 2 * len(e_cuts)
    for place, start in enumerate(e_cuts):
        product_blocks(refs[2 * place], refs[2 * place + 1], keep_ref, start)
    for place, start in enumerate(d_cuts):
        product_blocks(refs[at + 2 * place], refs[at + 2 * place + 1], other, start)
    e, d = keep_ref[...], other[...]
    keep_ref[...] = jnp.where(first, e, d)
    send_ref[...] = jnp.where(first, d, e)


def both_wgrads(sel, count, e_pairs, d_pairs):
    e_cuts, wide = columns(e_pairs)
    d_cuts, _ = columns(d_pairs)
    out = shape(count, e_pairs[0][0].shape[1] // count, wide)
    return call(
        functools.partial(both_wgrad_body, e_cuts, d_cuts), [out, out], sel,
        *[entry for pair in (*e_pairs, *d_pairs) for entry in pair],
        scratch=[pltpu.VMEM(out.shape, BF16)],
    )


def second_body(sel, left, right, c, c_got, out_ref, send_ref):
    product_blocks(left, right, out_ref, 0)
    wide = right.shape[1]
    out_ref[:, :, wide:] = (c[...].astype(F32) + c_got[...].astype(F32)).astype(BF16)
    send_ref[...] = out_ref[ring_block(sel, out_ref.shape[0], -1)]


def second_and_cross(sel, left, right, c, c_got):
    count, rows, wide = c.shape
    wide += right.shape[1]
    return call(
        second_body, [shape(count, rows, wide), shape(rows, wide)], sel, left, right, c, c_got
    )


def join_body(sel, e, e_got, d, d_got, out_ref, send_ref):
    first = sel[0] == 0
    own = jnp.where(first, e[...], d[...]).astype(F32)
    got = jnp.where(first, e_got[...], d_got[...]).astype(F32)
    out_ref[...] = (own + got).astype(BF16)
    send_ref[...] = out_ref[ring_block(sel, out_ref.shape[0], -1)]


def joined(sel, e, e_got, d, d_got):
    return call(
        join_body, [shape(*e.shape), shape(*e.shape[1:])], sel, e, e_got, d, d_got
    )


def ring_body(step, sel, grads, got, out):
    block = grads[ring_block(sel, grads.shape[0], step)]
    out[...] = (got[...].astype(F32) + block.astype(F32)).astype(BF16)


class Ring:
    def __init__(self, sel, grads, send):
        self.sel, self.grads, self.step = sel, grads, 0
        self.running = send
        self.flying = next_clip(send)

    def advance(self, also=()):
        self.running = call(
            functools.partial(ring_body, self.step), [shape(*self.running.shape)],
            self.sel, self.grads, self.flying, also=also,
        )[0]
        self.step += 1
        if self.step < self.grads.shape[0] - 1:
            self.flying = next_clip(self.running)

    def finish(self):
        while self.step < self.grads.shape[0] - 1:
            self.advance()
        return self.running


def sides_body(sel, second, ff_d, send):
    first = sel[0] == 0
    width = ff_d.shape[1] // 2
    send[:, :width] = jnp.where(first, ff_d[:, :width], second[:, :width])
    send[:, width:] = ff_d[:, width:]


def finish_body(sel, second, ff_d, got, both, own, own_got, w1, w2, proj):
    first = sel[0] == 0
    width = both.shape[1]
    heads = proj.shape[3]
    mine = jnp.where(first, second[:, :width], ff_d[:, :width]).astype(F32)
    w2[0] = mine + got[:, :width].astype(F32)
    shared = both[...].astype(F32)
    w1[0] = jnp.where(first, shared, ff_d[:, width:].astype(F32) + got[:, width:].astype(F32))
    mine = jnp.where(first, own[...].astype(F32) + own_got[...].astype(F32), shared)
    for place in range(4):
        proj[0, place] = mine[:, place * heads : (place + 1) * heads]
    for place in range(2):
        start = width + place * heads
        proj[0, 4 + place] = second[:, start : start + heads].astype(F32)


def pack_sums_body(ey, ex1, ex, dz2, dz1, dz, wide):
    rows = (
        (ex, 0), (ey, 0), (ex1, 0), (ex, 1), (ey, 1), (ex1, 1), (ex1, 2), (ey, 2),
        (dz, 0), (dz1, 0), (dz2, 0), (dz, 1), (dz1, 1), (dz2, 1), (dz1, 2), (dz2, 3),
    )
    for at, (ref, row) in enumerate(rows):
        wide[at : at + 1] = ref[row : row + 1]


def pack_slim_body(wide, wide_got, self_e, self_d, cross, inner_e, inner_d, out):
    width = cross.shape[1]
    count = wide.shape[0]
    out[:count] = wide[...] + wide_got[...]
    out[count:] = jnp.zeros((out.shape[0] - count, out.shape[1]), F32)
    for at, (own, place, inner) in enumerate(((self_e, 0, inner_e), (self_d, 1, inner_d))):
        row = count + 2 * at
        out[row : row + 1, :width] = own[:, :width]
        out[row : row + 1, width : 2 * width] = own[:, 2 * width :]
        out[row : row + 1, 2 * width : 3 * width] = cross[place : place + 1]
        out[row + 1 : row + 2] = inner[...]


def more_body(left, right, out):
    out[...] = left[...] + right[...]


def more(left, right):
    return call(more_body, [shape(*left.shape, dtype=F32)], left, right)[0]


def unpack_body(sel, left, right, gain, row, col, inner):
    total = left[...] + right[...]
    first = sel[0] == 0
    wide = jnp.where(first, total[:8], total[8:16])
    gain[0] = wide[:3]
    row[0] = wide[3:]
    width = col.shape[2]
    for place in range(3):
        cut = slice(place * width, (place + 1) * width)
        col[0, place : place + 1] = jnp.where(first, total[16:17, cut], total[18:19, cut])
    inner[...] = jnp.where(first, total[17:18], total[19:20])


class Total:
    def __init__(self, entry):
        self.entry, self.step = entry, 1
        self.send()

    def send(self):
        size = lax.axis_size("clip")
        if self.step < size:
            pairs = [(i, i ^ self.step) for i in range(size)]
            self.flying = lax.ppermute(self.entry, "clip", pairs)

    def advance(self):
        self.entry = more(self.entry, self.flying)
        self.step *= 2
        self.send()

    def finish(self):
        while self.step < lax.axis_size("clip"):
            self.advance()
        return self.entry


def local(
    enc_in, dec_in, stamp_flags, dec_lengths, proj_w, fc_in, fc_out,
    col_bias, ff_bias, norm_gain, row_bias, enc_cot, dec_cot,
):
    ORDER[0] = None
    place = lax.axis_index("pipe")
    spot = lax.axis_index("head")
    parity = lax.axis_index("clip") % 2
    row, core = spot // 2, spot % 2
    sel = [place, parity, 2 * row, 2 - 2 * row, 2 * row + 1, 3 - 2 * row, core, lax.axis_index("clip")]
    sel = jnp.stack(sel).astype(jnp.int32)
    width = norm_gain.shape[-1]

    clips = lax.axis_size("clip")
    own = jnp.swapaxes(proj_w[0], 1, 2)
    half_a, half_b = split(sel, [own], [(0, 0, 2), (0, 2, 4)])
    near_a, near_b = swap_pipe(half_a), swap_pipe(half_b)
    vown = call(
        pack_body, [shape(16, width, dtype=F32)],
        norm_gain[0], row_bias[0], ff_bias, col_bias[0],
    )[0]
    vecs = (vown, swap_pipe(vown))
    e_block, block = enc_in.shape[1], dec_in.shape[1]
    in_own = take(sel, enc_in, dec_in)
    in_rows = (in_own, swap_row(in_own))
    x = (*in_rows, 0, e_block)
    z = (*in_rows, e_block, block)
    (half_1,) = split(sel, [fc_in], [(0, 0, 1)], also=(near_a,))
    far_a, near_1 = swap_pair(near_a), swap_pipe(half_1)
    h1 = both_cores(norm_in(ENC, sel, x, vecs, also=(far_a,)))
    (whole_2,) = split(sel, [fc_out], [(0, 0, 1)], also=(near_b,), parts=1)
    far_b, got_2 = swap_pair(near_b), swap_pipe(whole_2)
    self_w = (own, near_a, far_a, near_b, far_b)
    cot_own = take(sel, dec_cot, enc_cot)
    cot_rows = (cot_own, swap_row(cot_own))
    dec_cots = (*cot_rows, 0, block)
    enc_cots = (*cot_rows, block, e_block)
    t1 = both_cores(norm_in(DEC, sel, z, vecs))
    dec_rows = stacked(dec_cots)
    gbr_z2 = both_cores(dec_rows)
    mask = (stamp_flags, dec_lengths)

    qkv, a, lse, x_pm, po = self_fwd(ENC, sel, h1, self_w, vecs, (), also=(t1, near_1, dec_rows))
    far_1 = swap_pair(near_1)
    x_recv = both_cores(po)
    x_got = swap_row(add_low(sel, x_pm, x_recv))
    (whole_c,) = split(sel, [own], [(0, 4, 6)], parts=1)
    got_c = swap_pipe(whole_c)
    dqkv, da, dlse, z_pm, po = self_fwd(DEC, sel, t1, self_w, vecs, mask)
    z_recv = both_cores(po)
    z_got = swap_row(add_low(sel, z_pm, z_recv))
    x1, hm = res_norm(ENC, sel, x, (x_pm, x_recv, x_got), vecs, 3, 2, also=(far_1,))
    h2 = both_cores(hm)
    ff_w = (fc_in[0], near_1[0], far_1[0], fc_out[0], got_2[0])
    u, g, y_pm, po = ff_fwd(ENC, sel, h2, ff_w, vecs)
    y_recv = both_cores(po)
    cross_w = (own, got_c)
    y_got = swap_row(add_low(sel, y_pm, y_recv))
    z1, tm = res_norm(DEC, sel, z, (z_pm, z_recv, z_got), vecs, 3, 1)
    t2 = both_cores(tm)
    y, em = res_norm(ENC, sel, x1, (y_pm, y_recv, y_got), vecs, 4, 1, also=(t2, gbr_z2))
    e = both_cores(em)
    cq, kv, c, clse, z_pm, po = cross_fwd(sel, t2, e, cross_w, vecs)
    z_recv = both_cores(po)
    z_got = swap_row(add_low(sel, z_pm, z_recv))
    z2, tm = res_norm(DEC, sel, z1, (z_pm, z_recv, z_got), vecs, None, 2)
    t3 = both_cores(tm)
    w_pre, w, r_pm, ro = ff_fwd(DEC, sel, t3, ff_w, vecs)

    gp_d, z_pm, po, inner_d = ff_bwd(DEC, sel, gbr_z2, w_pre, ff_w)
    z_recv = both_cores(po)
    z_got = swap_row(add_low(sel, z_pm, z_recv))
    ring_ff_d = Ring(sel, *wgrads(sel, clips, (gbr_z2, w), (t3, gp_d)))
    r_recv = both_cores(ro)
    r_got = swap_row(add_low(sel, r_pm, r_recv, block))
    gz2, gm, sums_z2 = norm_back(DEC, sel, z2, dec_cots, (z_pm, z_recv, z_got), vecs, 2)
    gbr_c = both_cores(gm)
    gcq, gkv, z_pm, zo, y_pm, yo, sums_c = cross_bwd(sel, gbr_c, cq, kv, clse, cross_w)
    y_recv = both_cores(yo)
    y_got = swap_row(add_low(sel, y_pm, y_recv))
    ring_ff_d.advance()
    z_recv = both_cores(zo)
    z_got = swap_row(add_low(sel, z_pm, z_recv))
    cross, send = both_wgrads(sel, clips, [(e, gkv)], [(t2, gcq), (gbr_c, c)])
    cross_got = swap_pipe(send)
    keep_fwd, send_fwd = last_fwd(sel, y, z2, (r_pm, r_recv, r_got), vecs)
    gy, gm, sums_y = norm_back(ENC, sel, y, enc_cots, (y_pm, y_recv, y_got), vecs, 1)
    gbr_y = both_cores(gm)
    gp_e, x_pm, po, inner_e = ff_bwd(ENC, sel, gbr_y, u, ff_w)
    x_recv = both_cores(po)
    x_got = swap_row(add_low(sel, x_pm, x_recv))
    ring_ff_d.advance()
    got_fwd = swap_pipe(send_fwd)
    ff_1, _ = wgrads(sel, clips, (h2, gp_e))
    ff_1_got = to_section(ff_1, ENC)
    ring_2 = Ring(sel, *second_and_cross(sel, gbr_y, g, cross, cross_got))
    gz1, gm, sums_z1 = norm_back(DEC, sel, z1, gz2, (z_pm, z_recv, z_got), vecs, 1)
    gbr_z1 = both_cores(gm)
    gqkv_d, z_pm, po_d, self_d = self_bwd(DEC, sel, gbr_z1, dqkv, dlse, self_w, mask)
    own_d, _ = wgrads(sel, clips, (t1, gqkv_d), (gbr_z1, da))
    own_d_got = to_section(own_d, DEC)
    ff_d = ring_ff_d.finish()
    gx1, gm, sums_x1 = norm_back(ENC, sel, x1, gy, (x_pm, x_recv, x_got), vecs, 2)
    gbr_x1 = both_cores(gm)
    ring_2.advance()
    e_out, d_out = placed(sel, keep_fwd, got_fwd, e_block)
    gqkv_e, x_pm, po, self_e = self_bwd(ENC, sel, gbr_x1, qkv, lse, self_w, ())
    x_recv = both_cores(po)
    z_recv = both_cores(po_d)
    last_got = swap_row(add_last(sel, x_pm, x_recv, z_pm, z_recv))
    ring_2.advance()
    ring_own = Ring(sel, *wgrads(sel, clips, (h1, gqkv_e), (gbr_x1, a)))
    keep, send, sums_x, sums_z = last_back(
        sel, in_own, gx1, gz1, (x_pm, x_recv, z_pm, z_recv, last_got), vecs
    )
    got = swap_pipe(send)
    ring_1 = Ring(sel, *joined(sel, ff_1, ff_1_got, own_d, own_d_got))
    wide = call(
        pack_sums_body, [shape(16, width, dtype=F32)],
        sums_y, sums_x1, sums_x, sums_z2, sums_z1, sums_z,
    )[0]
    wide = more(wide, swap_core(wide))
    wide_got = swap_row(wide)
    ff_2 = ring_2.finish()
    side_got = swap_pipe(call(sides_body, [shape(*ff_d.shape)], sel, ff_2, ff_d)[0])
    ring_own.advance()
    total = Total(
        call(
            pack_slim_body, [shape(24, width, dtype=F32)],
            wide, wide_got, self_e, self_d, sums_c, inner_e, inner_d,
        )[0]
    )
    ring_1.advance()
    total.advance()
    ge_out, gd_out = placed(sel, keep, got, e_block)
    ring_own.advance()
    packed = total.finish()
    packed_got = swap_pipe(packed)
    ring_1.advance()
    heads = own.shape[1]
    out_gain, out_row, out_col, out_inner = call(
        unpack_body,
        [
            shape(1, 3, width, dtype=F32), shape(1, 5, width, dtype=F32),
            shape(1, 3, heads, dtype=F32), shape(1, ff_bias.shape[1], dtype=F32),
        ],
        sel, packed, packed_got,
    )
    own_e = ring_own.finish()
    own_e_got = to_section(own_e, ENC)
    both = ring_1.finish()
    hidden, cut = fc_in.shape[-1], both.shape[0]
    out_first, out_second, out_proj = call(
        finish_body,
        [
            shape(1, cut, hidden, dtype=F32),
            shape(1, cut, hidden, dtype=F32),
            shape(1, 6, cut, heads, dtype=F32),
        ],
        sel, ff_2, ff_d, side_got, both, own_e, own_e_got,
    )
    return (
        e_out,
        d_out,
        ge_out,
        gd_out,
        out_proj,
        out_first,
        out_second,
        out_col,
        out_inner,
        out_gain,
        out_row,
    )


def solution(mesh):
    return jax.shard_map(
        local,
        mesh=mesh,
        in_specs=(
            P("clip", "head", None),
            P("clip", "head", None),
            P("clip"),
            P("clip"),
            P("pipe", None, None, "head"),
            P("pipe", None, "head"),
            P("pipe", None, "head"),
            P("pipe", None, "head"),
            P("pipe", "head"),
            P("pipe", None, None),
            P("pipe", None, None),
            P("clip", "head", None),
            P("clip", "head", None),
        ),
        out_specs=(
            P("clip", "head", "pipe"),
            P("clip", "head", "pipe"),
            P("clip", "head", "pipe"),
            P("clip", "head", "pipe"),
            P("pipe", None, "clip", "head"),
            P("pipe", "clip", "head"),
            P("pipe", "clip", "head"),
            P("pipe", None, "head"),
            P("pipe", "head"),
            P("pipe", None, None),
            P("pipe", None, None),
        ),
        check_vma=False,
    )
```

```python
import functools

import jax
import jax.numpy as jnp
from jax import lax
from jax.experimental import pallas as pl
from jax.experimental.pallas import tpu as pltpu
from jax.sharding import PartitionSpec as P

HEAD_DIM = 64
DEC_SHORT = 224
SCALE = HEAD_DIM ** (-0.5)
SCALE_2 = SCALE * 1.4426950408889634
F32 = jnp.float32
BF16 = jnp.bfloat16
ENC, DEC = 0, 1

CORE_GROUPS = [[0, 1], [2, 3]]
CORE_PAIRS = [(0, 1), (1, 0), (2, 3), (3, 2)]
ROW_PAIRS = [(0, 2), (2, 0), (1, 3), (3, 1)]
PIPE_PAIRS = [(0, 1), (1, 0)]

GAIN, ROW, FF, COL = 0, 3, 8, 9


def both_cores(entry):
    return lax.all_gather(entry, "head", axis=0, axis_index_groups=CORE_GROUPS, tiled=True)


def swap_core(entry):
    return lax.ppermute(entry, "head", CORE_PAIRS)


def swap_row(entry):
    return lax.ppermute(entry, "head", ROW_PAIRS)


def swap_pipe(entry):
    return lax.ppermute(entry, "pipe", PIPE_PAIRS)


def swap_pair(entry):
    size = lax.axis_size("clip")
    return lax.ppermute(entry, "clip", [(i, i ^ 1) for i in range(size)])


def next_clip(entry):
    size = lax.axis_size("clip")
    return lax.ppermute(entry, "clip", [(i, (i + 1) % size) for i in range(size)])


def nn(left, right):
    return lax.dot_general(left, right, (((1,), (0,)), ((), ())), preferred_element_type=F32)


def nt(left, right):
    return lax.dot_general(left, right, (((1,), (1,)), ((), ())), preferred_element_type=F32)


def tn(left, right):
    return lax.dot_general(left, right, (((0,), (0,)), ((), ())), preferred_element_type=F32)


def shape(*dims, dtype=BF16):
    return jax.ShapeDtypeStruct(dims, dtype)


SCHEDULE = (
    "weights_self", "vectors", "rows_in", "weights_1", "norm_e", "weights_2", "rows_cot",
    "norm_d", "stack_d", "self_e", "add_x", "weights_c", "self_d", "add_z", "res_x1", "ff_e",
    "add_y", "res_z1", "res_y", "cross", "add_c", "res_z2", "ff_d", "ff_back_d", "add_gz2",
    "wgrad_ff_d", "add_r", "back_z2", "cross_back", "ring_ff_d", "add_gy", "add_gz1",
    "wgrad_cross", "outputs", "back_y", "ring_ff_d", "ff_back_e", "add_gx1", "wgrad_first",
    "wgrad_second", "back_z1", "self_back_d", "wgrad_own_d", "ring_ff_d", "ring_2", "back_x1",
    "place_outputs", "self_back_e", "ring_2", "add_last_both", "wgrad_own_e", "ring_2", "join",
    "inputs", "vec_core", "ring_own", "vec_row", "vec_pipe", "ring_1", "place_inputs", "vec_clip",
    "side_1", "ring_own", "ring_1", "vec_half", "side_2", "ring_1", "unpack",
)
RINGS = ("ring_ff_d", "ring_2", "ring_own", "ring_1")
QUICK = ('self_back_d',)
ALSO = {}
ORDER = [None]
COST = dict(
    self_fwd=3.4, self_bwd=4.8, cross_fwd=3.5, cross_bwd=5.4, ff_fwd=2.4, ff_bwd=2.8, wgrad=1.7,
    both_wgrad=1.7, norm_in=0.8, res_norm=0.9, norm_back=1.2, take=1.2, last_back=1.2,
    join_two=1.9, finish=2.5, place=1.3,
)


def call(body, outs, *ins, flops=0, limit=12, scratch=(), anywhere=(), out_anywhere=False, also=()):
    vmem = pl.BlockSpec(memory_space=pltpu.VMEM)
    smem = pl.BlockSpec(memory_space=pltpu.SMEM)
    any_space = pl.BlockSpec(memory_space=pl.ANY)
    hbm = pl.BlockSpec(memory_space=pltpu.HBM)
    specs = [
        hbm if place in anywhere else smem if a.dtype == jnp.int32 else vmem
        for place, a in enumerate(ins)
    ]
    count = len(ins)
    before = (*(() if ORDER[0] is None else (ORDER[0],)), *also)

    def ordered(*refs):
        body(*refs[:count], *refs[count + len(before) :])

    name = getattr(body, "func", body).__name__[:-5]
    found = pl.pallas_call(
        ordered,
        name=name,
        out_shape=outs,
        in_specs=[*specs, *[any_space] * len(before)],
        out_specs=[hbm if out_anywhere else vmem] * len(outs),
        scratch_shapes=scratch,
        compiler_params=pltpu.CompilerParams(vmem_limit_bytes=limit << 20),
        cost_estimate=pl.CostEstimate(
            flops=int(COST.get(name, 0.6) * 1.15e9), bytes_accessed=1, transcendentals=0
        ),
    )(*ins, *before)
    ORDER[0] = found[-1]
    return found


def pick(sel, section, own, near, far):
    is_own = sel[0] == section
    even = sel[1] == 0
    half = near.shape[0]
    top = jnp.where(is_own, own[:half], jnp.where(even, near, far))
    bottom = jnp.where(is_own, own[half:], jnp.where(even, far, near))
    return jnp.concatenate([top, bottom])


def choose(sel, section, own, got):
    return jnp.where(sel[0] == section, own, got)


def vector(sel, section, vecs, row, width=None):
    own, got = vecs
    cut = slice(0, width if width else own.shape[1])
    return jnp.where(sel[0] == section, own[row : row + 1, cut], got[row : row + 1, cut])


def norm_parts(rows):
    centered = rows - jnp.mean(rows, axis=-1, keepdims=True)
    variance = jnp.mean(centered * centered, axis=-1, keepdims=True)
    inverse = lax.rsqrt(variance + 1e-05)
    return centered * inverse, inverse


def take_body(count, sel, *refs):
    out, sems = refs[-2:]
    copies, at = [], 0
    for i in range(count):
        rows = refs[i].shape[1]
        copies.append(
            pltpu.make_async_copy(refs[i].at[sel[0]], out.at[at : at + rows], sems.at[i])
        )
        at += rows
    for copy in copies:
        copy.start()
    for copy in copies:
        copy.wait()


def take(sel, *arrays, limit=12, also=()):
    count = len(arrays)
    rows = sum(a.shape[1] for a in arrays)
    return call(
        functools.partial(take_body, count), [shape(rows, arrays[0].shape[2])], sel, *arrays,
        anywhere=range(1, 1 + count), scratch=[pltpu.SemaphoreType.DMA((count,))], limit=limit,
        also=also,
    )[0]


def split_body(cuts, sel, *refs):
    count = max(source for source, _, _ in cuts) + 1
    sems = refs[-1]
    copies = []
    for place, (source, start, stop) in enumerate(cuts):
        out = refs[count + place]
        half = out.shape[1]
        rows = pl.ds(pl.multiple_of(sel[1] * half, half), half)
        if half == refs[source].shape[1]:
            rows = slice(None)
        copies.append(
            pltpu.make_async_copy(refs[source].at[start:stop, rows], out, sems.at[place])
        )
    for copy in copies:
        copy.start()
    for copy in copies:
        copy.wait()


def split(sel, arrays, cuts, also=(), limit=12, parts=2):
    outs = [
        shape(stop - start, arrays[source].shape[1] // parts, arrays[source].shape[2])
        for source, start, stop in cuts
    ]
    return call(
        functools.partial(split_body, cuts), outs, sel, *arrays,
        anywhere=range(1, 1 + len(arrays)), out_anywhere=True,
        scratch=[pltpu.SemaphoreType.DMA((len(cuts),))], also=also, limit=limit,
    )


def pack_body(gain, row, ff, col, out):
    out[...] = jnp.zeros_like(out)
    out[GAIN : GAIN + 3] = gain[...]
    out[ROW : ROW + 5] = row[...]
    out[FF : FF + 1] = ff[...]
    out[COL : COL + 3, : col.shape[1]] = col[...]


def from_other(sel, pm, recv):
    return (1 - sel[6]) * (recv.shape[0] - pm.shape[0])


def add_body(start, sel, pm, recv, low):
    count = low.shape[0]
    there = pl.ds(pl.multiple_of(from_other(sel, pm, recv) + start, count), count)
    low[...] = (pm[start : start + count] + recv[there].astype(F32)).astype(BF16)


def add_low(sel, pm, recv, start=0, also=()):
    rows, width = pm.shape
    return call(
        functools.partial(add_body, start), [shape(rows - start, width)], sel, pm, recv, also=also
    )[0]


def add_last_body(sel, xm, zm, xr, zr, low):
    at = 0
    for pm, recv in ((xm, xr), (zm, zr)):
        count = pm.shape[0] // 2
        there = pl.ds(pl.multiple_of(from_other(sel, pm, recv) + count, count), count)
        low[at : at + count] = (pm[count:] + recv[there].astype(F32)).astype(BF16)
        at += count


def add_last(sel, xm, zm, xr, zr):
    rows = (xm.shape[0] + zm.shape[0]) // 2
    return call(add_last_body, [shape(rows, xm.shape[1])], sel, xm, zm, xr, zr)[0]


def stack_body(start, block, own, got, out):
    out[:block] = own[start : start + block]
    out[block:] = got[start : start + block]


def stacked(rows):
    own, got, start, block = rows
    return call(
        functools.partial(stack_body, start, block), [shape(2 * block, own.shape[1])], own, got
    )[0]


def norm_in_body(section, at, sel, own, got, vown, vgot, hm_ref):
    gain = vector(sel, section, (vown, vgot), GAIN)
    bias = vector(sel, section, (vown, vgot), ROW)
    block = hm_ref.shape[0] // 2
    for start, part in ((0, own), (block, got)):
        unit, _ = norm_parts(part[at : at + block].astype(F32))
        hm_ref[start : start + block] = (unit * gain + bias).astype(BF16)


def norm_in(section, sel, rows, vecs, also=()):
    own, got, start, block = rows
    return call(
        functools.partial(norm_in_body, section, start), [shape(2 * block, own.shape[1])],
        sel, own, got, *vecs, also=also,
    )[0]


def summed(sel, pm, recv, got, rows, other):
    block = rows.stop - rows.start
    there = pl.ds(pl.multiple_of(from_other(sel, pm, recv) + rows.start, block), block)
    return pm[rows] + recv[there].astype(F32) + got[other].astype(F32)


def halves(block):
    return ((slice(0, block), slice(block, 2 * block)), (slice(block, 2 * block), slice(0, block)))


def res_norm_body(section, out_row, index, at, *refs):
    split = at is not None
    sel = refs[0]
    res = refs[1 : 3 if split else 2]
    pm, recv, got, vown, vgot, x_ref, hm_ref = refs[3 if split else 2 :]
    vecs = (vown, vgot)
    gain = vector(sel, section, vecs, GAIN + index)
    bias = vector(sel, section, vecs, ROW + index)
    block = pm.shape[0] // 2
    for place, (rows, other) in enumerate(halves(block)):
        base = res[place][at : at + block].astype(F32) if split else res[0][rows]
        now = base + summed(sel, pm, recv, got, rows, other)
        if out_row is not None:
            now = now + vector(sel, section, vecs, ROW + out_row)
        x_ref[rows] = now
        unit, _ = norm_parts(now)
        hm_ref[rows] = (unit * gain + bias).astype(BF16)


def res_norm(section, sel, res, sums, vecs, out_row, index, also=()):
    rows, width = sums[0].shape
    at, res = (res[2], res[:2]) if isinstance(res, tuple) else (None, (res,))
    return call(
        functools.partial(res_norm_body, section, out_row, index, at),
        [shape(rows, width, dtype=F32), shape(rows, width)],
        sel, *res, *sums, *vecs, also=also,
    )


def norm_grad(rows, gain, grad):
    unit, inverse = norm_parts(rows)
    scaled = grad * gain
    back = inverse * (
        scaled
        - jnp.mean(scaled, axis=-1, keepdims=True)
        - unit * jnp.mean(scaled * unit, axis=-1, keepdims=True)
    )
    return back, unit


def col_sum(entry):
    return jnp.sum(entry, axis=0, keepdims=True)


def norm_back_body(section, index, at, *refs):
    split = at is not None
    sel, x = refs[:2]
    res = refs[2 : 4 if split else 3]
    pm, recv, got, vown, vgot, g_ref, gm_ref, sum_ref = refs[4 if split else 3 :]
    gain = vector(sel, section, (vown, vgot), GAIN + index)
    block = pm.shape[0] // 2
    for place, (rows, other) in enumerate(halves(block)):
        grad = summed(sel, pm, recv, got, rows, other)
        base = res[place][at : at + block].astype(F32) if split else res[0][rows]
        back, unit = norm_grad(x[rows], gain, grad)
        now = base + back
        g_ref[rows] = now
        gm_ref[rows] = now.astype(BF16)
        if place == 0:
            sum_ref[0:1] = col_sum(grad * unit)
            sum_ref[1:2] = col_sum(grad)
            sum_ref[2:3] = col_sum(now)
            sum_ref[3:4] = col_sum(base)


def norm_back(section, sel, x, res, sums, vecs, index, also=()):
    rows, width = x.shape
    at, res = (res[2], res[:2]) if isinstance(res, tuple) else (None, (res,))
    return call(
        functools.partial(norm_back_body, section, index, at),
        [shape(rows, width, dtype=F32), shape(rows, width), shape(4, width, dtype=F32)],
        sel, x, *res, *sums, *vecs, also=also,
    )


def send_halves(sel, rows, low, keep_ref, send_ref):
    width = low.shape[1] // 2
    left, right = low[:, :width], low[:, width:]
    keep_ref[rows] = jnp.where(sel[0] == 0, left, right)
    send_ref[rows] = jnp.where(sel[0] == 0, right, left)


def last_fwd_body(sel, y, z2, pm, recv, got, vown, vgot, keep_ref, send_ref):
    block = got.shape[0]
    e_block = y.shape[0] // 2
    rows = slice(0, block)
    r = z2[rows] + summed(sel, pm, recv, got, rows, rows)
    r = r + vector(sel, DEC, (vown, vgot), ROW + 4)
    send_halves(sel, slice(0, e_block), y[:e_block].astype(BF16), keep_ref, send_ref)
    send_halves(sel, slice(e_block, e_block + block), r.astype(BF16), keep_ref, send_ref)


def last_fwd(sel, y, z2, sums, vecs):
    rows = y.shape[0] // 2 + sums[2].shape[0]
    width = y.shape[1] // 2
    return call(
        last_fwd_body, [shape(rows, width), shape(rows, width)], sel, y, z2, *sums, *vecs
    )


def last_back_body(
    sel, rows_in, gx1, gz1, xm, zm, xr, zr, all_got, vown, vgot,
    keep_ref, send_ref, sum_x, sum_z,
):
    vecs = (vown, vgot)
    start = 0
    for section, res, pm, recv, out in ((ENC, gx1, xm, xr, sum_x), (DEC, gz1, zm, zr, sum_z)):
        gain = vector(sel, section, vecs, GAIN)
        block = pm.shape[0] // 2
        rows = slice(0, block)
        grad = summed(sel, pm, recv, all_got, rows, slice(start, start + block))
        back, unit = norm_grad(rows_in[start : start + block].astype(F32), gain, grad)
        low = (res[rows] + back).astype(BF16)
        send_halves(sel, slice(start, start + block), low, keep_ref, send_ref)
        out[0:1] = col_sum(grad * unit)
        out[1:2] = col_sum(grad)
        start += block


def last_back(sel, rows_in, gx1, gz1, sums, vecs):
    rows, width = rows_in.shape
    return call(
        last_back_body,
        [
            shape(rows, width // 2), shape(rows, width // 2),
            shape(2, width, dtype=F32), shape(2, width, dtype=F32),
        ],
        sel, rows_in, gx1, gz1, *sums, *vecs,
    )


def place_body(sel, keep, got, *outs):
    start = 0
    for ref in outs:
        rows = slice(start, start + ref.shape[1])
        ref[0] = jnp.where(sel[0] == 0, keep[rows], got[rows])
        ref[1] = jnp.where(sel[0] == 0, got[rows], keep[rows])
        start += ref.shape[1]


def placed(sel, keep, got, block):
    rows, width = keep.shape
    return call(
        place_body, [shape(2, block, width), shape(2, rows - block, width)], sel, keep, got
    )


def places(sel, axis, dims):
    at = lax.broadcasted_iota(jnp.int32, dims, axis)
    size = dims[axis] // 4
    shift = sel[5] - 3
    for block in (2, 1, 0):
        shift = jnp.where(at < (block + 1) * size, sel[2 + block] - block, shift)
    return at + shift * size


def text_length(sel, flags, lengths):
    return jnp.minimum(lengths[sel[0]], DEC_SHORT * (1 + flags[sel[0]]))


def allowed(sel, flags, lengths, rows, key_axis):
    shapes = ((1, rows), (rows, 1)) if key_axis == 1 else ((rows, 1), (1, rows))
    keys = places(sel, key_axis, shapes[0])
    keys = jnp.where(keys < text_length(sel, flags, lengths), keys, rows)
    return keys <= places(sel, 1 - key_axis, shapes[1])


def attend(q_ref, q_at, kv_ref, k_at, v_at, mask, a_ref, lse_ref):
    rows, width = a_ref.shape
    ones = jnp.ones((kv_ref.shape[0], HEAD_DIM), BF16)
    if mask:
        keep = allowed(*mask, rows, 1)
    for head in range(width // HEAD_DIM):
        cut = slice(head * HEAD_DIM, (head + 1) * HEAD_DIM)
        k_head = kv_ref[:, k_at + cut.start : k_at + cut.stop]
        v_head = kv_ref[:, v_at + cut.start : v_at + cut.stop]
        scores = nt(q_ref[:, q_at + cut.start : q_at + cut.stop], k_head)
        if mask:
            scores = jnp.where(keep, scores, -1e30)
        top = jnp.max(scores, axis=-1, keepdims=True)
        low = jnp.exp2((scores - top) * SCALE_2).astype(BF16)
        both = nn(low, jnp.concatenate([v_head, ones], axis=1))
        total = both[:, HEAD_DIM : HEAD_DIM + 1]
        a_ref[:, cut] = (both[:, :HEAD_DIM] * (1.0 / total)).astype(BF16)
        lse_ref[:, head : head + 1] = top * SCALE_2 + jnp.log2(total)


def attend_back(
    q_ref, q_at, kv_ref, k_at, v_at, grad, lse, mask, gq_ref, gq_at, gkv_ref, gk_at, gv_at,
    rows_ref,
):
    rows, width = grad.shape
    rows_ref[:, : lse.shape[1]] = lse[...]
    sums = rows_ref[...].T
    if mask:
        keep = allowed(*mask, rows, 0)
    for head in range(width // HEAD_DIM):
        cut = slice(head * HEAD_DIM, (head + 1) * HEAD_DIM)
        q_head = q_ref[:, q_at + cut.start : q_at + cut.stop]
        o_head = grad[:, cut]
        k_head = kv_ref[:, k_at + cut.start : k_at + cut.stop]
        v_head = kv_ref[:, v_at + cut.start : v_at + cut.stop]
        scores = nt(k_head, q_head)
        if mask:
            scores = jnp.where(keep, scores, -1e30)
        weights = jnp.exp2(scores * SCALE_2 - sums[head : head + 1])
        both = weights * nt(v_head, o_head)
        grad_s = (both - weights * jnp.sum(both, axis=0, keepdims=True)).astype(BF16)
        gv = nn(weights.astype(BF16), o_head)
        gk = nn(grad_s, q_head) * SCALE
        gq = tn(grad_s, k_head) * SCALE
        gkv_ref[:, gk_at + cut.start : gk_at + cut.stop] = gk.astype(BF16)
        gkv_ref[:, gv_at + cut.start : gv_at + cut.stop] = gv.astype(BF16)
        gq_ref[:, gq_at + cut.start : gq_at + cut.stop] = gq.astype(BF16)


def halves_of(sel, half):
    mine = pl.ds(pl.multiple_of(sel[6] * half, half), half)
    other = pl.ds(pl.multiple_of((1 - sel[6]) * half, half), half)
    return mine, other


def project_out(sel, mixed_ref, weight, pm_ref, po_ref, by=nn):
    mine, other = halves_of(sel, pm_ref.shape[0])
    pm_ref[...] = by(mixed_ref[mine], weight)
    po_ref[...] = by(mixed_ref[other], weight).astype(BF16)


def self_fwd_body(section, masked, *refs):
    sel, h, own, near_a, far_a, near_b, far_b, vown, vgot = refs[:9]
    mask = (sel, *refs[9:11]) if masked else None
    qkv_ref, a_ref, lse_ref, pm_ref, po_ref = refs[11 if masked else 9 :]
    width = a_ref.shape[1]
    wq = pick(sel, section, own[0], near_a[0], far_a[0])
    wk = pick(sel, section, own[1], near_a[1], far_a[1])
    wv = pick(sel, section, own[2], near_b[0], far_b[0])
    bq = vector(sel, section, (vown, vgot), COL, width)
    bv = vector(sel, section, (vown, vgot), COL + 1, width)
    rows = h[...]
    qkv_ref[:, :width] = (nt(rows, wq) + bq).astype(BF16)
    qkv_ref[:, width : 2 * width] = nt(rows, wk).astype(BF16)
    qkv_ref[:, 2 * width :] = (nt(rows, wv) + bv).astype(BF16)
    attend(qkv_ref, 0, qkv_ref, width, 2 * width, mask, a_ref, lse_ref)
    wo = pick(sel, section, own[3], near_b[1], far_b[1])
    project_out(sel, a_ref, wo, pm_ref, po_ref)


def self_fwd(section, sel, h, weights, vecs, mask, also=()):
    rows, width = h.shape
    heads = weights[0].shape[1]
    outs = [
        shape(rows, 3 * heads), shape(rows, heads), shape(rows, heads // HEAD_DIM, dtype=F32),
        shape(rows // 2, width, dtype=F32), shape(rows // 2, width),
    ]
    return call(
        functools.partial(self_fwd_body, section, bool(mask)), outs, sel, h, *weights, *vecs, *mask,
        also=also,
    )


def back_scratch(rows, heads):
    return [pltpu.VMEM((rows, heads), BF16), pltpu.VMEM((rows, 128), F32)]


def self_bwd_body(section, masked, *refs):
    sel, g, qkv, lse, own, near_a, far_a, near_b, far_b = refs[:9]
    refs = refs[9:]
    mask, refs = ((sel, *refs[:2]), refs[2:]) if masked else (None, refs)
    gqkv_ref, pm_ref, po_ref, sum_ref, ga, spare = refs
    width = ga.shape[1]
    wo = pick(sel, section, own[3], near_b[1], far_b[1])
    ga[...] = nt(g[...], wo).astype(BF16)
    attend_back(
        qkv, 0, qkv, width, 2 * width, ga, lse, mask,
        gqkv_ref, 0, gqkv_ref, width, 2 * width, spare,
    )
    weight = jnp.concatenate(
        [
            pick(sel, section, own[0], near_a[0], far_a[0]),
            pick(sel, section, own[1], near_a[1], far_a[1]),
            pick(sel, section, own[2], near_b[0], far_b[0]),
        ]
    )
    project_out(sel, gqkv_ref, weight, pm_ref, po_ref)
    sum_ref[...] = col_sum(gqkv_ref[...].astype(F32))


def self_bwd(section, sel, g, qkv, lse, weights, mask, also=()):
    rows, width = g.shape
    heads = weights[0].shape[1]
    outs = [
        shape(rows, 3 * heads), shape(rows // 2, width, dtype=F32),
        shape(rows // 2, width), shape(1, 3 * heads, dtype=F32),
    ]
    return call(
        functools.partial(self_bwd_body, section, bool(mask)), outs, sel, g, qkv, lse,
        *weights, *mask, scratch=back_scratch(rows, heads), also=also,
    )


def cross_fwd_body(
    sel, t, e, own, got, vown, vgot, cq_ref, kv_ref, c_ref, lse_ref, pm_ref, po_ref
):
    width = cq_ref.shape[1]
    vecs = (vown, vgot)
    w4 = choose(sel, ENC, own[4], got[0])
    w5 = choose(sel, ENC, own[5], got[1])
    rows = e[...]
    kv_ref[:, :width] = nt(rows, w4).astype(BF16)
    kv_ref[:, width:] = (nt(rows, w5) + vector(sel, ENC, vecs, COL + 2, width)).astype(BF16)
    wq = choose(sel, DEC, own[4], got[0])
    cq_ref[...] = (nt(t[...], wq) + vector(sel, DEC, vecs, COL + 2, width)).astype(BF16)
    attend(cq_ref, 0, kv_ref, 0, width, None, c_ref, lse_ref)
    wo = choose(sel, DEC, own[5], got[1])
    project_out(sel, c_ref, wo, pm_ref, po_ref)


def cross_fwd(sel, t, e, weights, vecs, also=()):
    rows, width = t.shape
    e_rows, heads = e.shape[0], weights[0].shape[1]
    outs = [
        shape(rows, heads), shape(e_rows, 2 * heads), shape(rows, heads),
        shape(rows, heads // HEAD_DIM, dtype=F32), shape(rows // 2, width, dtype=F32),
        shape(rows // 2, width),
    ]
    return call(cross_fwd_body, outs, sel, t, e, *weights, *vecs, also=also)


def cross_bwd_body(
    sel, g, cq, kv, lse, own, got,
    gcq_ref, gkv_ref, pm_ref, po_ref, em_ref, eo_ref, sum_ref, gc, spare,
):
    width = cq.shape[1]
    wo = choose(sel, DEC, own[5], got[1])
    gc[...] = nt(g[...], wo).astype(BF16)
    attend_back(
        cq, 0, kv, 0, width, gc, lse, None, gcq_ref, 0, gkv_ref, 0, width, spare
    )
    weight = jnp.concatenate(
        [
            choose(sel, ENC, own[4], got[0]),
            choose(sel, ENC, own[5], got[1]),
        ]
    )
    project_out(sel, gkv_ref, weight, em_ref, eo_ref)
    project_out(sel, gcq_ref, choose(sel, DEC, own[4], got[0]), pm_ref, po_ref)
    sum_ref[0:1] = col_sum(gkv_ref[:, width:].astype(F32))
    sum_ref[1:2] = col_sum(gcq_ref[...].astype(F32))


def cross_bwd(sel, g, cq, kv, lse, weights, also=()):
    rows, width = g.shape
    e_rows, heads = kv.shape[0], cq.shape[1]
    outs = [
        shape(rows, heads), shape(e_rows, 2 * heads),
        shape(rows // 2, width, dtype=F32), shape(rows // 2, width),
        shape(e_rows // 2, width, dtype=F32), shape(e_rows // 2, width),
        shape(2, heads, dtype=F32),
    ]
    return call(
        cross_bwd_body, outs, sel, g, cq, kv, lse, *weights,
        scratch=back_scratch(rows, heads), also=also,
    )


def gelu(pre):
    return 0.5 * pre * (1.0 + lax.erf(pre * (0.5 ** 0.5)))


def pick_ff(sel, section, weights):
    own1, near1, far1, own2, got2 = weights
    w1 = pick(sel, section, own1[...], near1[...], far1[...])
    return w1, choose(sel, section, own2[...], got2[...])


def ff_fwd_body(section, sel, h, own1, near1, far1, own2, got2, vown, vgot, u_ref, g_ref, pm_ref, po_ref):
    w1, w2 = pick_ff(sel, section, (own1, near1, far1, own2, got2))
    u = nn(h[...], w1) + vector(sel, section, (vown, vgot), FF)
    u_ref[...] = u
    g_ref[...] = gelu(u).astype(BF16)
    project_out(sel, g_ref, w2, pm_ref, po_ref, nt)


def ff_fwd(section, sel, h, weights, vecs, also=()):
    rows, width = h.shape
    hidden = weights[0].shape[-1]
    outs = [
        shape(rows, hidden, dtype=F32), shape(rows, hidden),
        shape(rows // 2, width, dtype=F32), shape(rows // 2, width),
    ]
    return call(functools.partial(ff_fwd_body, section), outs, sel, h, *weights, *vecs, also=also)


def ff_bwd_body(section, sel, g, u, own1, near1, far1, own2, got2, gp_ref, pm_ref, po_ref, sum_ref):
    w1, w2 = pick_ff(sel, section, (own1, near1, far1, own2, got2))
    pre = u[...]
    bell = jnp.exp(-0.5 * pre * pre) * 0.3989422804014327
    slope = 0.5 * (1.0 + lax.erf(pre * (0.5 ** 0.5))) + pre * bell
    low = (slope * nn(g[...], w2)).astype(BF16)
    gp_ref[...] = low
    sum_ref[...] = col_sum(low.astype(F32))
    project_out(sel, gp_ref, w1, pm_ref, po_ref, nt)


def ff_bwd(section, sel, g, u, weights, also=()):
    rows, width = g.shape
    hidden = weights[0].shape[-1]
    outs = [
        shape(rows, hidden), shape(rows // 2, width, dtype=F32), shape(rows // 2, width),
        shape(1, hidden, dtype=F32),
    ]
    return call(functools.partial(ff_bwd_body, section), outs, sel, g, u, *weights, also=also)


def ring_block(sel, count, step):
    return lax.rem(sel[7] + 2 * count - step - 2, count)


def product_blocks(left, right, out_ref, start):
    found = tn(left[...], right[...])
    size = out_ref.shape[1]
    for block in range(out_ref.shape[0]):
        part = found[block * size : (block + 1) * size].astype(BF16)
        out_ref[block, :, start : start + found.shape[1]] = part


def wgrad_body(cuts, sel, *refs):
    grad_ref, send_ref = refs[-2:]
    for place, start in enumerate(cuts):
        product_blocks(refs[2 * place], refs[2 * place + 1], grad_ref, start)
    send_ref[...] = grad_ref[ring_block(sel, grad_ref.shape[0], -1)]


def columns(pairs):
    cuts, at = [], 0
    for _, right in pairs:
        cuts.append(at)
        at += right.shape[1]
    return cuts, at


def wgrads(sel, count, *pairs, also=()):
    cuts, wide = columns(pairs)
    rows = pairs[0][0].shape[1] // count
    return call(
        functools.partial(wgrad_body, cuts), [shape(count, rows, wide), shape(rows, wide)], sel,
        *[entry for pair in pairs for entry in pair], also=also,
    )


def both_wgrad_body(e_cuts, d_cuts, sel, *refs):
    keep_ref, send_ref, other = refs[-3:]
    first = sel[0] == 0
    at = 2 * len(e_cuts)
    for place, start in enumerate(e_cuts):
        product_blocks(refs[2 * place], refs[2 * place + 1], keep_ref, start)
    for place, start in enumerate(d_cuts):
        product_blocks(refs[at + 2 * place], refs[at + 2 * place + 1], other, start)
    e, d = keep_ref[...], other[...]
    keep_ref[...] = jnp.where(first, e, d)
    send_ref[...] = jnp.where(first, d, e)


def both_wgrads(sel, count, e_pairs, d_pairs):
    e_cuts, wide = columns(e_pairs)
    d_cuts, _ = columns(d_pairs)
    out = shape(count, e_pairs[0][0].shape[1] // count, wide)
    return call(
        functools.partial(both_wgrad_body, e_cuts, d_cuts), [out, out], sel,
        *[entry for pair in (*e_pairs, *d_pairs) for entry in pair],
        scratch=[pltpu.VMEM(out.shape, BF16)],
    )


def second_body(sel, left, right, c, c_got, out_ref, send_ref):
    product_blocks(left, right, out_ref, 0)
    wide = right.shape[1]
    out_ref[:, :, wide:] = (c[...].astype(F32) + c_got[...].astype(F32)).astype(BF16)
    send_ref[...] = out_ref[ring_block(sel, out_ref.shape[0], -1)]


def second_and_cross(sel, left, right, c, c_got):
    count, rows, wide = c.shape
    wide += right.shape[1]
    return call(
        second_body, [shape(count, rows, wide), shape(rows, wide)], sel, left, right, c, c_got
    )


def first_and_own_body(starts, sel, other, *refs):
    keep_ref, send_ref = refs[-2:]
    for place, start in enumerate(starts):
        product_blocks(refs[2 * place], refs[2 * place + 1], keep_ref, start)
    first = sel[0] == 0
    d, e = keep_ref[...], other[...]
    keep_ref[...] = jnp.where(first, e, d)
    send_ref[...] = jnp.where(first, d, e)


def first_and_own(sel, first, *pairs):
    starts, _ = columns(pairs)
    return call(
        functools.partial(first_and_own_body, starts), [shape(*first.shape)] * 2, sel, first,
        *[entry for pair in pairs for entry in pair],
    )


def join_body(sel, keep, got, out_ref, send_ref):
    out_ref[...] = (keep[...].astype(F32) + got[...].astype(F32)).astype(BF16)
    send_ref[...] = out_ref[ring_block(sel, out_ref.shape[0], -1)]


def joined(sel, keep, got):
    return call(join_body, [shape(*keep.shape), shape(*keep.shape[1:])], sel, keep, got)


def ring_body(step, sel, grads, got, out):
    block = grads[ring_block(sel, grads.shape[0], step)]
    out[...] = (got[...].astype(F32) + block.astype(F32)).astype(BF16)


class Ring:
    def __init__(self, sel, grads, send):
        self.sel, self.grads, self.step = sel, grads, 0
        self.running = send
        self.flying = next_clip(send)

    def advance(self, also=()):
        self.running = call(
            functools.partial(ring_body, self.step), [shape(*self.running.shape)],
            self.sel, self.grads, self.flying, also=also,
        )[0]
        self.step += 1
        if self.step < self.grads.shape[0] - 1:
            self.flying = next_clip(self.running)

    def finish(self):
        while self.step < self.grads.shape[0] - 1:
            self.advance()
        return self.running


def side_body(at, sel, e, d, send):
    width = send.shape[1]
    send[...] = jnp.where(sel[0] == 0, d[:, at : at + width], e[:, :width])


def side(sel, e, d, at):
    width = d.shape[1] // 2
    return call(functools.partial(side_body, at), [shape(d.shape[0], width)], sel, e, d)[0]


def finish_body(sel, second, ff_d, got, both, own, own_got, w1, w2, proj):
    first = sel[0] == 0
    width = both.shape[1]
    heads = proj.shape[3]
    mine = jnp.where(first, second[:, :width], ff_d[:, :width]).astype(F32)
    w2[0] = mine + got[...].astype(F32)
    shared = both[...].astype(F32)
    mine = jnp.where(first, own[...], ff_d[:, width:]).astype(F32) + own_got[...].astype(F32)
    w1[0] = jnp.where(first, shared, mine)
    mine = jnp.where(first, mine, shared)
    for place in range(4):
        proj[0, place] = mine[:, place * heads : (place + 1) * heads]
    for place in range(2):
        start = width + place * heads
        proj[0, 4 + place] = second[:, start : start + heads].astype(F32)


def pack_sums_body(ey, ex1, ex, dz2, dz1, dz, wide):
    rows = (
        (ex, 0), (ey, 0), (ex1, 0), (ex, 1), (ey, 1), (ex1, 1), (ex1, 2), (ey, 2),
        (dz, 0), (dz1, 0), (dz2, 0), (dz, 1), (dz1, 1), (dz2, 1), (dz1, 2), (dz2, 3),
    )
    for at, (ref, row) in enumerate(rows):
        wide[at : at + 1] = ref[row : row + 1]


def pack_slim_body(sel, wide, got, self_e, self_d, cross, inner_e, inner_d, keep, send):
    first = sel[0] == 0
    width = cross.shape[1]
    total = wide[...] + got[...]
    e, d = total[:8], total[8:]
    keep[...] = jnp.zeros_like(keep)
    send[...] = jnp.zeros_like(send)
    keep[:8] = jnp.where(first, e, d)
    send[:8] = jnp.where(first, d, e)
    pairs = [
        (self_e[:, :width], self_d[:, :width]),
        (self_e[:, 2 * width :], self_d[:, 2 * width :]),
        (cross[0:1], cross[1:2]),
    ]
    for at, (e, d) in enumerate(pairs):
        keep[8:9, at * width : (at + 1) * width] = jnp.where(first, e, d)
        send[8:9, at * width : (at + 1) * width] = jnp.where(first, d, e)
    e, d = inner_e[...], inner_d[...]
    keep[9:10] = jnp.where(first, e, d)
    send[9:10] = jnp.where(first, d, e)


def more_body(*refs):
    total = refs[0][...]
    for ref in refs[1:-1]:
        total = total + ref[...]
    refs[-1][...] = total


def more(*entries):
    return call(more_body, [shape(*entries[0].shape, dtype=F32)], *entries)[0]


def unpack_body(*refs):
    gain, row, col, inner = refs[-4:]
    total = refs[0][...]
    for ref in refs[1:-4]:
        total = total + ref[...]
    gain[0] = total[:3]
    row[0] = total[3:8]
    width = col.shape[2]
    for place in range(3):
        col[0, place : place + 1] = total[8:9, place * width : (place + 1) * width]
    inner[...] = total[9:10]


class Total:
    def __init__(self, entry):
        self.entry, self.step = entry, 1
        self.send()

    def send(self):
        size = lax.axis_size("clip")
        if self.step < size:
            pairs = [(i, i ^ self.step) for i in range(size)]
            self.flying = lax.ppermute(self.entry, "clip", pairs)

    def advance(self):
        self.entry = more(self.entry, self.flying)
        self.step *= 2
        self.send()

    def parts(self):
        while self.step * 2 < lax.axis_size("clip"):
            self.advance()
        return self.entry, self.flying


def local(
    enc_in, dec_in, stamp_flags, dec_lengths, proj_w, fc_in, fc_out,
    col_bias, ff_bias, norm_gain, row_bias, enc_cot, dec_cot,
):
    ORDER[0] = None
    place = lax.axis_index("pipe")
    spot = lax.axis_index("head")
    parity = lax.axis_index("clip") % 2
    row, core = spot // 2, spot % 2
    sel = [place, parity, 2 * row, 2 - 2 * row, 2 * row + 1, 3 - 2 * row, core, lax.axis_index("clip")]
    sel = jnp.stack(sel).astype(jnp.int32)
    width = norm_gain.shape[-1]

    clips = lax.axis_size("clip")
    own = jnp.swapaxes(proj_w[0], 1, 2)
    e_block, block = enc_in.shape[1], dec_in.shape[1]
    mask = (stamp_flags, dec_lengths)
    v = {}

    def also(name):
        return tuple(v[key] for key in ALSO.get(name, ()) if key in v)

    def cores(name, part):
        return swap_core(part) if name in QUICK else both_cores(part)

    def weights_self():
        half_a, half_b = split(sel, [own], [(0, 0, 2), (0, 2, 4)])
        v["near_a"], v["near_b"] = swap_pipe(half_a), swap_pipe(half_b)

    def vectors():
        vown = call(
            pack_body, [shape(16, width, dtype=F32)],
            norm_gain[0], row_bias[0], ff_bias, col_bias[0],
        )[0]
        v["vecs"] = (vown, swap_pipe(vown))

    def rows_in():
        v["in"] = take(sel, enc_in, dec_in, also=also("rows_in"))
        rows = (v["in"], swap_row(v["in"]))
        v["x"], v["z"] = (*rows, 0, e_block), (*rows, e_block, block)

    def weights_1():
        (half,) = split(sel, [fc_in], [(0, 0, 1)], also=(v["near_a"],))
        v["far_a"], v["near_1"] = swap_pair(v["near_a"]), swap_pipe(half)

    def norm_e():
        v["h1"] = both_cores(norm_in(ENC, sel, v["x"], v["vecs"], also=(v["far_a"],)))

    def weights_2():
        (whole,) = split(sel, [fc_out], [(0, 0, 1)], also=(v["near_b"],), parts=1)
        v["far_b"], v["got_2"] = swap_pair(v["near_b"]), swap_pipe(whole)
        v["self_w"] = (own, v["near_a"], v["far_a"], v["near_b"], v["far_b"])

    def rows_cot():
        cot = take(sel, dec_cot, enc_cot)
        rows = (cot, swap_row(cot))
        v["dec_cots"], v["enc_cots"] = (*rows, 0, block), (*rows, block, e_block)

    def norm_d():
        v["t1"] = both_cores(norm_in(DEC, sel, v["z"], v["vecs"]))

    def stack_d():
        v["dec_rows"] = stacked(v["dec_cots"])
        v["gbr_z2"] = both_cores(v["dec_rows"])

    def self_e():
        v["qkv"], v["a"], v["lse"], pm, po = self_fwd(
            ENC, sel, v["h1"], v["self_w"], v["vecs"], (),
            also=(v["t1"], v["near_1"], v["dec_rows"]),
        )
        v["far_1"] = swap_pair(v["near_1"])
        v["xs"] = (pm, cores("self_e", po))

    def add_x():
        v["xs"] = (*v["xs"], swap_row(add_low(sel, *v["xs"])))

    def weights_c():
        (whole,) = split(sel, [own], [(0, 4, 6)], parts=1)
        v["cross_w"] = (own, swap_pipe(whole))

    def self_d():
        v["dqkv"], v["da"], v["dlse"], pm, po = self_fwd(
            DEC, sel, v["t1"], v["self_w"], v["vecs"], mask
        )
        v["zs"] = (pm, cores("self_d", po))

    def add_z():
        v["zs"] = (*v["zs"], swap_row(add_low(sel, *v["zs"])))

    def res_x1():
        v["x1"], hm = res_norm(ENC, sel, v["x"], v["xs"], v["vecs"], 3, 2, also=(v["far_1"],))
        v["h2"] = both_cores(hm)

    def ff_e():
        v["ff_w"] = (fc_in[0], v["near_1"][0], v["far_1"][0], fc_out[0], v["got_2"][0])
        v["u"], v["g"], pm, po = ff_fwd(ENC, sel, v["h2"], v["ff_w"], v["vecs"])
        v["ys"] = (pm, cores("ff_e", po))

    def add_y():
        v["ys"] = (*v["ys"], swap_row(add_low(sel, *v["ys"])))

    def res_z1():
        v["z1"], tm = res_norm(DEC, sel, v["z"], v["zs"], v["vecs"], 3, 1)
        v["t2"] = both_cores(tm)

    def res_y():
        v["y"], em = res_norm(
            ENC, sel, v["x1"], v["ys"], v["vecs"], 4, 1, also=(v["t2"], v["gbr_z2"])
        )
        v["e"] = both_cores(em)

    def cross():
        v["cq"], v["kv"], v["c"], v["clse"], pm, po = cross_fwd(
            sel, v["t2"], v["e"], v["cross_w"], v["vecs"]
        )
        v["cs"] = (pm, cores("cross", po))

    def add_c():
        v["cs"] = (*v["cs"], swap_row(add_low(sel, *v["cs"])))

    def res_z2():
        v["z2"], tm = res_norm(DEC, sel, v["z1"], v["cs"], v["vecs"], None, 2)
        v["t3"] = both_cores(tm)

    def ff_d():
        v["w_pre"], v["w"], pm, po = ff_fwd(DEC, sel, v["t3"], v["ff_w"], v["vecs"])
        v["rs"] = (pm, po)

    def add_r():
        pm, po = v["rs"]
        recv = cores("ff_d", po)
        v["r_got"] = swap_row(add_low(sel, pm, recv, block))
        v["rs"] = (pm, recv, v["r_got"])

    def ff_back_d():
        v["gp_d"], pm, po, v["inner_d"] = ff_bwd(DEC, sel, v["gbr_z2"], v["w_pre"], v["ff_w"])
        v["gs"] = (pm, cores("ff_back_d", po))

    def add_gz2():
        v["gs"] = (*v["gs"], swap_row(add_low(sel, *v["gs"])))

    def wgrad_ff_d():
        v["ring_ff_d"] = Ring(
            sel, *wgrads(sel, clips, (v["gbr_z2"], v["w"]), (v["t3"], v["gp_d"]))
        )

    def back_z2():
        v["gz2"], gm, v["sums_z2"] = norm_back(
            DEC, sel, v["z2"], v["dec_cots"], v["gs"], v["vecs"], 2
        )
        v["gbr_c"] = both_cores(gm)

    def cross_back():
        v["gcq"], v["gkv"], zm, zo, ym, yo, v["sums_c"] = cross_bwd(
            sel, v["gbr_c"], v["cq"], v["kv"], v["clse"], v["cross_w"]
        )
        v["gys"], v["gzs"] = (ym, cores("cross_back", yo)), (zm, zo)

    def add_gy():
        v["gys"] = (*v["gys"], swap_row(add_low(sel, *v["gys"])))

    def add_gz1():
        pm, po = v["gzs"]
        recv = cores("cross_back_z", po)
        v["gzs"] = (pm, recv, swap_row(add_low(sel, pm, recv)))

    def wgrad_cross():
        v["cross_g"], send = both_wgrads(
            sel, clips, [(v["e"], v["gkv"])], [(v["t2"], v["gcq"]), (v["gbr_c"], v["c"])]
        )
        v["cross_got"] = swap_pipe(send)

    def outputs():
        v["keep_fwd"], send = last_fwd(sel, v["y"], v["z2"], v["rs"], v["vecs"])
        v["got_fwd"] = swap_pipe(send)

    def place_outputs():
        v["e_out"], v["d_out"] = placed(sel, v["keep_fwd"], v["got_fwd"], e_block)

    def back_y():
        v["gy"], gm, v["sums_y"] = norm_back(
            ENC, sel, v["y"], v["enc_cots"], v["gys"], v["vecs"], 1, also=also("back_y")
        )
        v["gbr_y"] = both_cores(gm)

    def ff_back_e():
        v["gp_e"], pm, po, v["inner_e"] = ff_bwd(
            ENC, sel, v["gbr_y"], v["u"], v["ff_w"], also=also("ff_back_e")
        )
        v["gxs"] = (pm, cores("ff_back_e", po))

    def add_gx1():
        v["gxs"] = (*v["gxs"], swap_row(add_low(sel, *v["gxs"])))

    def wgrad_first():
        v["ff_1"], _ = wgrads(sel, clips, (v["h2"], v["gp_e"]))

    def wgrad_second():
        v["ring_2"] = Ring(
            sel, *second_and_cross(sel, v["gbr_y"], v["g"], v["cross_g"], v["cross_got"])
        )

    def back_z1():
        v["gz1"], gm, v["sums_z1"] = norm_back(
            DEC, sel, v["z1"], v["gz2"], v["gzs"], v["vecs"], 1
        )
        v["gbr_z1"] = both_cores(gm)

    def self_back_d():
        v["gqkv_d"], pm, po, v["self_d_sum"] = self_bwd(
            DEC, sel, v["gbr_z1"], v["dqkv"], v["dlse"], v["self_w"], mask,
            also=also("self_back_d"),
        )
        v["lz"] = (pm, cores("self_back_d", po))

    def wgrad_own_d():
        v["pair_keep"], send = first_and_own(
            sel, v["ff_1"], (v["t1"], v["gqkv_d"]), (v["gbr_z1"], v["da"])
        )
        v["pair_got"] = swap_pipe(send)

    def back_x1():
        v["gx1"], gm, v["sums_x1"] = norm_back(
            ENC, sel, v["x1"], v["gy"], v["gxs"], v["vecs"], 2, also=also("back_x1")
        )
        v["gbr_x1"] = both_cores(gm)

    def self_back_e():
        v["gqkv_e"], pm, po, v["self_e_sum"] = self_bwd(
            ENC, sel, v["gbr_x1"], v["qkv"], v["lse"], v["self_w"], (), also=also("self_back_e")
        )
        v["lx"] = (pm, both_cores(po))

    def add_last_both():
        sums = (v["lx"][0], v["lz"][0], v["lx"][1], v["lz"][1])
        v["last"] = (*sums, swap_row(add_last(sel, *sums)))

    def wgrad_own_e():
        v["ring_own"] = Ring(
            sel, *wgrads(sel, clips, (v["h1"], v["gqkv_e"]), (v["gbr_x1"], v["a"]))
        )

    def inputs():
        v["keep"], send, v["sums_x"], v["sums_z"] = last_back(
            sel, v["in"], v["gx1"], v["gz1"], v["last"], v["vecs"]
        )
        v["got"] = swap_pipe(send)

    def place_inputs():
        v["ge_out"], v["gd_out"] = placed(sel, v["keep"], v["got"], e_block)

    def ring(name):
        def step():
            v[name].advance(also=also(f"{name}_{v[name].step}"))

        return step

    def join():
        v["ring_1"] = Ring(sel, *joined(sel, v["pair_keep"], v["pair_got"]))

    def side_1():
        v["side_got"] = swap_pipe(side(sel, v["ring_2"].finish(), v["ring_ff_d"].finish(), 0))

    def side_2():
        own_e, ff_d = v["ring_own"].finish(), v["ring_ff_d"].finish()
        v["own_e_got"] = swap_pipe(side(sel, own_e, ff_d, ff_d.shape[1] // 2))

    def vec_core():
        wide = call(
            pack_sums_body, [shape(16, width, dtype=F32)],
            v["sums_y"], v["sums_x1"], v["sums_x"], v["sums_z2"], v["sums_z1"], v["sums_z"],
        )[0]
        v["wide"] = (wide, swap_core(wide))

    def vec_row():
        wide = more(*v["wide"])
        v["wide"] = (wide, swap_row(wide))

    def vec_pipe():
        mine, other = call(
            pack_slim_body, [shape(16, width, dtype=F32), shape(16, width, dtype=F32)],
            sel, *v["wide"], v["self_e_sum"], v["self_d_sum"], v["sums_c"],
            v["inner_e"], v["inner_d"],
        )
        v["mine"] = (mine, swap_pipe(other))

    def vec_clip():
        v["total"] = Total(more(*v["mine"]))

    def vec_half():
        v["total"].advance()

    def unpack():
        v["vectors"] = call(
            unpack_body,
            [
                shape(1, 3, width, dtype=F32), shape(1, 5, width, dtype=F32),
                shape(1, 3, own.shape[1], dtype=F32), shape(1, ff_bias.shape[1], dtype=F32),
            ],
            *v["total"].parts(),
        )

    steps = dict(locals())
    for name in SCHEDULE:
        if name in RINGS:
            ring(name)()
        else:
            steps[name]()
    heads, hidden, cut = own.shape[1], fc_in.shape[-1], width // clips
    out_first, out_second, out_proj = call(
        finish_body,
        [
            shape(1, cut, hidden, dtype=F32),
            shape(1, cut, hidden, dtype=F32),
            shape(1, 6, cut, heads, dtype=F32),
        ],
        sel, v["ring_2"].finish(), v["ring_ff_d"].finish(), v["side_got"],
        v["ring_1"].finish(), v["ring_own"].finish(), v["own_e_got"],
    )
    out_gain, out_row, out_col, out_inner = v["vectors"]
    return (
        v["e_out"],
        v["d_out"],
        v["ge_out"],
        v["gd_out"],
        out_proj,
        out_first,
        out_second,
        out_col,
        out_inner,
        out_gain,
        out_row,
    )


def solution(mesh):
    return jax.shard_map(
        local,
        mesh=mesh,
        in_specs=(
            P("clip", "head", None),
            P("clip", "head", None),
            P("clip"),
            P("clip"),
            P("pipe", None, None, "head"),
            P("pipe", None, "head"),
            P("pipe", None, "head"),
            P("pipe", None, "head"),
            P("pipe", "head"),
            P("pipe", None, None),
            P("pipe", None, None),
            P("clip", "head", None),
            P("clip", "head", None),
        ),
        out_specs=(
            P("clip", "head", "pipe"),
            P("clip", "head", "pipe"),
            P("clip", "head", "pipe"),
            P("clip", "head", "pipe"),
            P("pipe", None, "clip", "head"),
            P("pipe", "clip", "head"),
            P("pipe", "clip", "head"),
            P("pipe", None, "head"),
            P("pipe", "head"),
            P("pipe", None, None),
            P("pipe", None, None),
        ),
        check_vma=False,
    )
```

```python
import functools
import types

import jax
import jax.numpy as jnp
from jax import lax
from jax.experimental import pallas as pl
from jax.experimental.pallas import tpu as pltpu
from jax.sharding import PartitionSpec as P

HEAD_DIM = 64
DEC_SHORT = 224
SCALE = HEAD_DIM ** (-0.5)
SCALE_2 = SCALE * 1.4426950408889634
F32 = jnp.float32
BF16 = jnp.bfloat16
ENC, DEC = 0, 1

CORE_GROUPS = [[0, 1], [2, 3]]
CORE_PAIRS = [(0, 1), (1, 0), (2, 3), (3, 2)]
ROW_PAIRS = [(0, 2), (2, 0), (1, 3), (3, 1)]
PIPE_PAIRS = [(0, 1), (1, 0)]

GAIN, ROW, FF, COL = 0, 3, 8, 9


def both_cores(entry):
    return lax.all_gather(entry, "head", axis=0, axis_index_groups=CORE_GROUPS, tiled=True)


def swap_core(entry):
    return lax.ppermute(entry, "head", CORE_PAIRS)


def swap_row(entry):
    return lax.ppermute(entry, "head", ROW_PAIRS)


def swap_pipe(entry):
    return lax.ppermute(entry, "pipe", PIPE_PAIRS)


def swap_pair(entry):
    size = lax.axis_size("clip")
    return lax.ppermute(entry, "clip", [(i, i ^ 1) for i in range(size)])


def next_clip(entry):
    size = lax.axis_size("clip")
    return lax.ppermute(entry, "clip", [(i, (i + 1) % size) for i in range(size)])


def nn(left, right):
    return lax.dot_general(left, right, (((1,), (0,)), ((), ())), preferred_element_type=F32)


def nt(left, right):
    return lax.dot_general(left, right, (((1,), (1,)), ((), ())), preferred_element_type=F32)


def tn(left, right):
    return lax.dot_general(left, right, (((0,), (0,)), ((), ())), preferred_element_type=F32)


def shape(*dims, dtype=BF16):
    return jax.ShapeDtypeStruct(dims, dtype)


ORDER = [None]
COST = dict(
    ring=0.05,
    self_fwd=3.4, self_bwd=4.8, cross_fwd=3.5, cross_bwd=5.4, ff_fwd=2.4, ff_bwd=2.8, wgrad=1.7,
    both_wgrad=1.7, norm_in=0.8, res_norm=0.9, norm_back=0.05, take=1.2, last_back=1.2,
    join_two=1.9, finish=2.5, place=1.3,
)


def call(body, outs, *ins, flops=0, limit=12, scratch=(), anywhere=(), out_anywhere=False, also=()):
    vmem = pl.BlockSpec(memory_space=pltpu.VMEM)
    smem = pl.BlockSpec(memory_space=pltpu.SMEM)
    any_space = pl.BlockSpec(memory_space=pl.ANY)
    hbm = pl.BlockSpec(memory_space=pltpu.HBM)
    specs = [
        hbm if place in anywhere else smem if a.dtype == jnp.int32 else vmem
        for place, a in enumerate(ins)
    ]
    count = len(ins)
    before = (*(() if ORDER[0] is None else (ORDER[0],)), *also)

    def ordered(*refs):
        body(*refs[:count], *refs[count + len(before) :])

    name = getattr(body, "func", body).__name__[:-5]
    found = pl.pallas_call(
        ordered,
        name=name,
        out_shape=outs,
        in_specs=[*specs, *[any_space] * len(before)],
        out_specs=[hbm if out_anywhere else vmem] * len(outs),
        scratch_shapes=scratch,
        compiler_params=pltpu.CompilerParams(vmem_limit_bytes=limit << 20),
        cost_estimate=pl.CostEstimate(
            flops=int(COST.get(name, 0.6) * 1.15e9), bytes_accessed=1, transcendentals=0
        ),
    )(*ins, *before)
    ORDER[0] = found[-1]
    return found


def pick(sel, section, own, near, far):
    is_own = sel[0] == section
    even = sel[1] == 0
    half = near.shape[0]
    top = jnp.where(is_own, own[:half], jnp.where(even, near, far))
    bottom = jnp.where(is_own, own[half:], jnp.where(even, far, near))
    return jnp.concatenate([top, bottom])


def choose(sel, section, own, got):
    return jnp.where(sel[0] == section, own, got)


def vector(sel, section, vecs, row, width=None):
    own, got = vecs
    cut = slice(0, width if width else own.shape[1])
    return jnp.where(sel[0] == section, own[row : row + 1, cut], got[row : row + 1, cut])


def norm_parts(rows):
    centered = rows - jnp.mean(rows, axis=-1, keepdims=True)
    variance = jnp.mean(centered * centered, axis=-1, keepdims=True)
    inverse = lax.rsqrt(variance + 1e-05)
    return centered * inverse, inverse


def take_body(count, sel, *refs):
    out, sems = refs[-2:]
    copies, at = [], 0
    for i in range(count):
        rows = refs[i].shape[1]
        copies.append(
            pltpu.make_async_copy(refs[i].at[sel[0]], out.at[at : at + rows], sems.at[i])
        )
        at += rows
    for copy in copies:
        copy.start()
    for copy in copies:
        copy.wait()


def take(sel, *arrays, limit=12, also=()):
    count = len(arrays)
    rows = sum(a.shape[1] for a in arrays)
    return call(
        functools.partial(take_body, count), [shape(rows, arrays[0].shape[2])], sel, *arrays,
        anywhere=range(1, 1 + count), scratch=[pltpu.SemaphoreType.DMA((count,))], limit=limit,
        also=also,
    )[0]


def split_body(cuts, sel, *refs):
    count = max(source for source, _, _ in cuts) + 1
    sems = refs[-1]
    copies = []
    for place, (source, start, stop) in enumerate(cuts):
        out = refs[count + place]
        half = out.shape[1]
        rows = pl.ds(pl.multiple_of(sel[1] * half, half), half)
        if half == refs[source].shape[1]:
            rows = slice(None)
        copies.append(
            pltpu.make_async_copy(refs[source].at[start:stop, rows], out, sems.at[place])
        )
    for copy in copies:
        copy.start()
    for copy in copies:
        copy.wait()


def split(sel, arrays, cuts, also=(), limit=12, parts=2):
    outs = [
        shape(stop - start, arrays[source].shape[1] // parts, arrays[source].shape[2])
        for source, start, stop in cuts
    ]
    return call(
        functools.partial(split_body, cuts), outs, sel, *arrays,
        anywhere=range(1, 1 + len(arrays)), out_anywhere=True,
        scratch=[pltpu.SemaphoreType.DMA((len(cuts),))], also=also, limit=limit,
    )


def pack_body(gain, row, ff, col, out):
    out[...] = jnp.zeros_like(out)
    out[GAIN : GAIN + 3] = gain[...]
    out[ROW : ROW + 5] = row[...]
    out[FF : FF + 1] = ff[...]
    out[COL : COL + 3, : col.shape[1]] = col[...]


def from_other(sel, pm, recv):
    return (1 - sel[6]) * (recv.shape[0] - pm.shape[0])


def add_body(start, sel, pm, recv, low):
    count = low.shape[0]
    there = pl.ds(pl.multiple_of(from_other(sel, pm, recv) + start, count), count)
    low[...] = (pm[start : start + count] + recv[there].astype(F32)).astype(BF16)


def add_low(sel, pm, recv, start=0, also=()):
    rows, width = pm.shape
    return call(
        functools.partial(add_body, start), [shape(rows - start, width)], sel, pm, recv, also=also
    )[0]


def add_last_body(sel, xm, zm, xr, zr, low):
    at = 0
    for pm, recv in ((xm, xr), (zm, zr)):
        count = pm.shape[0] // 2
        there = pl.ds(pl.multiple_of(from_other(sel, pm, recv) + count, count), count)
        low[at : at + count] = (pm[count:] + recv[there].astype(F32)).astype(BF16)
        at += count


def add_last(sel, xm, zm, xr, zr):
    rows = (xm.shape[0] + zm.shape[0]) // 2
    return call(add_last_body, [shape(rows, xm.shape[1])], sel, xm, zm, xr, zr)[0]


def stack_body(start, block, own, got, out):
    out[:block] = own[start : start + block]
    out[block:] = got[start : start + block]


def stacked(rows):
    own, got, start, block = rows
    return call(
        functools.partial(stack_body, start, block), [shape(2 * block, own.shape[1])], own, got
    )[0]


def norm_in_body(section, at, sel, own, got, vown, vgot, hm_ref):
    gain = vector(sel, section, (vown, vgot), GAIN)
    bias = vector(sel, section, (vown, vgot), ROW)
    block = hm_ref.shape[0] // 2
    for start, part in ((0, own), (block, got)):
        unit, _ = norm_parts(part[at : at + block].astype(F32))
        hm_ref[start : start + block] = (unit * gain + bias).astype(BF16)


def norm_in(section, sel, rows, vecs, also=()):
    own, got, start, block = rows
    return call(
        functools.partial(norm_in_body, section, start), [shape(2 * block, own.shape[1])],
        sel, own, got, *vecs, also=also,
    )[0]


def summed(sel, pm, recv, got, rows, other):
    block = rows.stop - rows.start
    there = pl.ds(pl.multiple_of(from_other(sel, pm, recv) + rows.start, block), block)
    return pm[rows] + recv[there].astype(F32) + got[other].astype(F32)


def halves(block):
    return ((slice(0, block), slice(block, 2 * block)), (slice(block, 2 * block), slice(0, block)))


def res_norm_body(section, out_row, index, at, *refs):
    split = at is not None
    sel = refs[0]
    res = refs[1 : 3 if split else 2]
    pm, recv, got, vown, vgot, x_ref, hm_ref = refs[3 if split else 2 :]
    vecs = (vown, vgot)
    gain = vector(sel, section, vecs, GAIN + index)
    bias = vector(sel, section, vecs, ROW + index)
    block = pm.shape[0] // 2
    for place, (rows, other) in enumerate(halves(block)):
        base = res[place][at : at + block].astype(F32) if split else res[0][rows]
        now = base + summed(sel, pm, recv, got, rows, other)
        if out_row is not None:
            now = now + vector(sel, section, vecs, ROW + out_row)
        x_ref[rows] = now
        unit, _ = norm_parts(now)
        hm_ref[rows] = (unit * gain + bias).astype(BF16)


def res_norm(section, sel, res, sums, vecs, out_row, index, also=()):
    rows, width = sums[0].shape
    at, res = (res[2], res[:2]) if isinstance(res, tuple) else (None, (res,))
    return call(
        functools.partial(res_norm_body, section, out_row, index, at),
        [shape(rows, width, dtype=F32), shape(rows, width)],
        sel, *res, *sums, *vecs, also=also,
    )


def norm_grad(rows, gain, grad):
    unit, inverse = norm_parts(rows)
    scaled = grad * gain
    back = inverse * (
        scaled
        - jnp.mean(scaled, axis=-1, keepdims=True)
        - unit * jnp.mean(scaled * unit, axis=-1, keepdims=True)
    )
    return back, unit


def col_sum(entry):
    return jnp.sum(entry, axis=0, keepdims=True)


def norm_back_body(section, index, at, *refs):
    split = at is not None
    sel, x = refs[:2]
    res = refs[2 : 4 if split else 3]
    pm, recv, got, vown, vgot, g_ref, gm_ref, sum_ref = refs[4 if split else 3 :]
    gain = vector(sel, section, (vown, vgot), GAIN + index)
    block = pm.shape[0] // 2
    for place, (rows, other) in enumerate(halves(block)):
        grad = summed(sel, pm, recv, got, rows, other)
        base = res[place][at : at + block].astype(F32) if split else res[0][rows]
        back, unit = norm_grad(x[rows], gain, grad)
        now = base + back
        g_ref[rows] = now
        gm_ref[rows] = now.astype(BF16)
        if place == 0:
            sum_ref[0:1] = col_sum(grad * unit)
            sum_ref[1:2] = col_sum(grad)
            sum_ref[2:3] = col_sum(now)
            sum_ref[3:4] = col_sum(base)


def norm_back(section, sel, x, res, sums, vecs, index, also=()):
    rows, width = x.shape
    at, res = (res[2], res[:2]) if isinstance(res, tuple) else (None, (res,))
    return call(
        functools.partial(norm_back_body, section, index, at),
        [shape(rows, width, dtype=F32), shape(rows, width), shape(4, width, dtype=F32)],
        sel, x, *res, *sums, *vecs, also=also,
    )


def send_halves(sel, rows, low, keep_ref, send_ref):
    width = low.shape[1] // 2
    left, right = low[:, :width], low[:, width:]
    keep_ref[rows] = jnp.where(sel[0] == 0, left, right)
    send_ref[rows] = jnp.where(sel[0] == 0, right, left)


def last_fwd_body(sel, y, z2, pm, recv, got, vown, vgot, keep_ref, send_ref):
    block = got.shape[0]
    e_block = y.shape[0] // 2
    rows = slice(0, block)
    r = z2[rows] + summed(sel, pm, recv, got, rows, rows)
    r = r + vector(sel, DEC, (vown, vgot), ROW + 4)
    send_halves(sel, slice(0, e_block), y[:e_block].astype(BF16), keep_ref, send_ref)
    send_halves(sel, slice(e_block, e_block + block), r.astype(BF16), keep_ref, send_ref)


def last_fwd(sel, y, z2, sums, vecs):
    rows = y.shape[0] // 2 + sums[2].shape[0]
    width = y.shape[1] // 2
    return call(
        last_fwd_body, [shape(rows, width), shape(rows, width)], sel, y, z2, *sums, *vecs
    )


def last_back_body(
    sel, rows_in, gx1, gz1, xm, zm, xr, zr, all_got, vown, vgot,
    keep_ref, send_ref, sum_x, sum_z,
):
    vecs = (vown, vgot)
    start = 0
    for section, res, pm, recv, out in ((ENC, gx1, xm, xr, sum_x), (DEC, gz1, zm, zr, sum_z)):
        gain = vector(sel, section, vecs, GAIN)
        block = pm.shape[0] // 2
        rows = slice(0, block)
        grad = summed(sel, pm, recv, all_got, rows, slice(start, start + block))
        back, unit = norm_grad(rows_in[start : start + block].astype(F32), gain, grad)
        low = (res[rows] + back).astype(BF16)
        send_halves(sel, slice(start, start + block), low, keep_ref, send_ref)
        out[0:1] = col_sum(grad * unit)
        out[1:2] = col_sum(grad)
        start += block


def last_back(sel, rows_in, gx1, gz1, sums, vecs):
    rows, width = rows_in.shape
    return call(
        last_back_body,
        [
            shape(rows, width // 2), shape(rows, width // 2),
            shape(2, width, dtype=F32), shape(2, width, dtype=F32),
        ],
        sel, rows_in, gx1, gz1, *sums, *vecs,
    )


def place_body(sel, keep, got, *outs):
    start = 0
    for ref in outs:
        rows = slice(start, start + ref.shape[1])
        ref[0] = jnp.where(sel[0] == 0, keep[rows], got[rows])
        ref[1] = jnp.where(sel[0] == 0, got[rows], keep[rows])
        start += ref.shape[1]


def placed(sel, keep, got, block):
    rows, width = keep.shape
    return call(
        place_body, [shape(2, block, width), shape(2, rows - block, width)], sel, keep, got
    )


def places(sel, axis, dims):
    at = lax.broadcasted_iota(jnp.int32, dims, axis)
    size = dims[axis] // 4
    shift = sel[5] - 3
    for block in (2, 1, 0):
        shift = jnp.where(at < (block + 1) * size, sel[2 + block] - block, shift)
    return at + shift * size


def text_length(sel, flags, lengths):
    return jnp.minimum(lengths[sel[0]], DEC_SHORT * (1 + flags[sel[0]]))


def allowed(sel, flags, lengths, rows, key_axis):
    shapes = ((1, rows), (rows, 1)) if key_axis == 1 else ((rows, 1), (1, rows))
    keys = places(sel, key_axis, shapes[0])
    keys = jnp.where(keys < text_length(sel, flags, lengths), keys, rows)
    return keys <= places(sel, 1 - key_axis, shapes[1])


def attend(q_ref, q_at, kv_ref, k_at, v_at, mask, a_ref, lse_ref):
    rows, width = a_ref.shape
    ones = jnp.ones((kv_ref.shape[0], HEAD_DIM), BF16)
    if mask:
        keep = allowed(*mask, rows, 1)
    for head in range(width // HEAD_DIM):
        cut = slice(head * HEAD_DIM, (head + 1) * HEAD_DIM)
        k_head = kv_ref[:, k_at + cut.start : k_at + cut.stop]
        v_head = kv_ref[:, v_at + cut.start : v_at + cut.stop]
        scores = nt(q_ref[:, q_at + cut.start : q_at + cut.stop], k_head)
        if mask:
            scores = jnp.where(keep, scores, -1e30)
        top = jnp.max(scores, axis=-1, keepdims=True)
        low = jnp.exp2((scores - top) * SCALE_2).astype(BF16)
        both = nn(low, jnp.concatenate([v_head, ones], axis=1))
        total = both[:, HEAD_DIM : HEAD_DIM + 1]
        a_ref[:, cut] = (both[:, :HEAD_DIM] * (1.0 / total)).astype(BF16)
        lse_ref[:, head : head + 1] = top * SCALE_2 + jnp.log2(total)


def attend_back(
    q_ref, q_at, kv_ref, k_at, v_at, grad, lse, mask, gq_ref, gq_at, gkv_ref, gk_at, gv_at,
    rows_ref,
):
    rows, width = grad.shape
    rows_ref[:, : lse.shape[1]] = lse[...]
    sums = rows_ref[...].T
    if mask:
        keep = allowed(*mask, rows, 0)
    for head in range(width // HEAD_DIM):
        cut = slice(head * HEAD_DIM, (head + 1) * HEAD_DIM)
        q_head = q_ref[:, q_at + cut.start : q_at + cut.stop]
        o_head = grad[:, cut]
        k_head = kv_ref[:, k_at + cut.start : k_at + cut.stop]
        v_head = kv_ref[:, v_at + cut.start : v_at + cut.stop]
        scores = nt(k_head, q_head)
        if mask:
            scores = jnp.where(keep, scores, -1e30)
        weights = jnp.exp2(scores * SCALE_2 - sums[head : head + 1])
        both = weights * nt(v_head, o_head)
        grad_s = (both - weights * jnp.sum(both, axis=0, keepdims=True)).astype(BF16)
        gv = nn(weights.astype(BF16), o_head)
        gk = nn(grad_s, q_head) * SCALE
        gq = tn(grad_s, k_head) * SCALE
        gkv_ref[:, gk_at + cut.start : gk_at + cut.stop] = gk.astype(BF16)
        gkv_ref[:, gv_at + cut.start : gv_at + cut.stop] = gv.astype(BF16)
        gq_ref[:, gq_at + cut.start : gq_at + cut.stop] = gq.astype(BF16)


def halves_of(sel, half):
    mine = pl.ds(pl.multiple_of(sel[6] * half, half), half)
    other = pl.ds(pl.multiple_of((1 - sel[6]) * half, half), half)
    return mine, other


def project_out(sel, mixed_ref, weight, pm_ref, po_ref, by=nn):
    mine, other = halves_of(sel, pm_ref.shape[0])
    pm_ref[...] = by(mixed_ref[mine], weight)
    po_ref[...] = by(mixed_ref[other], weight).astype(BF16)


def self_fwd_body(section, masked, *refs):
    sel, h, own, near_a, far_a, near_b, far_b, vown, vgot = refs[:9]
    mask = (sel, *refs[9:11]) if masked else None
    qkv_ref, a_ref, lse_ref, pm_ref, po_ref = refs[11 if masked else 9 :]
    width = a_ref.shape[1]
    wq = pick(sel, section, own[0], near_a[0], far_a[0])
    wk = pick(sel, section, own[1], near_a[1], far_a[1])
    wv = pick(sel, section, own[2], near_b[0], far_b[0])
    bq = vector(sel, section, (vown, vgot), COL, width)
    bv = vector(sel, section, (vown, vgot), COL + 1, width)
    rows = h[...]
    qkv_ref[:, :width] = (nt(rows, wq) + bq).astype(BF16)
    qkv_ref[:, width : 2 * width] = nt(rows, wk).astype(BF16)
    qkv_ref[:, 2 * width :] = (nt(rows, wv) + bv).astype(BF16)
    attend(qkv_ref, 0, qkv_ref, width, 2 * width, mask, a_ref, lse_ref)
    wo = pick(sel, section, own[3], near_b[1], far_b[1])
    project_out(sel, a_ref, wo, pm_ref, po_ref)


def self_fwd(section, sel, h, weights, vecs, mask, also=()):
    rows, width = h.shape
    heads = weights[0].shape[1]
    outs = [
        shape(rows, 3 * heads), shape(rows, heads), shape(rows, heads // HEAD_DIM, dtype=F32),
        shape(rows // 2, width, dtype=F32), shape(rows // 2, width),
    ]
    return call(
        functools.partial(self_fwd_body, section, bool(mask)), outs, sel, h, *weights, *vecs, *mask,
        also=also,
    )


def back_scratch(rows, heads):
    return [pltpu.VMEM((rows, heads), BF16), pltpu.VMEM((rows, 128), F32)]


def self_bwd_body(section, masked, *refs):
    sel, g, qkv, lse, own, near_a, far_a, near_b, far_b = refs[:9]
    refs = refs[9:]
    mask, refs = ((sel, *refs[:2]), refs[2:]) if masked else (None, refs)
    gqkv_ref, pm_ref, po_ref, sum_ref, ga, spare = refs
    width = ga.shape[1]
    wo = pick(sel, section, own[3], near_b[1], far_b[1])
    ga[...] = nt(g[...], wo).astype(BF16)
    attend_back(
        qkv, 0, qkv, width, 2 * width, ga, lse, mask,
        gqkv_ref, 0, gqkv_ref, width, 2 * width, spare,
    )
    weight = jnp.concatenate(
        [
            pick(sel, section, own[0], near_a[0], far_a[0]),
            pick(sel, section, own[1], near_a[1], far_a[1]),
            pick(sel, section, own[2], near_b[0], far_b[0]),
        ]
    )
    project_out(sel, gqkv_ref, weight, pm_ref, po_ref)
    sum_ref[...] = col_sum(gqkv_ref[...].astype(F32))


def self_bwd(section, sel, g, qkv, lse, weights, mask, also=()):
    rows, width = g.shape
    heads = weights[0].shape[1]
    outs = [
        shape(rows, 3 * heads), shape(rows // 2, width, dtype=F32),
        shape(rows // 2, width), shape(1, 3 * heads, dtype=F32),
    ]
    return call(
        functools.partial(self_bwd_body, section, bool(mask)), outs, sel, g, qkv, lse,
        *weights, *mask, scratch=back_scratch(rows, heads), also=also,
    )


def cross_fwd_body(
    sel, t, e, own, got, vown, vgot, cq_ref, kv_ref, c_ref, lse_ref, pm_ref, po_ref
):
    width = cq_ref.shape[1]
    vecs = (vown, vgot)
    w4 = choose(sel, ENC, own[4], got[0])
    w5 = choose(sel, ENC, own[5], got[1])
    rows = e[...]
    kv_ref[:, :width] = nt(rows, w4).astype(BF16)
    kv_ref[:, width:] = (nt(rows, w5) + vector(sel, ENC, vecs, COL + 2, width)).astype(BF16)
    wq = choose(sel, DEC, own[4], got[0])
    cq_ref[...] = (nt(t[...], wq) + vector(sel, DEC, vecs, COL + 2, width)).astype(BF16)
    attend(cq_ref, 0, kv_ref, 0, width, None, c_ref, lse_ref)
    wo = choose(sel, DEC, own[5], got[1])
    project_out(sel, c_ref, wo, pm_ref, po_ref)


def cross_fwd(sel, t, e, weights, vecs, also=()):
    rows, width = t.shape
    e_rows, heads = e.shape[0], weights[0].shape[1]
    outs = [
        shape(rows, heads), shape(e_rows, 2 * heads), shape(rows, heads),
        shape(rows, heads // HEAD_DIM, dtype=F32), shape(rows // 2, width, dtype=F32),
        shape(rows // 2, width),
    ]
    return call(cross_fwd_body, outs, sel, t, e, *weights, *vecs, also=also)


def cross_bwd_body(
    sel, g, cq, kv, lse, own, got,
    gcq_ref, gkv_ref, pm_ref, po_ref, em_ref, eo_ref, sum_ref, gc, spare,
):
    width = cq.shape[1]
    wo = choose(sel, DEC, own[5], got[1])
    gc[...] = nt(g[...], wo).astype(BF16)
    attend_back(
        cq, 0, kv, 0, width, gc, lse, None, gcq_ref, 0, gkv_ref, 0, width, spare
    )
    weight = jnp.concatenate(
        [
            choose(sel, ENC, own[4], got[0]),
            choose(sel, ENC, own[5], got[1]),
        ]
    )
    project_out(sel, gkv_ref, weight, em_ref, eo_ref)
    project_out(sel, gcq_ref, choose(sel, DEC, own[4], got[0]), pm_ref, po_ref)
    sum_ref[0:1] = col_sum(gkv_ref[:, width:].astype(F32))
    sum_ref[1:2] = col_sum(gcq_ref[...].astype(F32))


def cross_bwd(sel, g, cq, kv, lse, weights, also=()):
    rows, width = g.shape
    e_rows, heads = kv.shape[0], cq.shape[1]
    outs = [
        shape(rows, heads), shape(e_rows, 2 * heads),
        shape(rows // 2, width, dtype=F32), shape(rows // 2, width),
        shape(e_rows // 2, width, dtype=F32), shape(e_rows // 2, width),
        shape(2, heads, dtype=F32),
    ]
    return call(
        cross_bwd_body, outs, sel, g, cq, kv, lse, *weights,
        scratch=back_scratch(rows, heads), also=also,
    )


def gelu(pre):
    return 0.5 * pre * (1.0 + lax.erf(pre * (0.5 ** 0.5)))


def pick_ff(sel, section, weights):
    own1, near1, far1, own2, got2 = weights
    w1 = pick(sel, section, own1[...], near1[...], far1[...])
    return w1, choose(sel, section, own2[...], got2[...])


def ff_fwd_body(section, sel, h, own1, near1, far1, own2, got2, vown, vgot, u_ref, g_ref, pm_ref, po_ref):
    w1, w2 = pick_ff(sel, section, (own1, near1, far1, own2, got2))
    u = nn(h[...], w1) + vector(sel, section, (vown, vgot), FF)
    u_ref[...] = u
    g_ref[...] = gelu(u).astype(BF16)
    project_out(sel, g_ref, w2, pm_ref, po_ref, nt)


def ff_fwd(section, sel, h, weights, vecs, also=()):
    rows, width = h.shape
    hidden = weights[0].shape[-1]
    outs = [
        shape(rows, hidden, dtype=F32), shape(rows, hidden),
        shape(rows // 2, width, dtype=F32), shape(rows // 2, width),
    ]
    return call(functools.partial(ff_fwd_body, section), outs, sel, h, *weights, *vecs, also=also)


def ff_bwd_body(section, sel, g, u, own1, near1, far1, own2, got2, gp_ref, pm_ref, po_ref, sum_ref):
    w1, w2 = pick_ff(sel, section, (own1, near1, far1, own2, got2))
    pre = u[...]
    bell = jnp.exp(-0.5 * pre * pre) * 0.3989422804014327
    slope = 0.5 * (1.0 + lax.erf(pre * (0.5 ** 0.5))) + pre * bell
    low = (slope * nn(g[...], w2)).astype(BF16)
    gp_ref[...] = low
    sum_ref[...] = col_sum(low.astype(F32))
    project_out(sel, gp_ref, w1, pm_ref, po_ref, nt)


def ff_bwd(section, sel, g, u, weights, also=()):
    rows, width = g.shape
    hidden = weights[0].shape[-1]
    outs = [
        shape(rows, hidden), shape(rows // 2, width, dtype=F32), shape(rows // 2, width),
        shape(1, hidden, dtype=F32),
    ]
    return call(functools.partial(ff_bwd_body, section), outs, sel, g, u, *weights, also=also)


def ring_block(sel, count, step):
    return lax.rem(sel[7] + 2 * count - step - 2, count)


def product_blocks(left, right, out_ref, start):
    found = tn(left[...], right[...])
    size = out_ref.shape[1]
    for block in range(out_ref.shape[0]):
        part = found[block * size : (block + 1) * size].astype(BF16)
        out_ref[block, :, start : start + found.shape[1]] = part


def wgrad_body(cuts, sel, *refs):
    grad_ref, send_ref = refs[-2:]
    for place, start in enumerate(cuts):
        product_blocks(refs[2 * place], refs[2 * place + 1], grad_ref, start)
    send_ref[...] = grad_ref[ring_block(sel, grad_ref.shape[0], -1)]


def columns(pairs):
    cuts, at = [], 0
    for _, right in pairs:
        cuts.append(at)
        at += right.shape[1]
    return cuts, at


def wgrads(sel, count, *pairs, also=()):
    cuts, wide = columns(pairs)
    rows = pairs[0][0].shape[1] // count
    return call(
        functools.partial(wgrad_body, cuts), [shape(count, rows, wide), shape(rows, wide)], sel,
        *[entry for pair in pairs for entry in pair], also=also,
    )


def both_wgrad_body(e_cuts, d_cuts, sel, *refs):
    keep_ref, send_ref, other = refs[-3:]
    first = sel[0] == 0
    at = 2 * len(e_cuts)
    for place, start in enumerate(e_cuts):
        product_blocks(refs[2 * place], refs[2 * place + 1], keep_ref, start)
    for place, start in enumerate(d_cuts):
        product_blocks(refs[at + 2 * place], refs[at + 2 * place + 1], other, start)
    e, d = keep_ref[...], other[...]
    keep_ref[...] = jnp.where(first, e, d)
    send_ref[...] = jnp.where(first, d, e)


def both_wgrads(sel, count, e_pairs, d_pairs):
    e_cuts, wide = columns(e_pairs)
    d_cuts, _ = columns(d_pairs)
    out = shape(count, e_pairs[0][0].shape[1] // count, wide)
    return call(
        functools.partial(both_wgrad_body, e_cuts, d_cuts), [out, out], sel,
        *[entry for pair in (*e_pairs, *d_pairs) for entry in pair],
        scratch=[pltpu.VMEM(out.shape, BF16)],
    )


def second_body(sel, left, right, c, c_got, out_ref, send_ref):
    product_blocks(left, right, out_ref, 0)
    wide = right.shape[1]
    out_ref[:, :, wide:] = (c[...].astype(F32) + c_got[...].astype(F32)).astype(BF16)
    send_ref[...] = out_ref[ring_block(sel, out_ref.shape[0], -1)]


def second_and_cross(sel, left, right, c, c_got):
    count, rows, wide = c.shape
    wide += right.shape[1]
    return call(
        second_body, [shape(count, rows, wide), shape(rows, wide)], sel, left, right, c, c_got
    )


def first_and_own_body(starts, sel, other, *refs):
    keep_ref, send_ref = refs[-2:]
    for place, start in enumerate(starts):
        product_blocks(refs[2 * place], refs[2 * place + 1], keep_ref, start)
    first = sel[0] == 0
    d, e = keep_ref[...], other[...]
    keep_ref[...] = jnp.where(first, e, d)
    send_ref[...] = jnp.where(first, d, e)


def first_and_own(sel, first, *pairs):
    starts, _ = columns(pairs)
    return call(
        functools.partial(first_and_own_body, starts), [shape(*first.shape)] * 2, sel, first,
        *[entry for pair in pairs for entry in pair],
    )


def join_body(sel, keep, got, out_ref, send_ref):
    out_ref[...] = (keep[...].astype(F32) + got[...].astype(F32)).astype(BF16)
    send_ref[...] = out_ref[ring_block(sel, out_ref.shape[0], -1)]


def joined(sel, keep, got):
    return call(join_body, [shape(*keep.shape), shape(*keep.shape[1:])], sel, keep, got)


def ring_body(step, sel, grads, got, out):
    block = grads[ring_block(sel, grads.shape[0], step)]
    out[...] = (got[...].astype(F32) + block.astype(F32)).astype(BF16)


class Ring:
    def __init__(self, sel, grads, send):
        self.sel, self.grads, self.step = sel, grads, 0
        self.running = send
        self.flying = next_clip(send)

    def advance(self, also=()):
        self.running = call(
            functools.partial(ring_body, self.step), [shape(*self.running.shape)],
            self.sel, self.grads, self.flying, also=also,
        )[0]
        self.step += 1
        if self.step < self.grads.shape[0] - 1:
            self.flying = next_clip(self.running)

    def finish(self):
        while self.step < self.grads.shape[0] - 1:
            self.advance()
        return self.running


def side_body(at, sel, e, d, send):
    width = send.shape[1]
    send[...] = jnp.where(sel[0] == 0, d[:, at : at + width], e[:, :width])


def side(sel, e, d, at):
    width = d.shape[1] // 2
    return call(functools.partial(side_body, at), [shape(d.shape[0], width)], sel, e, d)[0]


def finish_body(sel, second, ff_d, got, both, own, own_got, w1, w2, proj):
    first = sel[0] == 0
    width = both.shape[1]
    heads = proj.shape[3]
    mine = jnp.where(first, second[:, :width], ff_d[:, :width]).astype(F32)
    w2[0] = mine + got[...].astype(F32)
    shared = both[...].astype(F32)
    mine = jnp.where(first, own[...], ff_d[:, width:]).astype(F32) + own_got[...].astype(F32)
    w1[0] = jnp.where(first, shared, mine)
    mine = jnp.where(first, mine, shared)
    for place in range(4):
        proj[0, place] = mine[:, place * heads : (place + 1) * heads]
    for place in range(2):
        start = width + place * heads
        proj[0, 4 + place] = second[:, start : start + heads].astype(F32)


def pack_sums_body(ey, ex1, ex, dz2, dz1, dz, wide):
    rows = (
        (ex, 0), (ey, 0), (ex1, 0), (ex, 1), (ey, 1), (ex1, 1), (ex1, 2), (ey, 2),
        (dz, 0), (dz1, 0), (dz2, 0), (dz, 1), (dz1, 1), (dz2, 1), (dz1, 2), (dz2, 3),
    )
    for at, (ref, row) in enumerate(rows):
        wide[at : at + 1] = ref[row : row + 1]


def pack_slim_body(sel, wide, got, self_e, self_d, cross, inner_e, inner_d, keep, send):
    first = sel[0] == 0
    width = cross.shape[1]
    total = wide[...] + got[...]
    e, d = total[:8], total[8:]
    keep[...] = jnp.zeros_like(keep)
    send[...] = jnp.zeros_like(send)
    keep[:8] = jnp.where(first, e, d)
    send[:8] = jnp.where(first, d, e)
    pairs = [
        (self_e[:, :width], self_d[:, :width]),
        (self_e[:, 2 * width :], self_d[:, 2 * width :]),
        (cross[0:1], cross[1:2]),
    ]
    for at, (e, d) in enumerate(pairs):
        keep[8:9, at * width : (at + 1) * width] = jnp.where(first, e, d)
        send[8:9, at * width : (at + 1) * width] = jnp.where(first, d, e)
    e, d = inner_e[...], inner_d[...]
    keep[9:10] = jnp.where(first, e, d)
    send[9:10] = jnp.where(first, d, e)


def more_body(*refs):
    total = refs[0][...]
    for ref in refs[1:-1]:
        total = total + ref[...]
    refs[-1][...] = total


def more(*entries):
    return call(more_body, [shape(*entries[0].shape, dtype=F32)], *entries)[0]


def unpack_body(*refs):
    gain, row, col, inner = refs[-4:]
    total = refs[0][...]
    for ref in refs[1:-4]:
        total = total + ref[...]
    gain[0] = total[:3]
    row[0] = total[3:8]
    width = col.shape[2]
    for place in range(3):
        col[0, place : place + 1] = total[8:9, place * width : (place + 1) * width]
    inner[...] = total[9:10]


class Total:
    def __init__(self, entry):
        self.entry, self.step = entry, 1
        self.send()

    def send(self):
        size = lax.axis_size("clip")
        if self.step < size:
            pairs = [(i, i ^ self.step) for i in range(size)]
            self.flying = lax.ppermute(self.entry, "clip", pairs)

    def advance(self):
        self.entry = more(self.entry, self.flying)
        self.step *= 2
        self.send()

    def parts(self):
        while self.step * 2 < lax.axis_size("clip"):
            self.advance()
        return self.entry, self.flying


def local(
    enc_in, dec_in, stamp_flags, dec_lengths, proj_w, fc_in, fc_out,
    col_bias, ff_bias, norm_gain, row_bias, enc_cot, dec_cot,
):
    ORDER[0] = None
    place = lax.axis_index("pipe")
    spot = lax.axis_index("head")
    parity = lax.axis_index("clip") % 2
    row, core = spot // 2, spot % 2
    sel = [place, parity, 2 * row, 2 - 2 * row, 2 * row + 1, 3 - 2 * row, core, lax.axis_index("clip")]
    sel = jnp.stack(sel).astype(jnp.int32)
    width = norm_gain.shape[-1]

    clips = lax.axis_size("clip")
    own = jnp.swapaxes(proj_w[0], 1, 2)
    e_block, block = enc_in.shape[1], dec_in.shape[1]
    mask = (stamp_flags, dec_lengths)
    v = types.SimpleNamespace()

    def weights_self():
        half_a, half_b = split(sel, [own], [(0, 0, 2), (0, 2, 4)])
        v.near_a, v.near_b = swap_pipe(half_a), swap_pipe(half_b)

    def vectors():
        vown = call(
            pack_body, [shape(16, width, dtype=F32)],
            norm_gain[0], row_bias[0], ff_bias, col_bias[0],
        )[0]
        v.vecs = (vown, swap_pipe(vown))

    def rows_in():
        v.rows = take(sel, enc_in, dec_in)
        rows = (v.rows, swap_row(v.rows))
        v.x, v.z = (*rows, 0, e_block), (*rows, e_block, block)

    def weights_1():
        (half,) = split(sel, [fc_in], [(0, 0, 1)], also=(v.near_a,))
        v.far_a, v.near_1 = swap_pair(v.near_a), swap_pipe(half)

    def norm_e():
        v.h1 = both_cores(norm_in(ENC, sel, v.x, v.vecs, also=(v.far_a,)))

    def weights_2():
        (whole,) = split(sel, [fc_out], [(0, 0, 1)], also=(v.near_b,), parts=1)
        v.far_b, v.got_2 = swap_pair(v.near_b), swap_pipe(whole)
        v.self_w = (own, v.near_a, v.far_a, v.near_b, v.far_b)

    def rows_cot():
        cot = take(sel, dec_cot, enc_cot)
        rows = (cot, swap_row(cot))
        v.dec_cots, v.enc_cots = (*rows, 0, block), (*rows, block, e_block)

    def norm_d():
        v.t1 = both_cores(norm_in(DEC, sel, v.z, v.vecs))

    def stack_d():
        v.dec_rows = stacked(v.dec_cots)
        v.gbr_z2 = both_cores(v.dec_rows)

    def self_e():
        v.qkv, v.a, v.lse, pm, po = self_fwd(
            ENC, sel, v.h1, v.self_w, v.vecs, (),
            also=(v.t1, v.near_1, v.dec_rows),
        )
        v.far_1 = swap_pair(v.near_1)
        v.xs = (pm, both_cores(po))

    def add_x():
        v.xs = (*v.xs, swap_row(add_low(sel, *v.xs)))

    def weights_c():
        (whole,) = split(sel, [own], [(0, 4, 6)], parts=1)
        v.cross_w = (own, swap_pipe(whole))

    def self_d():
        v.dqkv, v.da, v.dlse, pm, po = self_fwd(
            DEC, sel, v.t1, v.self_w, v.vecs, mask
        )
        v.zs = (pm, both_cores(po))

    def add_z():
        v.zs = (*v.zs, swap_row(add_low(sel, *v.zs)))

    def res_x1():
        v.x1, hm = res_norm(ENC, sel, v.x, v.xs, v.vecs, 3, 2, also=(v.far_1,))
        v.h2 = both_cores(hm)

    def ff_e():
        v.ff_w = (fc_in[0], v.near_1[0], v.far_1[0], fc_out[0], v.got_2[0])
        v.u, v.g, pm, po = ff_fwd(ENC, sel, v.h2, v.ff_w, v.vecs)
        v.ys = (pm, both_cores(po))

    def add_y():
        v.ys = (*v.ys, swap_row(add_low(sel, *v.ys)))

    def res_z1():
        v.z1, tm = res_norm(DEC, sel, v.z, v.zs, v.vecs, 3, 1)
        v.t2 = both_cores(tm)

    def res_y():
        v.y, em = res_norm(
            ENC, sel, v.x1, v.ys, v.vecs, 4, 1, also=(v.t2, v.gbr_z2)
        )
        v.e = both_cores(em)

    def cross():
        v.cq, v.kv, v.c, v.clse, pm, po = cross_fwd(
            sel, v.t2, v.e, v.cross_w, v.vecs
        )
        v.cs = (pm, both_cores(po))

    def add_c():
        v.cs = (*v.cs, swap_row(add_low(sel, *v.cs)))

    def res_z2():
        v.z2, tm = res_norm(DEC, sel, v.z1, v.cs, v.vecs, None, 2)
        v.t3 = both_cores(tm)

    def ff_d():
        v.w_pre, v.w, pm, po = ff_fwd(DEC, sel, v.t3, v.ff_w, v.vecs)
        v.rs = (pm, po)

    def add_r():
        pm, po = v.rs
        recv = both_cores(po)
        v.r_got = swap_row(add_low(sel, pm, recv, block))
        v.rs = (pm, recv, v.r_got)

    def ff_back_d():
        v.gp_d, pm, po, v.inner_d = ff_bwd(DEC, sel, v.gbr_z2, v.w_pre, v.ff_w)
        v.gs = (pm, both_cores(po))

    def add_gz2():
        v.gs = (*v.gs, swap_row(add_low(sel, *v.gs)))

    def wgrad_ff_d():
        v.ring_ff_d = Ring(
            sel, *wgrads(sel, clips, (v.gbr_z2, v.w), (v.t3, v.gp_d))
        )

    def back_z2():
        v.gz2, gm, v.sums_z2 = norm_back(
            DEC, sel, v.z2, v.dec_cots, v.gs, v.vecs, 2
        )
        v.gbr_c = both_cores(gm)

    def cross_back():
        v.gcq, v.gkv, zm, zo, ym, yo, v.sums_c = cross_bwd(
            sel, v.gbr_c, v.cq, v.kv, v.clse, v.cross_w
        )
        v.gys, v.gzs = (ym, both_cores(yo)), (zm, zo)

    def add_gy():
        v.gys = (*v.gys, swap_row(add_low(sel, *v.gys)))

    def add_gz1():
        pm, po = v.gzs
        recv = both_cores(po)
        v.gzs = (pm, recv, swap_row(add_low(sel, pm, recv)))

    def wgrad_cross():
        v.cross_g, send = both_wgrads(
            sel, clips, [(v.e, v.gkv)], [(v.t2, v.gcq), (v.gbr_c, v.c)]
        )
        v.cross_got = swap_pipe(send)

    def outputs():
        v.keep_fwd, send = last_fwd(sel, v.y, v.z2, v.rs, v.vecs)
        v.got_fwd = swap_pipe(send)

    def place_outputs():
        v.e_out, v.d_out = placed(sel, v.keep_fwd, v.got_fwd, e_block)

    def back_y():
        v.gy, gm, v.sums_y = norm_back(
            ENC, sel, v.y, v.enc_cots, v.gys, v.vecs, 1
        )
        v.gbr_y = both_cores(gm)

    def ff_back_e():
        v.gp_e, pm, po, v.inner_e = ff_bwd(
            ENC, sel, v.gbr_y, v.u, v.ff_w
        )
        v.gxs = (pm, both_cores(po))

    def add_gx1():
        v.gxs = (*v.gxs, swap_row(add_low(sel, *v.gxs)))

    def wgrad_first():
        v.ff_1, _ = wgrads(sel, clips, (v.h2, v.gp_e))

    def wgrad_second():
        v.ring_2 = Ring(
            sel, *second_and_cross(sel, v.gbr_y, v.g, v.cross_g, v.cross_got)
        )

    def back_z1():
        v.gz1, gm, v.sums_z1 = norm_back(
            DEC, sel, v.z1, v.gz2, v.gzs, v.vecs, 1
        )
        v.gbr_z1 = both_cores(gm)

    def self_back_d():
        v.gqkv_d, pm, po, v.self_d_sum = self_bwd(
            DEC, sel, v.gbr_z1, v.dqkv, v.dlse, v.self_w, mask
        )
        v.lz = (pm, swap_core(po))

    def wgrad_own_d():
        v.pair_keep, send = first_and_own(
            sel, v.ff_1, (v.t1, v.gqkv_d), (v.gbr_z1, v.da)
        )
        v.pair_got = swap_pipe(send)

    def back_x1():
        v.gx1, gm, v.sums_x1 = norm_back(
            ENC, sel, v.x1, v.gy, v.gxs, v.vecs, 2
        )
        v.gbr_x1 = both_cores(gm)

    def self_back_e():
        v.gqkv_e, pm, po, v.self_e_sum = self_bwd(
            ENC, sel, v.gbr_x1, v.qkv, v.lse, v.self_w, ()
        )
        v.lx = (pm, both_cores(po))

    def add_last_both():
        sums = (v.lx[0], v.lz[0], v.lx[1], v.lz[1])
        v.last = (*sums, swap_row(add_last(sel, *sums)))

    def wgrad_own_e():
        v.ring_own = Ring(
            sel, *wgrads(sel, clips, (v.h1, v.gqkv_e), (v.gbr_x1, v.a))
        )

    def inputs():
        v.keep, send, v.sums_x, v.sums_z = last_back(
            sel, v.rows, v.gx1, v.gz1, v.last, v.vecs
        )
        v.got = swap_pipe(send)

    def place_inputs():
        v.ge_out, v.gd_out = placed(sel, v.keep, v.got, e_block)

    def ring_ff_d():
        v.ring_ff_d.advance()

    def ring_2():
        v.ring_2.advance()

    def ring_own():
        v.ring_own.advance()

    def ring_1():
        v.ring_1.advance()

    def join():
        v.ring_1 = Ring(sel, *joined(sel, v.pair_keep, v.pair_got))

    def side_1():
        v.side_got = swap_pipe(side(sel, v.ring_2.finish(), v.ring_ff_d.finish(), 0))

    def side_2():
        own_e, ff_d = v.ring_own.finish(), v.ring_ff_d.finish()
        v.own_e_got = swap_pipe(side(sel, own_e, ff_d, ff_d.shape[1] // 2))

    def vec_core():
        wide = call(
            pack_sums_body, [shape(16, width, dtype=F32)],
            v.sums_y, v.sums_x1, v.sums_x, v.sums_z2, v.sums_z1, v.sums_z,
        )[0]
        v.wide = (wide, swap_core(wide))

    def vec_row():
        wide = more(*v.wide)
        v.wide = (wide, swap_row(wide))

    def vec_pipe():
        mine, other = call(
            pack_slim_body, [shape(16, width, dtype=F32), shape(16, width, dtype=F32)],
            sel, *v.wide, v.self_e_sum, v.self_d_sum, v.sums_c,
            v.inner_e, v.inner_d,
        )
        v.mine = (mine, swap_pipe(other))

    def vec_clip():
        v.total = Total(more(*v.mine))

    def vec_half():
        v.total.advance()

    def unpack():
        v.vectors = call(
            unpack_body,
            [
                shape(1, 3, width, dtype=F32), shape(1, 5, width, dtype=F32),
                shape(1, 3, own.shape[1], dtype=F32), shape(1, ff_bias.shape[1], dtype=F32),
            ],
            *v.total.parts(),
        )

    for step in (
        weights_self, vectors, rows_in, weights_1, norm_e, weights_2, rows_cot, norm_d, stack_d,
        self_e, add_x, weights_c, self_d, add_z, res_x1, ff_e, add_y, res_z1, res_y, cross, add_c,
        res_z2, ff_d, ff_back_d, add_gz2, wgrad_ff_d, add_r, back_z2, cross_back, ring_ff_d,
        add_gy, add_gz1, wgrad_cross, outputs, ring_ff_d, back_y, ff_back_e, add_gx1, wgrad_first,
        wgrad_second, back_z1, self_back_d, wgrad_own_d, ring_ff_d, ring_2, back_x1,
        place_outputs, self_back_e, ring_2, add_last_both, wgrad_own_e, ring_2, join, inputs,
        vec_core, ring_own, vec_row, vec_pipe, ring_1, side_1, place_inputs, vec_clip, ring_own,
        ring_1, vec_half, side_2, unpack, ring_1,
    ):
        step()
    heads, hidden, cut = own.shape[1], fc_in.shape[-1], width // clips
    out_first, out_second, out_proj = call(
        finish_body,
        [
            shape(1, cut, hidden, dtype=F32),
            shape(1, cut, hidden, dtype=F32),
            shape(1, 6, cut, heads, dtype=F32),
        ],
        sel, v.ring_2.finish(), v.ring_ff_d.finish(), v.side_got,
        v.ring_1.finish(), v.ring_own.finish(), v.own_e_got,
    )
    out_gain, out_row, out_col, out_inner = v.vectors
    return (
        v.e_out,
        v.d_out,
        v.ge_out,
        v.gd_out,
        out_proj,
        out_first,
        out_second,
        out_col,
        out_inner,
        out_gain,
        out_row,
    )


def solution(mesh):
    return jax.shard_map(
        local,
        mesh=mesh,
        in_specs=(
            P("clip", "head", None),
            P("clip", "head", None),
            P("clip"),
            P("clip"),
            P("pipe", None, None, "head"),
            P("pipe", None, "head"),
            P("pipe", None, "head"),
            P("pipe", None, "head"),
            P("pipe", "head"),
            P("pipe", None, None),
            P("pipe", None, None),
            P("clip", "head", None),
            P("clip", "head", None),
        ),
        out_specs=(
            P("clip", "head", "pipe"),
            P("clip", "head", "pipe"),
            P("clip", "head", "pipe"),
            P("clip", "head", "pipe"),
            P("pipe", None, "clip", "head"),
            P("pipe", "clip", "head"),
            P("pipe", "clip", "head"),
            P("pipe", None, "head"),
            P("pipe", "head"),
            P("pipe", None, None),
            P("pipe", None, None),
        ),
        check_vma=False,
    )
```

```python
import functools
import types

import jax
import jax.numpy as jnp
from jax import lax
from jax.experimental import pallas as pl
from jax.experimental.pallas import tpu as pltpu
from jax.sharding import PartitionSpec as P

HEAD_DIM = 64
DEC_SHORT = 224
SCALE = HEAD_DIM ** (-0.5)
SCALE_2 = SCALE * 1.4426950408889634
F32 = jnp.float32
BF16 = jnp.bfloat16
ENC, DEC = 0, 1

CORE_GROUPS = [[0, 1], [2, 3]]
CORE_PAIRS = [(0, 1), (1, 0), (2, 3), (3, 2)]
ROW_PAIRS = [(0, 2), (2, 0), (1, 3), (3, 1)]
PIPE_PAIRS = [(0, 1), (1, 0)]

GAIN, ROW, FF, COL = 0, 3, 8, 9


def both_cores(entry):
    return lax.all_gather(entry, "head", axis=0, axis_index_groups=CORE_GROUPS, tiled=True)


def swap_core(entry):
    return lax.ppermute(entry, "head", CORE_PAIRS)


def swap_row(entry):
    return lax.ppermute(entry, "head", ROW_PAIRS)


def swap_pipe(entry):
    return lax.ppermute(entry, "pipe", PIPE_PAIRS)


def swap_pair(entry):
    size = lax.axis_size("clip")
    return lax.ppermute(entry, "clip", [(i, i ^ 1) for i in range(size)])


def next_clip(entry):
    size = lax.axis_size("clip")
    return lax.ppermute(entry, "clip", [(i, (i + 1) % size) for i in range(size)])


def nn(left, right):
    return lax.dot_general(left, right, (((1,), (0,)), ((), ())), preferred_element_type=F32)


def nt(left, right):
    return lax.dot_general(left, right, (((1,), (1,)), ((), ())), preferred_element_type=F32)


def tn(left, right):
    return lax.dot_general(left, right, (((0,), (0,)), ((), ())), preferred_element_type=F32)


def shape(*dims, dtype=BF16):
    return jax.ShapeDtypeStruct(dims, dtype)


ORDER = [None]
COST = dict(
    ring=0.05,
    self_fwd=3.4, self_bwd=4.8, cross_fwd=3.5, cross_bwd=5.4, ff_fwd=2.4, ff_bwd=2.8, wgrad=1.7,
    both_wgrad=1.7, norm_in=0.8, res_norm=0.9, norm_back=0.05, take=1.2, last_back=1.2,
    join_two=1.9, finish=2.5, place=1.3,
)


def call(body, outs, *ins, flops=0, limit=12, scratch=(), anywhere=(), out_anywhere=False, also=()):
    vmem = pl.BlockSpec(memory_space=pltpu.VMEM)
    smem = pl.BlockSpec(memory_space=pltpu.SMEM)
    any_space = pl.BlockSpec(memory_space=pl.ANY)
    hbm = pl.BlockSpec(memory_space=pltpu.HBM)
    specs = [
        hbm if place in anywhere else smem if a.dtype == jnp.int32 else vmem
        for place, a in enumerate(ins)
    ]
    count = len(ins)
    before = (*(() if ORDER[0] is None else (ORDER[0],)), *also)

    def ordered(*refs):
        body(*refs[:count], *refs[count + len(before) :])

    name = getattr(body, "func", body).__name__[:-5]
    found = pl.pallas_call(
        ordered,
        name=name,
        out_shape=outs,
        in_specs=[*specs, *[any_space] * len(before)],
        out_specs=[hbm if out_anywhere else vmem] * len(outs),
        scratch_shapes=scratch,
        compiler_params=pltpu.CompilerParams(vmem_limit_bytes=limit << 20),
        cost_estimate=pl.CostEstimate(
            flops=int(COST.get(name, 0.6) * 1.15e9), bytes_accessed=1, transcendentals=0
        ),
    )(*ins, *before)
    ORDER[0] = found[-1]
    return found


def pick(sel, section, own, near, far):
    is_own = sel[0] == section
    even = sel[1] == 0
    half = near.shape[0]
    top = jnp.where(is_own, own[:half], jnp.where(even, near, far))
    bottom = jnp.where(is_own, own[half:], jnp.where(even, far, near))
    return jnp.concatenate([top, bottom])


def choose(sel, section, own, got):
    return jnp.where(sel[0] == section, own, got)


def vector(sel, section, vecs, row, width=None):
    own, got = vecs
    cut = slice(0, width if width else own.shape[1])
    return jnp.where(sel[0] == section, own[row : row + 1, cut], got[row : row + 1, cut])


def norm_parts(rows):
    centered = rows - jnp.mean(rows, axis=-1, keepdims=True)
    variance = jnp.mean(centered * centered, axis=-1, keepdims=True)
    inverse = lax.rsqrt(variance + 1e-05)
    return centered * inverse, inverse


def take_body(count, sel, *refs):
    out, sems = refs[-2:]
    copies, at = [], 0
    for i in range(count):
        rows = refs[i].shape[1]
        copies.append(
            pltpu.make_async_copy(refs[i].at[sel[0]], out.at[at : at + rows], sems.at[i])
        )
        at += rows
    for copy in copies:
        copy.start()
    for copy in copies:
        copy.wait()


def take(sel, *arrays, limit=12, also=()):
    count = len(arrays)
    rows = sum(a.shape[1] for a in arrays)
    return call(
        functools.partial(take_body, count), [shape(rows, arrays[0].shape[2])], sel, *arrays,
        anywhere=range(1, 1 + count), scratch=[pltpu.SemaphoreType.DMA((count,))], limit=limit,
        also=also,
    )[0]


def split_body(cuts, sel, *refs):
    count = max(source for source, _, _ in cuts) + 1
    sems = refs[-1]
    copies = []
    for place, (source, start, stop) in enumerate(cuts):
        out = refs[count + place]
        half = out.shape[1]
        rows = pl.ds(pl.multiple_of(sel[1] * half, half), half)
        if half == refs[source].shape[1]:
            rows = slice(None)
        copies.append(
            pltpu.make_async_copy(refs[source].at[start:stop, rows], out, sems.at[place])
        )
    for copy in copies:
        copy.start()
    for copy in copies:
        copy.wait()


def split(sel, arrays, cuts, also=(), limit=12, parts=2):
    outs = [
        shape(stop - start, arrays[source].shape[1] // parts, arrays[source].shape[2])
        for source, start, stop in cuts
    ]
    return call(
        functools.partial(split_body, cuts), outs, sel, *arrays,
        anywhere=range(1, 1 + len(arrays)), out_anywhere=True,
        scratch=[pltpu.SemaphoreType.DMA((len(cuts),))], also=also, limit=limit,
    )


def pack_body(gain, row, ff, col, out):
    out[...] = jnp.zeros_like(out)
    out[GAIN : GAIN + 3] = gain[...]
    out[ROW : ROW + 5] = row[...]
    out[FF : FF + 1] = ff[...]
    out[COL : COL + 3, : col.shape[1]] = col[...]


def from_other(sel, pm, recv):
    return (1 - sel[6]) * (recv.shape[0] - pm.shape[0])


def add_body(start, sel, pm, recv, low):
    count = low.shape[0]
    there = pl.ds(pl.multiple_of(from_other(sel, pm, recv) + start, count), count)
    low[...] = (pm[start : start + count] + recv[there].astype(F32)).astype(BF16)


def add_low(sel, pm, recv, start=0, also=()):
    rows, width = pm.shape
    return call(
        functools.partial(add_body, start), [shape(rows - start, width)], sel, pm, recv, also=also
    )[0]


def add_last_body(sel, xm, zm, xr, zr, low):
    at = 0
    for pm, recv in ((xm, xr), (zm, zr)):
        count = pm.shape[0] // 2
        there = pl.ds(pl.multiple_of(from_other(sel, pm, recv) + count, count), count)
        low[at : at + count] = (pm[count:] + recv[there].astype(F32)).astype(BF16)
        at += count


def add_last(sel, xm, zm, xr, zr):
    rows = (xm.shape[0] + zm.shape[0]) // 2
    return call(add_last_body, [shape(rows, xm.shape[1])], sel, xm, zm, xr, zr)[0]


def stack_body(start, block, own, got, out):
    out[:block] = own[start : start + block]
    out[block:] = got[start : start + block]


def stacked(rows):
    own, got, start, block = rows
    return call(
        functools.partial(stack_body, start, block), [shape(2 * block, own.shape[1])], own, got
    )[0]


def norm_in_body(section, at, sel, own, got, vown, vgot, hm_ref):
    gain = vector(sel, section, (vown, vgot), GAIN)
    bias = vector(sel, section, (vown, vgot), ROW)
    block = hm_ref.shape[0] // 2
    for start, part in ((0, own), (block, got)):
        unit, _ = norm_parts(part[at : at + block].astype(F32))
        hm_ref[start : start + block] = (unit * gain + bias).astype(BF16)


def norm_in(section, sel, rows, vecs, also=()):
    own, got, start, block = rows
    return call(
        functools.partial(norm_in_body, section, start), [shape(2 * block, own.shape[1])],
        sel, own, got, *vecs, also=also,
    )[0]


def summed(sel, pm, recv, got, rows, other):
    block = rows.stop - rows.start
    there = pl.ds(pl.multiple_of(from_other(sel, pm, recv) + rows.start, block), block)
    return pm[rows] + recv[there].astype(F32) + got[other].astype(F32)


def halves(block):
    return ((slice(0, block), slice(block, 2 * block)), (slice(block, 2 * block), slice(0, block)))


def res_norm_body(section, out_row, index, at, *refs):
    split = at is not None
    sel = refs[0]
    res = refs[1 : 3 if split else 2]
    pm, recv, got, vown, vgot, x_ref, hm_ref = refs[3 if split else 2 :]
    vecs = (vown, vgot)
    gain = vector(sel, section, vecs, GAIN + index)
    bias = vector(sel, section, vecs, ROW + index)
    block = pm.shape[0] // 2
    for place, (rows, other) in enumerate(halves(block)):
        base = res[place][at : at + block].astype(F32) if split else res[0][rows]
        now = base + summed(sel, pm, recv, got, rows, other)
        if out_row is not None:
            now = now + vector(sel, section, vecs, ROW + out_row)
        x_ref[rows] = now
        unit, _ = norm_parts(now)
        hm_ref[rows] = (unit * gain + bias).astype(BF16)


def res_norm(section, sel, res, sums, vecs, out_row, index, also=()):
    rows, width = sums[0].shape
    at, res = (res[2], res[:2]) if isinstance(res, tuple) else (None, (res,))
    return call(
        functools.partial(res_norm_body, section, out_row, index, at),
        [shape(rows, width, dtype=F32), shape(rows, width)],
        sel, *res, *sums, *vecs, also=also,
    )


def norm_grad(rows, gain, grad):
    unit, inverse = norm_parts(rows)
    scaled = grad * gain
    back = inverse * (
        scaled
        - jnp.mean(scaled, axis=-1, keepdims=True)
        - unit * jnp.mean(scaled * unit, axis=-1, keepdims=True)
    )
    return back, unit


def col_sum(entry):
    return jnp.sum(entry, axis=0, keepdims=True)


def norm_back_body(section, index, at, *refs):
    split = at is not None
    sel, x = refs[:2]
    res = refs[2 : 4 if split else 3]
    pm, recv, got, vown, vgot, g_ref, gm_ref, sum_ref = refs[4 if split else 3 :]
    gain = vector(sel, section, (vown, vgot), GAIN + index)
    block = pm.shape[0] // 2
    for place, (rows, other) in enumerate(halves(block)):
        grad = summed(sel, pm, recv, got, rows, other)
        base = res[place][at : at + block].astype(F32) if split else res[0][rows]
        back, unit = norm_grad(x[rows], gain, grad)
        now = base + back
        g_ref[rows] = now
        gm_ref[rows] = now.astype(BF16)
        if place == 0:
            sum_ref[0:1] = col_sum(grad * unit)
            sum_ref[1:2] = col_sum(grad)
            sum_ref[2:3] = col_sum(now)
            sum_ref[3:4] = col_sum(base)


def norm_back(section, sel, x, res, sums, vecs, index, also=()):
    rows, width = x.shape
    at, res = (res[2], res[:2]) if isinstance(res, tuple) else (None, (res,))
    return call(
        functools.partial(norm_back_body, section, index, at),
        [shape(rows, width, dtype=F32), shape(rows, width), shape(4, width, dtype=F32)],
        sel, x, *res, *sums, *vecs, also=also,
    )


def send_halves(sel, rows, low, keep_ref, send_ref):
    width = low.shape[1] // 2
    left, right = low[:, :width], low[:, width:]
    keep_ref[rows] = jnp.where(sel[0] == 0, left, right)
    send_ref[rows] = jnp.where(sel[0] == 0, right, left)


def last_fwd_body(sel, y, z2, pm, recv, got, vown, vgot, keep_ref, send_ref):
    block = got.shape[0]
    e_block = y.shape[0] // 2
    rows = slice(0, block)
    r = z2[rows] + summed(sel, pm, recv, got, rows, rows)
    r = r + vector(sel, DEC, (vown, vgot), ROW + 4)
    send_halves(sel, slice(0, e_block), y[:e_block].astype(BF16), keep_ref, send_ref)
    send_halves(sel, slice(e_block, e_block + block), r.astype(BF16), keep_ref, send_ref)


def last_fwd(sel, y, z2, sums, vecs):
    rows = y.shape[0] // 2 + sums[2].shape[0]
    width = y.shape[1] // 2
    return call(
        last_fwd_body, [shape(rows, width), shape(rows, width)], sel, y, z2, *sums, *vecs
    )


def last_back_body(
    sel, rows_in, gx1, gz1, xm, zm, xr, zr, all_got, vown, vgot,
    keep_ref, send_ref, sum_x, sum_z,
):
    vecs = (vown, vgot)
    start = 0
    for section, res, pm, recv, out in ((ENC, gx1, xm, xr, sum_x), (DEC, gz1, zm, zr, sum_z)):
        gain = vector(sel, section, vecs, GAIN)
        block = pm.shape[0] // 2
        rows = slice(0, block)
        grad = summed(sel, pm, recv, all_got, rows, slice(start, start + block))
        back, unit = norm_grad(rows_in[start : start + block].astype(F32), gain, grad)
        low = (res[rows] + back).astype(BF16)
        send_halves(sel, slice(start, start + block), low, keep_ref, send_ref)
        out[0:1] = col_sum(grad * unit)
        out[1:2] = col_sum(grad)
        start += block


def last_back(sel, rows_in, gx1, gz1, sums, vecs):
    rows, width = rows_in.shape
    return call(
        last_back_body,
        [
            shape(rows, width // 2), shape(rows, width // 2),
            shape(2, width, dtype=F32), shape(2, width, dtype=F32),
        ],
        sel, rows_in, gx1, gz1, *sums, *vecs,
    )


def place_body(sel, keep, got, *outs):
    start = 0
    for ref in outs:
        rows = slice(start, start + ref.shape[1])
        ref[0] = jnp.where(sel[0] == 0, keep[rows], got[rows])
        ref[1] = jnp.where(sel[0] == 0, got[rows], keep[rows])
        start += ref.shape[1]


def placed(sel, keep, got, block):
    rows, width = keep.shape
    return call(
        place_body, [shape(2, block, width), shape(2, rows - block, width)], sel, keep, got
    )


def places(sel, axis, dims):
    at = lax.broadcasted_iota(jnp.int32, dims, axis)
    size = dims[axis] // 4
    shift = sel[5] - 3
    for block in (2, 1, 0):
        shift = jnp.where(at < (block + 1) * size, sel[2 + block] - block, shift)
    return at + shift * size


def text_length(sel, flags, lengths):
    return jnp.minimum(lengths[sel[0]], DEC_SHORT * (1 + flags[sel[0]]))


def allowed(sel, flags, lengths, rows, key_axis):
    shapes = ((1, rows), (rows, 1)) if key_axis == 1 else ((rows, 1), (1, rows))
    keys = places(sel, key_axis, shapes[0])
    keys = jnp.where(keys < text_length(sel, flags, lengths), keys, rows)
    return keys <= places(sel, 1 - key_axis, shapes[1])


def attend(q_ref, q_at, kv_ref, k_at, v_at, mask, a_ref, lse_ref):
    rows, width = a_ref.shape
    if mask:
        keep = allowed(*mask, rows, 1)
    for head in range(width // HEAD_DIM):
        cut = slice(head * HEAD_DIM, (head + 1) * HEAD_DIM)
        k_head = kv_ref[:, k_at + cut.start : k_at + cut.stop]
        v_head = kv_ref[:, v_at + cut.start : v_at + cut.stop]
        scores = nt(q_ref[:, q_at + cut.start : q_at + cut.stop], k_head)
        if mask:
            scores = jnp.where(keep, scores, -1e30)
        top = jnp.max(scores, axis=-1, keepdims=True)
        shifted = jnp.exp2((scores - top) * SCALE_2)
        total = jnp.sum(shifted, axis=-1, keepdims=True)
        low = (shifted * (1.0 / total)).astype(BF16)
        a_ref[:, cut] = nn(low, v_head).astype(BF16)
        lse_ref[:, head : head + 1] = top * SCALE_2 + jnp.log2(total)


def attend_back(
    q_ref, q_at, kv_ref, k_at, v_at, grad, lse, mask, gq_ref, gq_at, gkv_ref, gk_at, gv_at,
    rows_ref,
):
    rows, width = grad.shape
    rows_ref[:, : lse.shape[1]] = lse[...]
    sums = rows_ref[...].T
    if mask:
        keep = allowed(*mask, rows, 0)
    for head in range(width // HEAD_DIM):
        cut = slice(head * HEAD_DIM, (head + 1) * HEAD_DIM)
        q_head = q_ref[:, q_at + cut.start : q_at + cut.stop]
        o_head = grad[:, cut]
        k_head = kv_ref[:, k_at + cut.start : k_at + cut.stop]
        v_head = kv_ref[:, v_at + cut.start : v_at + cut.stop]
        scores = nt(k_head, q_head)
        if mask:
            scores = jnp.where(keep, scores, -1e30)
        weights = jnp.exp2(scores * SCALE_2 - sums[head : head + 1])
        both = weights * nt(v_head, o_head)
        grad_s = (both - weights * jnp.sum(both, axis=0, keepdims=True)).astype(BF16)
        gv = nn(weights.astype(BF16), o_head)
        gk = nn(grad_s, q_head) * SCALE
        gq = tn(grad_s, k_head) * SCALE
        gkv_ref[:, gk_at + cut.start : gk_at + cut.stop] = gk.astype(BF16)
        gkv_ref[:, gv_at + cut.start : gv_at + cut.stop] = gv.astype(BF16)
        gq_ref[:, gq_at + cut.start : gq_at + cut.stop] = gq.astype(BF16)


def halves_of(sel, half):
    mine = pl.ds(pl.multiple_of(sel[6] * half, half), half)
    other = pl.ds(pl.multiple_of((1 - sel[6]) * half, half), half)
    return mine, other


def project_out(sel, mixed_ref, weight, pm_ref, po_ref, by=nn):
    mine, other = halves_of(sel, pm_ref.shape[0])
    pm_ref[...] = by(mixed_ref[mine], weight)
    po_ref[...] = by(mixed_ref[other], weight).astype(BF16)


def self_fwd_body(section, masked, *refs):
    sel, h, own, near_a, far_a, near_b, far_b, vown, vgot = refs[:9]
    mask = (sel, *refs[9:11]) if masked else None
    qkv_ref, a_ref, lse_ref, pm_ref, po_ref = refs[11 if masked else 9 :]
    width = a_ref.shape[1]
    wq = pick(sel, section, own[0], near_a[0], far_a[0])
    wk = pick(sel, section, own[1], near_a[1], far_a[1])
    wv = pick(sel, section, own[2], near_b[0], far_b[0])
    bq = vector(sel, section, (vown, vgot), COL, width)
    bv = vector(sel, section, (vown, vgot), COL + 1, width)
    rows = h[...]
    qkv_ref[:, :width] = (nt(rows, wq) + bq).astype(BF16)
    qkv_ref[:, width : 2 * width] = nt(rows, wk).astype(BF16)
    qkv_ref[:, 2 * width :] = (nt(rows, wv) + bv).astype(BF16)
    attend(qkv_ref, 0, qkv_ref, width, 2 * width, mask, a_ref, lse_ref)
    wo = pick(sel, section, own[3], near_b[1], far_b[1])
    project_out(sel, a_ref, wo, pm_ref, po_ref)


def self_fwd(section, sel, h, weights, vecs, mask, also=()):
    rows, width = h.shape
    heads = weights[0].shape[1]
    outs = [
        shape(rows, 3 * heads), shape(rows, heads), shape(rows, heads // HEAD_DIM, dtype=F32),
        shape(rows // 2, width, dtype=F32), shape(rows // 2, width),
    ]
    return call(
        functools.partial(self_fwd_body, section, bool(mask)), outs, sel, h, *weights, *vecs, *mask,
        also=also,
    )


def back_scratch(rows, heads):
    return [pltpu.VMEM((rows, heads), BF16), pltpu.VMEM((rows, 128), F32)]


def self_bwd_body(section, masked, *refs):
    sel, g, qkv, lse, own, near_a, far_a, near_b, far_b = refs[:9]
    refs = refs[9:]
    mask, refs = ((sel, *refs[:2]), refs[2:]) if masked else (None, refs)
    gqkv_ref, pm_ref, po_ref, sum_ref, ga, spare = refs
    width = ga.shape[1]
    wo = pick(sel, section, own[3], near_b[1], far_b[1])
    ga[...] = nt(g[...], wo).astype(BF16)
    attend_back(
        qkv, 0, qkv, width, 2 * width, ga, lse, mask,
        gqkv_ref, 0, gqkv_ref, width, 2 * width, spare,
    )
    weight = jnp.concatenate(
        [
            pick(sel, section, own[0], near_a[0], far_a[0]),
            pick(sel, section, own[1], near_a[1], far_a[1]),
            pick(sel, section, own[2], near_b[0], far_b[0]),
        ]
    )
    project_out(sel, gqkv_ref, weight, pm_ref, po_ref)
    sum_ref[...] = col_sum(gqkv_ref[...].astype(F32))


def self_bwd(section, sel, g, qkv, lse, weights, mask, also=()):
    rows, width = g.shape
    heads = weights[0].shape[1]
    outs = [
        shape(rows, 3 * heads), shape(rows // 2, width, dtype=F32),
        shape(rows // 2, width), shape(1, 3 * heads, dtype=F32),
    ]
    return call(
        functools.partial(self_bwd_body, section, bool(mask)), outs, sel, g, qkv, lse,
        *weights, *mask, scratch=back_scratch(rows, heads), also=also,
    )


def cross_fwd_body(
    sel, t, e, own, got, vown, vgot, cq_ref, kv_ref, c_ref, lse_ref, pm_ref, po_ref
):
    width = cq_ref.shape[1]
    vecs = (vown, vgot)
    w4 = choose(sel, ENC, own[4], got[0])
    w5 = choose(sel, ENC, own[5], got[1])
    rows = e[...]
    kv_ref[:, :width] = nt(rows, w4).astype(BF16)
    kv_ref[:, width:] = (nt(rows, w5) + vector(sel, ENC, vecs, COL + 2, width)).astype(BF16)
    wq = choose(sel, DEC, own[4], got[0])
    cq_ref[...] = (nt(t[...], wq) + vector(sel, DEC, vecs, COL + 2, width)).astype(BF16)
    attend(cq_ref, 0, kv_ref, 0, width, None, c_ref, lse_ref)
    wo = choose(sel, DEC, own[5], got[1])
    project_out(sel, c_ref, wo, pm_ref, po_ref)


def cross_fwd(sel, t, e, weights, vecs, also=()):
    rows, width = t.shape
    e_rows, heads = e.shape[0], weights[0].shape[1]
    outs = [
        shape(rows, heads), shape(e_rows, 2 * heads), shape(rows, heads),
        shape(rows, heads // HEAD_DIM, dtype=F32), shape(rows // 2, width, dtype=F32),
        shape(rows // 2, width),
    ]
    return call(cross_fwd_body, outs, sel, t, e, *weights, *vecs, also=also)


def cross_bwd_body(
    sel, g, cq, kv, lse, own, got,
    gcq_ref, gkv_ref, pm_ref, po_ref, em_ref, eo_ref, sum_ref, gc, spare,
):
    width = cq.shape[1]
    wo = choose(sel, DEC, own[5], got[1])
    gc[...] = nt(g[...], wo).astype(BF16)
    attend_back(
        cq, 0, kv, 0, width, gc, lse, None, gcq_ref, 0, gkv_ref, 0, width, spare
    )
    weight = jnp.concatenate(
        [
            choose(sel, ENC, own[4], got[0]),
            choose(sel, ENC, own[5], got[1]),
        ]
    )
    project_out(sel, gkv_ref, weight, em_ref, eo_ref)
    project_out(sel, gcq_ref, choose(sel, DEC, own[4], got[0]), pm_ref, po_ref)
    sum_ref[0:1] = col_sum(gkv_ref[:, width:].astype(F32))
    sum_ref[1:2] = col_sum(gcq_ref[...].astype(F32))


def cross_bwd(sel, g, cq, kv, lse, weights, also=()):
    rows, width = g.shape
    e_rows, heads = kv.shape[0], cq.shape[1]
    outs = [
        shape(rows, heads), shape(e_rows, 2 * heads),
        shape(rows // 2, width, dtype=F32), shape(rows // 2, width),
        shape(e_rows // 2, width, dtype=F32), shape(e_rows // 2, width),
        shape(2, heads, dtype=F32),
    ]
    return call(
        cross_bwd_body, outs, sel, g, cq, kv, lse, *weights,
        scratch=back_scratch(rows, heads), also=also,
    )


def gelu(pre):
    return 0.5 * pre * (1.0 + lax.erf(pre * (0.5 ** 0.5)))


def pick_ff(sel, section, weights):
    own1, near1, far1, own2, got2 = weights
    w1 = pick(sel, section, own1[...], near1[...], far1[...])
    return w1, choose(sel, section, own2[...], got2[...])


def ff_fwd_body(section, sel, h, own1, near1, far1, own2, got2, vown, vgot, u_ref, g_ref, pm_ref, po_ref):
    w1, w2 = pick_ff(sel, section, (own1, near1, far1, own2, got2))
    u = nn(h[...], w1) + vector(sel, section, (vown, vgot), FF)
    u_ref[...] = u
    g_ref[...] = gelu(u).astype(BF16)
    project_out(sel, g_ref, w2, pm_ref, po_ref, nt)


def ff_fwd(section, sel, h, weights, vecs, also=()):
    rows, width = h.shape
    hidden = weights[0].shape[-1]
    outs = [
        shape(rows, hidden, dtype=F32), shape(rows, hidden),
        shape(rows // 2, width, dtype=F32), shape(rows // 2, width),
    ]
    return call(functools.partial(ff_fwd_body, section), outs, sel, h, *weights, *vecs, also=also)


def ff_bwd_body(section, sel, g, u, own1, near1, far1, own2, got2, gp_ref, pm_ref, po_ref, sum_ref):
    w1, w2 = pick_ff(sel, section, (own1, near1, far1, own2, got2))
    pre = u[...]
    bell = jnp.exp(-0.5 * pre * pre) * 0.3989422804014327
    slope = 0.5 * (1.0 + lax.erf(pre * (0.5 ** 0.5))) + pre * bell
    low = (slope * nn(g[...], w2)).astype(BF16)
    gp_ref[...] = low
    sum_ref[...] = col_sum(low.astype(F32))
    project_out(sel, gp_ref, w1, pm_ref, po_ref, nt)


def ff_bwd(section, sel, g, u, weights, also=()):
    rows, width = g.shape
    hidden = weights[0].shape[-1]
    outs = [
        shape(rows, hidden), shape(rows // 2, width, dtype=F32), shape(rows // 2, width),
        shape(1, hidden, dtype=F32),
    ]
    return call(functools.partial(ff_bwd_body, section), outs, sel, g, u, *weights, also=also)


def ring_block(sel, count, step):
    return lax.rem(sel[7] + 2 * count - step - 2, count)


def product_blocks(left, right, out_ref, start):
    found = tn(left[...], right[...])
    size = out_ref.shape[1]
    for block in range(out_ref.shape[0]):
        part = found[block * size : (block + 1) * size].astype(BF16)
        out_ref[block, :, start : start + found.shape[1]] = part


def wgrad_body(cuts, sel, *refs):
    grad_ref, send_ref = refs[-2:]
    for place, start in enumerate(cuts):
        product_blocks(refs[2 * place], refs[2 * place + 1], grad_ref, start)
    send_ref[...] = grad_ref[ring_block(sel, grad_ref.shape[0], -1)]


def columns(pairs):
    cuts, at = [], 0
    for _, right in pairs:
        cuts.append(at)
        at += right.shape[1]
    return cuts, at


def wgrads(sel, count, *pairs, also=()):
    cuts, wide = columns(pairs)
    rows = pairs[0][0].shape[1] // count
    return call(
        functools.partial(wgrad_body, cuts), [shape(count, rows, wide), shape(rows, wide)], sel,
        *[entry for pair in pairs for entry in pair], also=also,
    )


def both_wgrad_body(e_cuts, d_cuts, sel, *refs):
    keep_ref, send_ref, other = refs[-3:]
    first = sel[0] == 0
    at = 2 * len(e_cuts)
    for place, start in enumerate(e_cuts):
        product_blocks(refs[2 * place], refs[2 * place + 1], keep_ref, start)
    for place, start in enumerate(d_cuts):
        product_blocks(refs[at + 2 * place], refs[at + 2 * place + 1], other, start)
    e, d = keep_ref[...], other[...]
    keep_ref[...] = jnp.where(first, e, d)
    send_ref[...] = jnp.where(first, d, e)


def both_wgrads(sel, count, e_pairs, d_pairs):
    e_cuts, wide = columns(e_pairs)
    d_cuts, _ = columns(d_pairs)
    out = shape(count, e_pairs[0][0].shape[1] // count, wide)
    return call(
        functools.partial(both_wgrad_body, e_cuts, d_cuts), [out, out], sel,
        *[entry for pair in (*e_pairs, *d_pairs) for entry in pair],
        scratch=[pltpu.VMEM(out.shape, BF16)],
    )


def second_body(sel, left, right, c, c_got, out_ref, send_ref):
    product_blocks(left, right, out_ref, 0)
    wide = right.shape[1]
    out_ref[:, :, wide:] = (c[...].astype(F32) + c_got[...].astype(F32)).astype(BF16)
    send_ref[...] = out_ref[ring_block(sel, out_ref.shape[0], -1)]


def second_and_cross(sel, left, right, c, c_got):
    count, rows, wide = c.shape
    wide += right.shape[1]
    return call(
        second_body, [shape(count, rows, wide), shape(rows, wide)], sel, left, right, c, c_got
    )


def first_and_own_body(starts, sel, other, *refs):
    keep_ref, send_ref = refs[-2:]
    for place, start in enumerate(starts):
        product_blocks(refs[2 * place], refs[2 * place + 1], keep_ref, start)
    first = sel[0] == 0
    d, e = keep_ref[...], other[...]
    keep_ref[...] = jnp.where(first, e, d)
    send_ref[...] = jnp.where(first, d, e)


def first_and_own(sel, first, *pairs):
    starts, _ = columns(pairs)
    return call(
        functools.partial(first_and_own_body, starts), [shape(*first.shape)] * 2, sel, first,
        *[entry for pair in pairs for entry in pair],
    )


def join_body(sel, keep, got, out_ref, send_ref):
    out_ref[...] = (keep[...].astype(F32) + got[...].astype(F32)).astype(BF16)
    send_ref[...] = out_ref[ring_block(sel, out_ref.shape[0], -1)]


def joined(sel, keep, got):
    return call(join_body, [shape(*keep.shape), shape(*keep.shape[1:])], sel, keep, got)


def ring_body(step, sel, grads, got, out):
    block = grads[ring_block(sel, grads.shape[0], step)]
    out[...] = (got[...].astype(F32) + block.astype(F32)).astype(BF16)


class Ring:
    def __init__(self, sel, grads, send):
        self.sel, self.grads, self.step = sel, grads, 0
        self.running = send
        self.flying = next_clip(send)

    def advance(self, also=()):
        self.running = call(
            functools.partial(ring_body, self.step), [shape(*self.running.shape)],
            self.sel, self.grads, self.flying, also=also,
        )[0]
        self.step += 1
        if self.step < self.grads.shape[0] - 1:
            self.flying = next_clip(self.running)

    def finish(self):
        while self.step < self.grads.shape[0] - 1:
            self.advance()
        return self.running


def side_body(at, sel, e, d, send):
    width = send.shape[1]
    send[...] = jnp.where(sel[0] == 0, d[:, at : at + width], e[:, :width])


def side(sel, e, d, at):
    width = d.shape[1] // 2
    return call(functools.partial(side_body, at), [shape(d.shape[0], width)], sel, e, d)[0]


def finish_body(sel, second, ff_d, got, both, own, own_got, w1, w2, proj):
    first = sel[0] == 0
    width = both.shape[1]
    heads = proj.shape[3]
    mine = jnp.where(first, second[:, :width], ff_d[:, :width]).astype(F32)
    w2[0] = mine + got[...].astype(F32)
    shared = both[...].astype(F32)
    mine = jnp.where(first, own[...], ff_d[:, width:]).astype(F32) + own_got[...].astype(F32)
    w1[0] = jnp.where(first, shared, mine)
    mine = jnp.where(first, mine, shared)
    for place in range(4):
        proj[0, place] = mine[:, place * heads : (place + 1) * heads]
    for place in range(2):
        start = width + place * heads
        proj[0, 4 + place] = second[:, start : start + heads].astype(F32)


def pack_sums_body(ey, ex1, ex, dz2, dz1, dz, wide):
    rows = (
        (ex, 0), (ey, 0), (ex1, 0), (ex, 1), (ey, 1), (ex1, 1), (ex1, 2), (ey, 2),
        (dz, 0), (dz1, 0), (dz2, 0), (dz, 1), (dz1, 1), (dz2, 1), (dz1, 2), (dz2, 3),
    )
    for at, (ref, row) in enumerate(rows):
        wide[at : at + 1] = ref[row : row + 1]


def pack_slim_body(sel, wide, got, self_e, self_d, cross, inner_e, inner_d, keep, send):
    first = sel[0] == 0
    width = cross.shape[1]
    total = wide[...] + got[...]
    e, d = total[:8], total[8:]
    keep[...] = jnp.zeros_like(keep)
    send[...] = jnp.zeros_like(send)
    keep[:8] = jnp.where(first, e, d)
    send[:8] = jnp.where(first, d, e)
    pairs = [
        (self_e[:, :width], self_d[:, :width]),
        (self_e[:, 2 * width :], self_d[:, 2 * width :]),
        (cross[0:1], cross[1:2]),
    ]
    for at, (e, d) in enumerate(pairs):
        keep[8:9, at * width : (at + 1) * width] = jnp.where(first, e, d)
        send[8:9, at * width : (at + 1) * width] = jnp.where(first, d, e)
    e, d = inner_e[...], inner_d[...]
    keep[9:10] = jnp.where(first, e, d)
    send[9:10] = jnp.where(first, d, e)


def more_body(*refs):
    total = refs[0][...]
    for ref in refs[1:-1]:
        total = total + ref[...]
    refs[-1][...] = total


def more(*entries):
    return call(more_body, [shape(*entries[0].shape, dtype=F32)], *entries)[0]


def unpack_body(*refs):
    gain, row, col, inner = refs[-4:]
    total = refs[0][...]
    for ref in refs[1:-4]:
        total = total + ref[...]
    gain[0] = total[:3]
    row[0] = total[3:8]
    width = col.shape[2]
    for place in range(3):
        col[0, place : place + 1] = total[8:9, place * width : (place + 1) * width]
    inner[...] = total[9:10]


class Total:
    def __init__(self, entry):
        self.entry, self.step = entry, 1
        self.send()

    def send(self):
        size = lax.axis_size("clip")
        if self.step < size:
            pairs = [(i, i ^ self.step) for i in range(size)]
            self.flying = lax.ppermute(self.entry, "clip", pairs)

    def advance(self):
        self.entry = more(self.entry, self.flying)
        self.step *= 2
        self.send()

    def parts(self):
        while self.step * 2 < lax.axis_size("clip"):
            self.advance()
        return self.entry, self.flying


def local(
    enc_in, dec_in, stamp_flags, dec_lengths, proj_w, fc_in, fc_out,
    col_bias, ff_bias, norm_gain, row_bias, enc_cot, dec_cot,
):
    ORDER[0] = None
    place = lax.axis_index("pipe")
    spot = lax.axis_index("head")
    parity = lax.axis_index("clip") % 2
    row, core = spot // 2, spot % 2
    sel = [place, parity, 2 * row, 2 - 2 * row, 2 * row + 1, 3 - 2 * row, core, lax.axis_index("clip")]
    sel = jnp.stack(sel).astype(jnp.int32)
    width = norm_gain.shape[-1]

    clips = lax.axis_size("clip")
    own = jnp.swapaxes(proj_w[0], 1, 2)
    e_block, block = enc_in.shape[1], dec_in.shape[1]
    mask = (stamp_flags, dec_lengths)
    v = types.SimpleNamespace()

    def weights_self():
        half_a, half_b = split(sel, [own], [(0, 0, 2), (0, 2, 4)])
        v.near_a, v.near_b = swap_pipe(half_a), swap_pipe(half_b)

    def vectors():
        vown = call(
            pack_body, [shape(16, width, dtype=F32)],
            norm_gain[0], row_bias[0], ff_bias, col_bias[0],
        )[0]
        v.vecs = (vown, swap_pipe(vown))

    def rows_in():
        v.rows = take(sel, enc_in, dec_in)
        rows = (v.rows, swap_row(v.rows))
        v.x, v.z = (*rows, 0, e_block), (*rows, e_block, block)

    def weights_1():
        (half,) = split(sel, [fc_in], [(0, 0, 1)], also=(v.near_a,))
        v.far_a, v.near_1 = swap_pair(v.near_a), swap_pipe(half)

    def norm_e():
        v.h1 = both_cores(norm_in(ENC, sel, v.x, v.vecs, also=(v.far_a,)))

    def weights_2():
        (whole,) = split(sel, [fc_out], [(0, 0, 1)], also=(v.near_b,), parts=1)
        v.far_b, v.got_2 = swap_pair(v.near_b), swap_pipe(whole)
        v.self_w = (own, v.near_a, v.far_a, v.near_b, v.far_b)

    def rows_cot():
        cot = take(sel, dec_cot, enc_cot)
        rows = (cot, swap_row(cot))
        v.dec_cots, v.enc_cots = (*rows, 0, block), (*rows, block, e_block)

    def norm_d():
        v.t1 = both_cores(norm_in(DEC, sel, v.z, v.vecs))

    def stack_d():
        v.dec_rows = stacked(v.dec_cots)
        v.gbr_z2 = both_cores(v.dec_rows)

    def self_e():
        v.qkv, v.a, v.lse, pm, po = self_fwd(
            ENC, sel, v.h1, v.self_w, v.vecs, (),
            also=(v.t1, v.near_1, v.dec_rows),
        )
        v.far_1 = swap_pair(v.near_1)
        v.xs = (pm, both_cores(po))

    def add_x():
        v.xs = (*v.xs, swap_row(add_low(sel, *v.xs)))

    def weights_c():
        (whole,) = split(sel, [own], [(0, 4, 6)], parts=1)
        v.cross_w = (own, swap_pipe(whole))

    def self_d():
        v.dqkv, v.da, v.dlse, pm, po = self_fwd(
            DEC, sel, v.t1, v.self_w, v.vecs, mask
        )
        v.zs = (pm, both_cores(po))

    def add_z():
        v.zs = (*v.zs, swap_row(add_low(sel, *v.zs)))

    def res_x1():
        v.x1, hm = res_norm(ENC, sel, v.x, v.xs, v.vecs, 3, 2, also=(v.far_1,))
        v.h2 = both_cores(hm)

    def ff_e():
        v.ff_w = (fc_in[0], v.near_1[0], v.far_1[0], fc_out[0], v.got_2[0])
        v.u, v.g, pm, po = ff_fwd(ENC, sel, v.h2, v.ff_w, v.vecs)
        v.ys = (pm, both_cores(po))

    def add_y():
        v.ys = (*v.ys, swap_row(add_low(sel, *v.ys)))

    def res_z1():
        v.z1, tm = res_norm(DEC, sel, v.z, v.zs, v.vecs, 3, 1)
        v.t2 = both_cores(tm)

    def res_y():
        v.y, em = res_norm(
            ENC, sel, v.x1, v.ys, v.vecs, 4, 1, also=(v.t2, v.gbr_z2)
        )
        v.e = both_cores(em)

    def cross():
        v.cq, v.kv, v.c, v.clse, pm, po = cross_fwd(
            sel, v.t2, v.e, v.cross_w, v.vecs
        )
        v.cs = (pm, both_cores(po))

    def add_c():
        v.cs = (*v.cs, swap_row(add_low(sel, *v.cs)))

    def res_z2():
        v.z2, tm = res_norm(DEC, sel, v.z1, v.cs, v.vecs, None, 2)
        v.t3 = both_cores(tm)

    def ff_d():
        v.w_pre, v.w, pm, po = ff_fwd(DEC, sel, v.t3, v.ff_w, v.vecs)
        v.rs = (pm, po)

    def add_r():
        pm, po = v.rs
        recv = both_cores(po)
        v.r_got = swap_row(add_low(sel, pm, recv, block))
        v.rs = (pm, recv, v.r_got)

    def ff_back_d():
        v.gp_d, pm, po, v.inner_d = ff_bwd(DEC, sel, v.gbr_z2, v.w_pre, v.ff_w)
        v.gs = (pm, both_cores(po))

    def add_gz2():
        v.gs = (*v.gs, swap_row(add_low(sel, *v.gs)))

    def wgrad_ff_d():
        v.ring_ff_d = Ring(
            sel, *wgrads(sel, clips, (v.gbr_z2, v.w), (v.t3, v.gp_d))
        )

    def back_z2():
        v.gz2, gm, v.sums_z2 = norm_back(
            DEC, sel, v.z2, v.dec_cots, v.gs, v.vecs, 2
        )
        v.gbr_c = both_cores(gm)

    def cross_back():
        v.gcq, v.gkv, zm, zo, ym, yo, v.sums_c = cross_bwd(
            sel, v.gbr_c, v.cq, v.kv, v.clse, v.cross_w
        )
        v.gys, v.gzs = (ym, both_cores(yo)), (zm, zo)

    def add_gy():
        v.gys = (*v.gys, swap_row(add_low(sel, *v.gys)))

    def add_gz1():
        pm, po = v.gzs
        recv = both_cores(po)
        v.gzs = (pm, recv, swap_row(add_low(sel, pm, recv)))

    def wgrad_cross():
        v.cross_g, send = both_wgrads(
            sel, clips, [(v.e, v.gkv)], [(v.t2, v.gcq), (v.gbr_c, v.c)]
        )
        v.cross_got = swap_pipe(send)

    def outputs():
        v.keep_fwd, send = last_fwd(sel, v.y, v.z2, v.rs, v.vecs)
        v.got_fwd = swap_pipe(send)

    def place_outputs():
        v.e_out, v.d_out = placed(sel, v.keep_fwd, v.got_fwd, e_block)

    def back_y():
        v.gy, gm, v.sums_y = norm_back(
            ENC, sel, v.y, v.enc_cots, v.gys, v.vecs, 1
        )
        v.gbr_y = both_cores(gm)

    def ff_back_e():
        v.gp_e, pm, po, v.inner_e = ff_bwd(
            ENC, sel, v.gbr_y, v.u, v.ff_w
        )
        v.gxs = (pm, both_cores(po))

    def add_gx1():
        v.gxs = (*v.gxs, swap_row(add_low(sel, *v.gxs)))

    def wgrad_first():
        v.ff_1, _ = wgrads(sel, clips, (v.h2, v.gp_e))

    def wgrad_second():
        v.ring_2 = Ring(
            sel, *second_and_cross(sel, v.gbr_y, v.g, v.cross_g, v.cross_got)
        )

    def back_z1():
        v.gz1, gm, v.sums_z1 = norm_back(
            DEC, sel, v.z1, v.gz2, v.gzs, v.vecs, 1
        )
        v.gbr_z1 = both_cores(gm)

    def self_back_d():
        v.gqkv_d, pm, po, v.self_d_sum = self_bwd(
            DEC, sel, v.gbr_z1, v.dqkv, v.dlse, v.self_w, mask
        )
        v.lz = (pm, swap_core(po))

    def wgrad_own_d():
        v.pair_keep, send = first_and_own(
            sel, v.ff_1, (v.t1, v.gqkv_d), (v.gbr_z1, v.da)
        )
        v.pair_got = swap_pipe(send)

    def back_x1():
        v.gx1, gm, v.sums_x1 = norm_back(
            ENC, sel, v.x1, v.gy, v.gxs, v.vecs, 2
        )
        v.gbr_x1 = both_cores(gm)

    def self_back_e():
        v.gqkv_e, pm, po, v.self_e_sum = self_bwd(
            ENC, sel, v.gbr_x1, v.qkv, v.lse, v.self_w, ()
        )
        v.lx = (pm, both_cores(po))

    def add_last_both():
        sums = (v.lx[0], v.lz[0], v.lx[1], v.lz[1])
        v.last = (*sums, swap_row(add_last(sel, *sums)))

    def wgrad_own_e():
        v.ring_own = Ring(
            sel, *wgrads(sel, clips, (v.h1, v.gqkv_e), (v.gbr_x1, v.a))
        )

    def inputs():
        v.keep, send, v.sums_x, v.sums_z = last_back(
            sel, v.rows, v.gx1, v.gz1, v.last, v.vecs
        )
        v.got = swap_pipe(send)

    def place_inputs():
        v.ge_out, v.gd_out = placed(sel, v.keep, v.got, e_block)

    def ring_ff_d():
        v.ring_ff_d.advance()

    def ring_2():
        v.ring_2.advance()

    def ring_own():
        v.ring_own.advance()

    def ring_1():
        v.ring_1.advance()

    def join():
        v.ring_1 = Ring(sel, *joined(sel, v.pair_keep, v.pair_got))

    def side_1():
        v.side_got = swap_pipe(side(sel, v.ring_2.finish(), v.ring_ff_d.finish(), 0))

    def side_2():
        own_e, ff_d = v.ring_own.finish(), v.ring_ff_d.finish()
        v.own_e_got = swap_pipe(side(sel, own_e, ff_d, ff_d.shape[1] // 2))

    def vec_core():
        wide = call(
            pack_sums_body, [shape(16, width, dtype=F32)],
            v.sums_y, v.sums_x1, v.sums_x, v.sums_z2, v.sums_z1, v.sums_z,
        )[0]
        v.wide = (wide, swap_core(wide))

    def vec_row():
        wide = more(*v.wide)
        v.wide = (wide, swap_row(wide))

    def vec_pipe():
        mine, other = call(
            pack_slim_body, [shape(16, width, dtype=F32), shape(16, width, dtype=F32)],
            sel, *v.wide, v.self_e_sum, v.self_d_sum, v.sums_c,
            v.inner_e, v.inner_d,
        )
        v.mine = (mine, swap_pipe(other))

    def vec_clip():
        v.total = Total(more(*v.mine))

    def vec_half():
        v.total.advance()

    def unpack():
        v.vectors = call(
            unpack_body,
            [
                shape(1, 3, width, dtype=F32), shape(1, 5, width, dtype=F32),
                shape(1, 3, own.shape[1], dtype=F32), shape(1, ff_bias.shape[1], dtype=F32),
            ],
            *v.total.parts(),
        )

    for step in (
        weights_self, vectors, rows_in, weights_1, norm_e, weights_2, rows_cot, norm_d, stack_d,
        self_e, add_x, weights_c, self_d, add_z, res_x1, ff_e, add_y, res_z1, res_y, cross, add_c,
        res_z2, ff_d, ff_back_d, add_gz2, wgrad_ff_d, add_r, back_z2, cross_back, ring_ff_d,
        add_gy, add_gz1, wgrad_cross, outputs, ring_ff_d, back_y, ff_back_e, add_gx1, wgrad_first,
        wgrad_second, back_z1, self_back_d, wgrad_own_d, ring_ff_d, ring_2, back_x1,
        place_outputs, self_back_e, ring_2, add_last_both, wgrad_own_e, ring_2, join, inputs,
        vec_core, ring_own, vec_row, vec_pipe, ring_1, side_1, place_inputs, vec_clip, ring_own,
        ring_1, vec_half, side_2, unpack, ring_1,
    ):
        step()
    heads, hidden, cut = own.shape[1], fc_in.shape[-1], width // clips
    out_first, out_second, out_proj = call(
        finish_body,
        [
            shape(1, cut, hidden, dtype=F32),
            shape(1, cut, hidden, dtype=F32),
            shape(1, 6, cut, heads, dtype=F32),
        ],
        sel, v.ring_2.finish(), v.ring_ff_d.finish(), v.side_got,
        v.ring_1.finish(), v.ring_own.finish(), v.own_e_got,
    )
    out_gain, out_row, out_col, out_inner = v.vectors
    return (
        v.e_out,
        v.d_out,
        v.ge_out,
        v.gd_out,
        out_proj,
        out_first,
        out_second,
        out_col,
        out_inner,
        out_gain,
        out_row,
    )


def solution(mesh):
    return jax.shard_map(
        local,
        mesh=mesh,
        in_specs=(
            P("clip", "head", None),
            P("clip", "head", None),
            P("clip"),
            P("clip"),
            P("pipe", None, None, "head"),
            P("pipe", None, "head"),
            P("pipe", None, "head"),
            P("pipe", None, "head"),
            P("pipe", "head"),
            P("pipe", None, None),
            P("pipe", None, None),
            P("clip", "head", None),
            P("clip", "head", None),
        ),
        out_specs=(
            P("clip", "head", "pipe"),
            P("clip", "head", "pipe"),
            P("clip", "head", "pipe"),
            P("clip", "head", "pipe"),
            P("pipe", None, "clip", "head"),
            P("pipe", "clip", "head"),
            P("pipe", "clip", "head"),
            P("pipe", None, "head"),
            P("pipe", "head"),
            P("pipe", None, None),
            P("pipe", None, None),
        ),
        check_vma=False,
    )
```
